256 devices in a mesh: ctx: 32 (over z, y_lo, core), head: 8 (over x, y_hi).
Axes of the slice: x: 4, y: 4 (y_hi: 2, y_lo: 2; y = y_hi * 2 + y_lo), z: 8, core: 2. Of those that a mesh axis runs over, the one named last changes fastest.
Arguments:
- queries: bfloat16 [16384, 4096], P('ctx', 'head'), may hold values from -180 to 180
- keys_values: bfloat16 [2, 16384, 1024], P(None, 'ctx', 'head'), may hold values from -6 to 6
- trace_lengths: int32 [7], replicated, may hold values from 1 to 4096, as said below
- step_rows: int32 [7, 32], replicated, may hold values from 0 to 16383, as said below
- prompt_ids: int32 [7], replicated, may hold values from 0 to 1
- cluster_ids: int32 [7], replicated, may hold values from 0 to 3
- step_stream: bfloat16 [224, 8192], P(None, 'ctx'), may hold values from -0.29882812 to 0.29882812
- out_weight: bfloat16 [4096, 8192], P('head', 'ctx'), may hold values from -3.59375 to 3.59375
- score_weight: bfloat16 [8192, 8192], P('ctx', 'head'), may hold values from -0.0625 to 0.0625
- class_weight: bfloat16 [8192, 2], P('head'), may hold values from -0.125 to 0.125
Outputs:
- attended: float32 [16384, 4096], P('ctx', 'head')
- step_scores: float32 [7, 32], replicated
- votes: float32 [2, 4], replicated
The draws below stay inside these ranges and needn't reach their ends.
Inputs may be any that keep to these rules, and one draw needn't show every extreme that they name: `trace_lengths`: the traces lie end to end from row 0 and fill the context; one trace has exactly 4096 rows. `step_rows`: each trace's step rows lie inside that trace and rise strictly; the last one is the trace's last row.
All inputs are finite; a program needn't handle non-finite values.
Results may differ from the reference program's by a relative error of at most 0.033.
Values may be sent and summed in bfloat16 or wider, within the bound.
No kernel may reach another device: no remote copies, remote signals or barrier semaphores. Data moves between devices by JAX's collectives and lax.ppermute only.
A program may use at most 64 MiB of HBM per device.

```python
import jax
import jax.numpy as jnp
from jax import lax

D = 8192
HQ = 32
KVH = 8
HD = 128
TRACES = 7
STEPS = 32
PROMPTS = 2
CLUSTERS = 4
TOTAL = 16384
MOST = 4096


def base_keys(key):
    return jnp.clip(jax.random.normal(key, (TOTAL, KVH * HD), jnp.float32), -6.0, 6.0)


def trace_layout(key):
    key = jax.random.fold_in(key, 17)
    remainder = TOTAL - MOST
    typical = remainder // (TRACES - 1)
    pair_count = (TRACES - 1) // 2
    spread_by = jax.random.randint(key, (pair_count,), -(typical // 2), typical // 2 + 1)
    others = jnp.concatenate([typical + spread_by, typical - spread_by])
    lengths = jnp.concatenate([jnp.full((1,), MOST, jnp.int32), others.astype(jnp.int32)])
    shuffle = jax.random.permutation(jax.random.fold_in(key, 18), TRACES)
    return lengths[shuffle].astype(jnp.int32)


def draw_queries(key, part):
    key = jax.random.fold_in(key, 5)
    return jnp.clip(jax.random.normal(key, (TOTAL, HQ * HD), jnp.float32), -6.0, 6.0).astype(jnp.bfloat16)


def draw_keys_values(key, part):
    shared = base_keys(key)
    key = jax.random.fold_in(key, 7)
    keys_part = shared
    values_part = jnp.clip(0.5 * jax.random.normal(key, (TOTAL, KVH * HD), jnp.float32), -2.0, 2.0)
    return jnp.stack([keys_part, values_part]).astype(jnp.bfloat16)


def draw_trace_lengths(key, part):
    lengths = trace_layout(key)
    return lengths


def draw_step_rows(key, part):
    lengths = trace_layout(key)
    key = jax.random.fold_in(key, 23)
    starts = jnp.cumsum(lengths) - lengths
    step_marks = jnp.arange(1, STEPS + 1, dtype=jnp.int32)
    step_ends = step_marks[None, :] * lengths[:, None] // STEPS - 1
    slack_rows = jnp.maximum(lengths // (2 * STEPS), 1)
    jitter = jax.random.randint(key, (TRACES, STEPS), 0, 1 << 20) % slack_rows[:, None]
    jitter = jnp.where(step_marks[None, :] == STEPS, 0, jitter)
    return (starts[:, None] + step_ends - jitter).astype(jnp.int32)


def with_ends(array, key, least, top_value):
    place = [jax.random.randint(jax.random.fold_in(key, axis), (), 0, length) for axis, length in enumerate(array.shape)]
    longest = array.shape.index(max(array.shape))
    next_to = place[:longest] + [(place[longest] + 1) % array.shape[longest]] + place[longest + 1:]
    return array.at[tuple(place)].set(least).at[tuple(next_to)].set(top_value)


def shard_levels(own_key, extent, cuts, least, largest):
    gain = 1.0
    for axis_at, shards_of in cuts:
        draws = jax.random.uniform(jax.random.fold_in(jax.random.fold_in(own_key, 6), axis_at), (shards_of,), jnp.float32, least / len(cuts), largest / len(cuts))
        gain = gain * jnp.repeat(jnp.exp(draws), extent[axis_at] // shards_of).reshape((-1,) + (1,) * (len(extent) - 1 - axis_at))
    return gain


def noise(own_key, shape, width, reach, split=(), kind=jnp.bfloat16):
    values = width * jax.random.normal(own_key, shape, jnp.float32)
    if split:
        values = values * shard_levels(own_key, shape, split, -0.22, 0.18)
    return jnp.clip(values, -reach, reach).astype(kind)


def setup_inputs(seed: int = 0) -> dict:
    key_list = jax.random.split(jax.random.key(seed), 11)
    return {
        "queries": draw_queries(jax.random.fold_in(key_list[10], 71), 0),
        "keys_values": draw_keys_values(jax.random.fold_in(key_list[10], 71), 0),
        "trace_lengths": draw_trace_lengths(jax.random.fold_in(key_list[10], 71), 0),
        "step_rows": draw_step_rows(jax.random.fold_in(key_list[10], 71), 0),
        "prompt_ids": with_ends(jax.random.randint(key_list[4], (TRACES,), 0, PROMPTS), jax.random.fold_in(key_list[4], 1), 0, PROMPTS - 1).astype(jnp.int32),
        "cluster_ids": with_ends(jax.random.randint(key_list[5], (TRACES,), 0, CLUSTERS), jax.random.fold_in(key_list[5], 1), 0, CLUSTERS - 1).astype(jnp.int32),
        "step_stream": noise(key_list[6], (TRACES * STEPS, D), 0.05, 0.29882812, ((1, 32),)),
        "out_weight": noise(key_list[7], (HQ * HD, D), 0.6, 3.59375, ((0, 8), (1, 32))),
        "score_weight": noise(key_list[8], (D, D), D ** -0.5, 0.0625, ((0, 32), (1, 8))),
        "class_weight": noise(key_list[9], (D, 2), (D // 4) ** -0.5, 0.125, ((0, 8),)),
    }


def trace_of(positions, trace_lengths):
    trace_ends = jnp.cumsum(trace_lengths).astype(jnp.int32)
    return jnp.sum((positions[:, None] >= trace_ends[None, :]).astype(jnp.int32), axis=1)


def reference(queries, keys_values, trace_lengths, step_rows, prompt_ids, cluster_ids, step_stream, out_weight, score_weight, class_weight):
    all_rows = queries.shape[0]
    blk_rows = min(512, all_rows)
    key_window = min(MOST + blk_rows, all_rows)
    per_group = HQ // KVH
    positions = jnp.arange(all_rows, dtype=jnp.int32)
    row_owner = trace_of(positions, trace_lengths)
    score_scale = HD ** -0.5

    def one_block(block_index):
        first_row = (block_index * blk_rows).astype(jnp.int32)
        key_start = jnp.clip(first_row - MOST, 0, all_rows - key_window).astype(jnp.int32)
        q_rows = lax.dynamic_slice_in_dim(queries, first_row, blk_rows, 0).astype(jnp.float32)
        q_rows = q_rows.reshape(blk_rows, KVH, per_group, HD)
        kv_rows = lax.dynamic_slice_in_dim(keys_values, key_start, key_window, 1).astype(jnp.float32)
        keys_blk = kv_rows[0].reshape(key_window, KVH, HD)
        values_blk = kv_rows[1].reshape(key_window, KVH, HD)
        logits_blk = jnp.einsum("qhgd,khd->hgqk", q_rows, keys_blk) * score_scale
        q_pos = first_row + jnp.arange(blk_rows, dtype=jnp.int32)
        k_pos = key_start + jnp.arange(key_window, dtype=jnp.int32)
        q_owner = lax.dynamic_slice_in_dim(row_owner, first_row, blk_rows, 0)
        k_owner = lax.dynamic_slice_in_dim(row_owner, key_start, key_window, 0)
        allowed = (q_owner[:, None] == k_owner[None, :]) & (k_pos[None, :] <= q_pos[:, None])
        logits_blk = jnp.where(allowed[None, None], logits_blk, -jnp.inf)
        row_top = jnp.max(logits_blk, axis=3, keepdims=True)
        weights = jnp.exp(logits_blk - row_top)
        weight_sum = jnp.sum(weights, axis=3)
        rounded = lax.optimization_barrier(weights.astype(jnp.bfloat16)).astype(jnp.float32)
        summed = jnp.einsum("hgqk,khd->qhgd", rounded, values_blk)
        normed = summed / jnp.transpose(weight_sum, (2, 0, 1))[..., None]
        return normed.reshape(blk_rows, HQ * HD)

    attended = lax.map(one_block, jnp.arange(all_rows // blk_rows, dtype=jnp.int32))
    attended = attended.reshape(all_rows, HQ * HD)
    flat_rows = step_rows.reshape(-1)
    picked = attended[flat_rows].astype(jnp.bfloat16)
    projected = jnp.dot(picked, out_weight, preferred_element_type=jnp.float32)
    stream = (step_stream.astype(jnp.float32) + projected).astype(jnp.bfloat16)
    inner = jnp.dot(stream, score_weight, preferred_element_type=jnp.float32)
    hidden = jnp.maximum(inner, 0.0).astype(jnp.bfloat16)
    logits = jnp.dot(hidden, class_weight, preferred_element_type=jnp.float32)
    step_scores = jax.nn.sigmoid(logits[:, 1] - logits[:, 0]).reshape(TRACES, STEPS)
    chain = jnp.min(step_scores, axis=1)
    prompt_mask = (prompt_ids[:, None] == jnp.arange(PROMPTS, dtype=jnp.int32)[None, :]).astype(jnp.float32)
    cluster_mask = (cluster_ids[:, None] == jnp.arange(CLUSTERS, dtype=jnp.int32)[None, :]).astype(jnp.float32)
    votes = jnp.sum(prompt_mask[:, :, None] * cluster_mask[:, None, :] * chain[:, None, None], axis=0)
    return attended, step_scores, votes
```

```python
import functools
import math

import jax
import jax.numpy as jnp
from jax import lax
from jax.experimental import pallas as pl
from jax.experimental.pallas import tpu as pltpu
from jax.sharding import PartitionSpec as P

HD = 128
PROMPTS = 2
CLUSTERS = 4
TRACES = 7
STEPS = 32
PER_GROUP = 4
BLOCK = 512
TILE = 256
Z = 8
PLANE = 4
PAD = 8
GROUP = Z * PAD
WIDE = 1024
COEF = HD**-0.5 * math.log2(math.e)
LOW = -1e30
VMEM = pl.BlockSpec(memory_space=pltpu.VMEM)
SMEM = pl.BlockSpec(memory_space=pltpu.SMEM)
BF16 = jnp.bfloat16
F32 = jnp.float32


def first_key(row, lengths):
    start = row * 0
    end = jnp.int32(0)
    for t in range(TRACES):
        end = end + lengths[t]
        start = jnp.where(row >= end, end, start)
    return start


def attend_kernel(slots, first, last, *refs):
    refs = list(refs)
    me_ref, lengths, q_ref = refs[:3]
    kv_refs = refs[3 : 3 + len(slots)]
    refs = refs[3 + len(slots) :]
    if last:
        rows_ref, refs = refs[0], refs[1:]
    if not first:
        m_in, l_in, acc_in = refs[:3]
        refs = refs[3:]
    if last:
        out_ref, keep_ref, pass_ref, send_ref, m_ref, l_ref, acc_ref, half_ref = refs
        m_ref[...] = m_in[...]
        l_ref[...] = l_in[...]
        acc_ref[...] = acc_in[...]
    else:
        m_ref, l_ref, acc_ref = refs
        if not first:
            m_ref[...] = m_in[...]
            l_ref[...] = l_in[...]
            acc_ref[...] = acc_in[...]
    me = me_ref[0]
    place = me % PLANE
    row0 = me * BLOCK
    ones = jnp.ones((BLOCK, HD), BF16)

    def weigh(rows, h, keys, ext, mask, fresh):
        cols = slice(h * HD, (h + 1) * HD)
        s = lax.dot_general(
            q_ref[rows, cols], keys, (((1,), (1,)), ((), ())), preferred_element_type=F32
        )
        if mask is not None:
            s = jnp.where(mask, s, LOW)
        top = jnp.max(s, axis=1, keepdims=True)
        if fresh:
            top = jnp.broadcast_to(top, (TILE, HD))
        else:
            before = m_ref[rows, cols]
            top = jnp.maximum(before, top)
        wide = jnp.concatenate([top] * (s.shape[1] // HD), axis=1)
        p = jnp.exp2((s - wide) * COEF).astype(BF16)
        pv = jnp.dot(p, ext, preferred_element_type=F32)
        m_ref[rows, cols] = top
        if fresh:
            acc_ref[rows, cols] = pv[:, :HD]
            l_ref[rows, cols] = pv[:, HD:]
        else:
            scale = jnp.exp2((before - top) * COEF)
            acc_ref[rows, cols] = acc_ref[rows, cols] * scale + pv[:, :HD]
            l_ref[rows, cols] = l_ref[rows, cols] * scale + pv[:, HD:]

    def own_block(kv):
        for tile in range(BLOCK // TILE):
            width = (tile + 1) * TILE
            rows = slice(tile * TILE, width)
            keys = kv[0, :width, :]
            ext = jnp.concatenate([kv[1, :width, :], ones[:width]], axis=1)
            q_pos = row0 + tile * TILE + lax.broadcasted_iota(jnp.int32, (TILE, width), 0)
            k_pos = row0 + lax.broadcasted_iota(jnp.int32, (TILE, width), 1)
            starts = first_key(
                row0 + tile * TILE + lax.broadcasted_iota(jnp.int32, (TILE, HD), 0), lengths
            )
            starts = jnp.concatenate([starts] * (width // HD), axis=1)
            mask = (k_pos <= q_pos) & (k_pos >= starts)
            for h in range(PER_GROUP):
                weigh(rows, h, keys, ext, mask, True)

    def other_block(kv, block):
        key0 = block * BLOCK

        def one_tile(tile, carry):
            begin = pl.multiple_of(tile * TILE, TILE)
            rows = pl.ds(begin, TILE)
            low = first_key(row0 + begin, lengths)
            high = first_key(row0 + begin + TILE - 1, lengths)
            some = (block < me) & (key0 + BLOCK > low)
            every = key0 >= high

            def run(masked):
                keys = kv[0]
                ext = jnp.concatenate([kv[1], ones], axis=1)
                mask = None
                if masked:
                    starts = first_key(
                        row0 + begin + lax.broadcasted_iota(jnp.int32, (TILE, HD), 0), lengths
                    )
                    starts = jnp.concatenate([starts] * (BLOCK // HD), axis=1)
                    k_pos = key0 + lax.broadcasted_iota(jnp.int32, (TILE, BLOCK), 1)
                    mask = k_pos >= starts
                for h in range(PER_GROUP):
                    weigh(rows, h, keys, ext, mask, False)

            pl.when(some & every)(functools.partial(run, False))
            pl.when(some & jnp.logical_not(every))(functools.partial(run, True))
            return carry

        lax.fori_loop(0, BLOCK // TILE, one_tile, 0)

    for (back, flip), kv in zip(slots, kv_refs):
        if back == 0 and flip == 0:
            own_block(kv)
        else:
            other_block(kv, me - place - back * PLANE + (place ^ flip))

    if last:
        normed = acc_ref[...] / l_ref[...]
        out_ref[...] = normed
        half_ref[...] = normed.astype(BF16)
        at = lax.broadcasted_iota(jnp.int32, (PLANE * GROUP, BLOCK), 1) + row0
        chosen = jnp.where(rows_ref[...] == at, 1.0, 0.0).astype(BF16)
        got = jnp.dot(chosen, half_ref[...], preferred_element_type=F32).astype(BF16)
        keep_ref[...] = got[:GROUP]
        pass_ref[...] = got[GROUP : 2 * GROUP]
        send_ref[...] = got[2 * GROUP :]


def attend(slots, me, lengths, queries, kvs, state, rows):
    first, last = state is None, rows is not None
    heads = jax.ShapeDtypeStruct((BLOCK, PER_GROUP * HD), F32)
    operands = [me, lengths, queries, *kvs]
    specs = [SMEM, SMEM] + [VMEM] * (1 + len(kvs))
    if last:
        operands.append(rows)
        specs.append(VMEM)
    aliases = {}
    if not first:
        if not last:
            aliases = {len(operands) + k: k for k in range(3)}
        operands += state
        specs += [VMEM] * 3
    scratch = []
    if last:
        shapes = (
            heads,
            jax.ShapeDtypeStruct((GROUP, PER_GROUP * HD), BF16),
            jax.ShapeDtypeStruct((GROUP, PER_GROUP * HD), BF16),
            jax.ShapeDtypeStruct((2 * GROUP, PER_GROUP * HD), BF16),
        )
        scratch = [pltpu.VMEM((BLOCK, PER_GROUP * HD), F32)] * 3
        scratch.append(pltpu.VMEM((BLOCK, PER_GROUP * HD), BF16))
    else:
        shapes = (heads,) * 3
    work = PER_GROUP * BLOCK * BLOCK * len(slots)
    return pl.pallas_call(
        functools.partial(attend_kernel, slots, first, last),
        out_shape=shapes,
        in_specs=specs,
        out_specs=[VMEM] * len(shapes),
        scratch_shapes=scratch,
        input_output_aliases=aliases,
        compiler_params=pltpu.CompilerParams(vmem_limit_bytes=32 << 20),
        cost_estimate=pl.CostEstimate(
            flops=4 * HD * work, bytes_accessed=4 << 20, transcendentals=work
        ),
        name="attend_%d" % len(slots),
    )(*operands)


def small_call(kernel, shape, operands, specs=None, **kw):
    return pl.pallas_call(
        kernel,
        out_shape=shape,
        in_specs=specs or [VMEM] * len(operands),
        out_specs=jax.tree.map(lambda _: VMEM, shape),
        compiler_params=pltpu.CompilerParams(vmem_limit_bytes=24 << 20),
        **kw,
    )(*operands)


def project_kernel(got_ref, *refs):
    packs, out_ref = refs[:-1], refs[-1]
    got = got_ref[0].astype(F32)
    for k in range(1, Z):
        got = got + got_ref[k].astype(F32)
    got = got.astype(BF16)
    for k, pack in enumerate(packs):
        part = jnp.dot(got, pack[:BLOCK, :], preferred_element_type=F32)
        out_ref[:, k * 256 : (k + 1) * 256] = part.astype(BF16)


def inner_kernel(me_ref, mine_ref, other_ref, *refs):
    packs, out_ref = refs[:-1], refs[-1]
    place = me_ref[0] % PLANE
    at = pl.multiple_of(BLOCK + 4 * 256 + place * GROUP, GROUP)
    streams = []
    for k, pack in enumerate(packs):
        cols = slice(k * 256, (k + 1) * 256)
        total = mine_ref[:, cols].astype(F32) + other_ref[:, cols].astype(F32)
        streams.append((pack[pl.ds(at, GROUP), :].astype(F32) + total).astype(BF16))
    for n in range(4):
        inner = jnp.zeros((GROUP, 256), F32)
        for stream, pack in zip(streams, packs):
            weight = pack[BLOCK + n * 256 : BLOCK + (n + 1) * 256, :]
            inner = inner + jnp.dot(stream, weight, preferred_element_type=F32)
        out_ref[:, n * 256 : (n + 1) * 256] = inner.astype(BF16)


def hidden_kernel(me_ref, got_ref, class_ref, out_ref):
    inner = got_ref[0].astype(F32)
    for k in range(1, Z):
        inner = inner + got_ref[k].astype(F32)
    hidden = jnp.maximum(inner, 0.0).astype(BF16)
    logits = jnp.dot(hidden, class_ref[...], preferred_element_type=F32)
    gap = logits[:, 1:2] - logits[:, 0:1]
    lane = lax.broadcasted_iota(jnp.int32, (PAD, HD), 1)
    mine = jnp.where(lane == me_ref[0], gap, 0.0)
    for k in range(out_ref.shape[0]):
        out_ref[k] = mine


def vote_kernel(prompts, clusters, got_ref, scores_ref, votes_ref):
    gap = jnp.sum(got_ref[...], axis=0)
    scores = 1.0 / (1.0 + jnp.exp(-gap))
    scores_ref[...] = scores[:TRACES, :STEPS]
    lane = lax.broadcasted_iota(jnp.int32, (PAD, HD), 1)
    chain = jnp.min(jnp.where(lane < STEPS, scores, 2.0), axis=1, keepdims=True)
    prompt = lax.broadcasted_iota(jnp.int32, (PROMPTS, CLUSTERS), 0)
    cluster = lax.broadcasted_iota(jnp.int32, (PROMPTS, CLUSTERS), 1)
    votes = jnp.zeros((PROMPTS, CLUSTERS), F32)
    for t in range(TRACES):
        here = (prompt == prompts[t]) & (cluster == clusters[t])
        votes = votes + jnp.where(here, chain[t : t + 1, :], 0.0)
    votes_ref[...] = votes


def swapped(value, axis, bit):
    count = lax.axis_size(axis)
    return lax.ppermute(value, axis, [(s, s ^ bit) for s in range(count)])


def raised(value):
    count = lax.axis_size("ctx")
    return lax.ppermute(value, "ctx", [(s, (s + PLANE) % count) for s in range(count)])


def per_device(
    queries,
    keys_values,
    trace_lengths,
    step_rows,
    prompt_ids,
    cluster_ids,
    step_stream,
    out_weight,
    score_weight,
    class_weight,
):
    here = lax.axis_index("ctx").astype(jnp.int32)
    core, side = here % 2, (here // 2) % 2
    me = here.reshape(1)
    columns = [[PLANE * z + j for z in range(Z)] for j in range(PLANE)]

    kv0 = keys_values
    kv1 = raised(kv0)
    across0 = swapped(kv0, "ctx", 2)
    core0 = swapped(kv0, "ctx", 1)
    kv2 = raised(kv1)
    across1 = swapped(kv1, "ctx", 2)
    core0y = swapped(across0, "ctx", 1)
    core1 = swapped(kv1, "ctx", 1)
    across2 = swapped(kv2, "ctx", 2)
    core1y = swapped(across1, "ctx", 1)
    core2 = swapped(kv2, "ctx", 1)
    core2y = swapped(across2, "ctx", 1)

    wanted = step_rows.reshape(TRACES, Z, 2, 2).transpose(3, 2, 1, 0)
    wanted = jnp.pad(wanted, ((0, 0), (0, 0), (0, 0), (0, PAD - TRACES)), constant_values=-1)
    wanted = jnp.where(core == 1, wanted[::-1], wanted)
    wanted = jnp.where(side == 1, wanted[:, ::-1], wanted)
    wanted = wanted.reshape(PLANE * GROUP, 1)

    stream = step_stream.reshape(TRACES, Z, PLANE, 256).transpose(2, 1, 0, 3)
    stream = jnp.pad(stream, ((0, 0), (0, 0), (0, PAD - TRACES), (0, 0)))
    pack = jnp.concatenate(
        [out_weight]
        + [score_weight[:, n * 256 : (n + 1) * 256] for n in range(4)]
        + [stream.reshape(PLANE * GROUP, 256)],
        axis=0,
    )
    pack, across2 = lax.optimization_barrier((pack, across2))
    packs = [pack, swapped(pack, "ctx", 1), swapped(pack, "ctx", 2)]
    packs.append(swapped(packs[2], "ctx", 1))

    state = attend([(0, 0), (0, 1)], me, trace_lengths, queries, [kv0, core0], None, None)
    state = attend(
        [(0, 2), (0, 3), (1, 0), (1, 1)],
        me,
        trace_lengths,
        queries,
        [across0, core0y, kv1, core1],
        state,
        None,
    )
    state = attend(
        [(1, 2), (1, 3), (2, 0), (2, 1)],
        me,
        trace_lengths,
        queries,
        [across1, core1y, kv2, core2],
        state,
        None,
    )
    attended, keep, passed, sent = attend(
        [(2, 2), (2, 3)], me, trace_lengths, queries, [across2, core2y], state, wanted
    )

    arrived = swapped(sent, "ctx", 1)
    across = swapped(passed + arrived[GROUP:], "ctx", 2)
    picked = keep + arrived[:GROUP] + across
    spread = jnp.broadcast_to(picked[None], (Z, GROUP, PER_GROUP * HD))
    gathered = lax.all_to_all(spread, "ctx", 0, 0, axis_index_groups=columns)

    projected = small_call(
        project_kernel, jax.ShapeDtypeStruct((GROUP, WIDE), BF16), [gathered, *packs], name="project"
    )
    projected = projected + swapped(projected, "head", 2)
    projected = projected + swapped(projected, "head", 4)
    other = swapped(projected, "head", 1)

    inner = small_call(
        inner_kernel,
        jax.ShapeDtypeStruct((GROUP, WIDE), BF16),
        [me, projected, other, *packs],
        [SMEM] + [VMEM] * 6,
        name="inner",
    )
    inner = lax.all_to_all(
        inner.reshape(Z, PAD, WIDE), "ctx", 0, 0, axis_index_groups=columns
    )
    heads, count = lax.axis_size("head"), lax.axis_size("ctx")
    gap = small_call(
        hidden_kernel,
        jax.ShapeDtypeStruct((heads, PAD, HD), F32),
        [me, inner, class_weight],
        [SMEM, VMEM, VMEM],
        name="hidden",
    )
    gap = jnp.sum(lax.all_to_all(gap, "head", 0, 0), axis=0)
    gap = lax.all_to_all(jnp.broadcast_to(gap[None], (count, PAD, HD)), "ctx", 0, 0)
    step_scores, votes = small_call(
        vote_kernel,
        (
            jax.ShapeDtypeStruct((TRACES, STEPS), F32),
            jax.ShapeDtypeStruct((PROMPTS, CLUSTERS), F32),
        ),
        [prompt_ids, cluster_ids, gap],
        [SMEM, SMEM, VMEM],
        name="vote",
    )
    return (attended, step_scores, votes)


def solution(mesh):
    placed = (
        P("ctx", "head"),
        P(None, "ctx", "head"),
        P(),
        P(),
        P(),
        P(),
        P(None, "ctx"),
        P("head", "ctx"),
        P("ctx", "head"),
        P("head", None),
    )
    return jax.shard_map(
        per_device,
        mesh=mesh,
        in_specs=placed,
        out_specs=(P("ctx", "head"), P(), P()),
        check_vma=False,
    )
```

```python
import functools
import math

import jax
import jax.numpy as jnp
from jax import lax
from jax.experimental import pallas as pl
from jax.experimental.pallas import tpu as pltpu
from jax.sharding import PartitionSpec as P

HD = 128
PROMPTS = 2
CLUSTERS = 4
TRACES = 7
STEPS = 32
PER_GROUP = 4
BLOCK = 512
TILE = 256
Z = 8
PLANE = 4
PAD = 8
GROUP = Z * PAD
WIDE = 1024
COEF = HD**-0.5 * math.log2(math.e)
LOW = -1e30
NONE = -60000.0
VMEM = pl.BlockSpec(memory_space=pltpu.VMEM)
SMEM = pl.BlockSpec(memory_space=pltpu.SMEM)
BF16 = jnp.bfloat16
F32 = jnp.float32


def first_key(row, lengths):
    start = row * 0
    end = jnp.int32(0)
    for t in range(TRACES):
        end = end + lengths[t]
        start = jnp.where(row >= end, end, start)
    return start


def pick_kernel(me_ref, steps_ref, q_ref, keep_ref, pass_ref, send_ref, all_ref):
    me = me_ref[0]
    core, side = me % 2, (me // 2) % 2
    at = lax.broadcasted_iota(jnp.int32, (TRACES, BLOCK), 1) + me * BLOCK
    none = jnp.zeros((PAD - TRACES, BLOCK), F32)
    steps = steps_ref[...]
    for c in range(2):
        for y in range(2):
            parts = []
            for z in range(Z):
                step = PLANE * z + 2 * y + c
                parts.append(jnp.where(steps[:, step : step + 1] == at, 1.0, 0.0))
                parts.append(none)
            chosen = jnp.concatenate(parts, axis=0).astype(BF16)
            got = jnp.dot(chosen, q_ref[...], preferred_element_type=F32)
            all_ref[pl.ds((2 * c + y) * GROUP, GROUP), :] = got.astype(BF16)

    def group(c, y):
        return all_ref[pl.ds(pl.multiple_of((2 * c + y) * GROUP, GROUP), GROUP), :]

    keep_ref[...] = group(core, side)
    pass_ref[...] = group(core, 1 - side)
    send_ref[:GROUP] = group(1 - core, side)
    send_ref[GROUP:] = group(1 - core, 1 - side)


def picked_kernel(me_ref, lengths, steps_ref, q_ref, *refs):
    kv_refs, out_ref = refs[:PLANE], refs[PLANE]
    me = me_ref[0]
    place = me % PLANE
    steps = steps_ref[...]
    lane = lax.broadcasted_iota(jnp.int32, (TRACES, STEPS), 1)
    none = jnp.full((PAD - TRACES, HD), -1, jnp.int32)
    parts = []
    for z in range(Z):
        mine = jnp.where(lane == PLANE * z + place, steps, 0)
        mine = jnp.sum(mine, axis=1, keepdims=True)
        parts.append(jnp.broadcast_to(mine, (TRACES, HD)))
        parts.append(none)
    row = jnp.concatenate(parts, axis=0)
    start = first_key(row, lengths)
    row = jnp.concatenate([row] * (BLOCK // HD), axis=1)
    start = jnp.concatenate([start] * (BLOCK // HD), axis=1)
    masks = []
    for k in range(PLANE):
        key0 = (me - place + (place ^ k)) * BLOCK
        k_pos = key0 + lax.broadcasted_iota(jnp.int32, (GROUP, BLOCK), 1)
        masks.append((k_pos <= row) & (k_pos >= start))
    q = q_ref[0].astype(F32)
    for z in range(1, Z):
        q = q + q_ref[z].astype(F32)
    q = q.astype(BF16)
    lanes = lax.broadcasted_iota(jnp.int32, (GROUP, HD), 1)
    stats = jnp.zeros((GROUP, HD), F32)
    ones = jnp.ones((BLOCK, HD), BF16)
    for h in range(PER_GROUP):
        mine = q[:, h * HD : (h + 1) * HD]
        scores = []
        for kv, mask in zip(kv_refs, masks):
            s = lax.dot_general(
                mine, kv[0], (((1,), (1,)), ((), ())), preferred_element_type=F32
            )
            scores.append(jnp.where(mask, s, LOW))
        top = jnp.maximum(
            jnp.maximum(scores[0], scores[1]), jnp.maximum(scores[2], scores[3])
        )
        top = jnp.maximum(jnp.max(top, axis=1, keepdims=True), 0.1 * LOW)
        pv = jnp.zeros((GROUP, 2 * HD), F32)
        for kv, s in zip(kv_refs, scores):
            p = jnp.exp2((s - top) * COEF).astype(BF16)
            pv = pv + jnp.dot(
                p, jnp.concatenate([kv[1], ones], axis=1), preferred_element_type=F32
            )
        total = pv[:, HD:]
        some = total > 0.0
        total = jnp.where(some, total, 1.0)
        out_ref[:, h * HD : (h + 1) * HD] = pv[:, :HD] / total
        size = jnp.where(some, top * COEF + jnp.log2(total), NONE)
        for k in range(3):
            coarse = size.astype(BF16).astype(F32)
            stats = jnp.where(lanes == PER_GROUP * k + h, coarse, stats)
            size = size - coarse
    out_ref[:, PER_GROUP * HD :] = stats


def attend_kernel(slots, first, last, *refs):
    me_ref, lengths, q_ref = refs[:3]
    kv_refs = refs[3 : 3 + len(slots)]
    if last:
        m_ref, l_ref, acc_ref, out_ref = refs[-4:]
    else:
        m_ref, l_ref, acc_ref = refs[-3:]
    me = me_ref[0]
    place = me % PLANE
    row0 = me * BLOCK
    ones = jnp.ones((BLOCK, HD), BF16)

    def weigh(rows, h, keys, ext, mask, fresh):
        cols = slice(h * HD, (h + 1) * HD)
        s = lax.dot_general(
            q_ref[rows, cols], keys, (((1,), (1,)), ((), ())), preferred_element_type=F32
        )
        if mask is not None:
            s = jnp.where(mask, s, LOW)
        top = jnp.max(s, axis=1, keepdims=True)
        if fresh:
            top = jnp.broadcast_to(top, (TILE, HD))
        else:
            before = m_ref[rows, cols]
            top = jnp.maximum(before, top)
        wide = jnp.concatenate([top] * (s.shape[1] // HD), axis=1)
        p = jnp.exp2((s - wide) * COEF).astype(BF16)
        pv = jnp.dot(p, ext, preferred_element_type=F32)
        m_ref[rows, cols] = top
        if fresh:
            acc_ref[rows, cols] = pv[:, :HD]
            l_ref[rows, cols] = pv[:, HD:]
        else:
            scale = jnp.exp2((before - top) * COEF)
            acc_ref[rows, cols] = acc_ref[rows, cols] * scale + pv[:, :HD]
            l_ref[rows, cols] = l_ref[rows, cols] * scale + pv[:, HD:]

    def own_block(kv):
        for tile in range(BLOCK // TILE):
            width = (tile + 1) * TILE
            rows = slice(tile * TILE, width)
            keys = kv[0, :width, :]
            ext = jnp.concatenate([kv[1, :width, :], ones[:width]], axis=1)
            q_pos = row0 + tile * TILE + lax.broadcasted_iota(jnp.int32, (TILE, width), 0)
            k_pos = row0 + lax.broadcasted_iota(jnp.int32, (TILE, width), 1)
            starts = first_key(
                row0 + tile * TILE + lax.broadcasted_iota(jnp.int32, (TILE, HD), 0), lengths
            )
            starts = jnp.concatenate([starts] * (width // HD), axis=1)
            mask = (k_pos <= q_pos) & (k_pos >= starts)
            for h in range(PER_GROUP):
                weigh(rows, h, keys, ext, mask, True)

    def other_block(kv, block):
        key0 = block * BLOCK

        def one_tile(tile, carry):
            begin = pl.multiple_of(tile * TILE, TILE)
            rows = pl.ds(begin, TILE)
            low = first_key(row0 + begin, lengths)
            high = first_key(row0 + begin + TILE - 1, lengths)
            some = (block < me) & (key0 + BLOCK > low)
            every = key0 >= high

            def run(masked):
                keys = kv[0]
                ext = jnp.concatenate([kv[1], ones], axis=1)
                mask = None
                if masked:
                    starts = first_key(
                        row0 + begin + lax.broadcasted_iota(jnp.int32, (TILE, HD), 0), lengths
                    )
                    starts = jnp.concatenate([starts] * (BLOCK // HD), axis=1)
                    k_pos = key0 + lax.broadcasted_iota(jnp.int32, (TILE, BLOCK), 1)
                    mask = k_pos >= starts
                for h in range(PER_GROUP):
                    weigh(rows, h, keys, ext, mask, False)

            pl.when(some & every)(functools.partial(run, False))
            pl.when(some & jnp.logical_not(every))(functools.partial(run, True))
            return carry

        lax.fori_loop(0, BLOCK // TILE, one_tile, 0)

    for (back, flip), kv in zip(slots, kv_refs):
        if back == 0 and flip == 0:
            own_block(kv)
        else:
            other_block(kv, me - place - back * PLANE + (place ^ flip))

    if last:
        out_ref[...] = acc_ref[...] / l_ref[...]


def attend(slots, me, lengths, queries, kvs, state, last=False):
    heads = jax.ShapeDtypeStruct((BLOCK, PER_GROUP * HD), F32)
    operands = [me, lengths, queries, *kvs]
    aliases = {}
    if state is not None:
        aliases = {len(operands) + k: k for k in range(3)}
        operands += state
    shapes = (heads,) * (4 if last else 3)
    work = PER_GROUP * BLOCK * BLOCK * len(slots)
    got = pl.pallas_call(
        functools.partial(attend_kernel, slots, state is None, last),
        out_shape=shapes,
        in_specs=[SMEM, SMEM] + [VMEM] * (len(operands) - 2),
        out_specs=[VMEM] * len(shapes),
        input_output_aliases=aliases,
        compiler_params=pltpu.CompilerParams(vmem_limit_bytes=24 << 20),
        cost_estimate=pl.CostEstimate(
            flops=4 * HD * work, bytes_accessed=4 << 20, transcendentals=work
        ),
        name="attend_%d_%d" % slots[0],
    )(*operands)
    return got[3] if last else got


def small_call(kernel, shape, operands, specs=None, **kw):
    return pl.pallas_call(
        kernel,
        out_shape=shape,
        in_specs=specs or [VMEM] * len(operands),
        out_specs=jax.tree.map(lambda _: VMEM, shape),
        compiler_params=pltpu.CompilerParams(vmem_limit_bytes=24 << 20),
        **kw,
    )(*operands)


def project_kernel(got_ref, *refs):
    packs, out_ref = refs[:-1], refs[-1]
    picked = []
    for h in range(PER_GROUP):
        sizes = []
        for z in range(Z):
            at = PER_GROUP * HD + h
            size = got_ref[z, :, at : at + 1]
            for k in range(1, 3):
                size = size + got_ref[z, :, at + PER_GROUP * k : at + PER_GROUP * k + 1]
            sizes.append(size)
        top = functools.reduce(jnp.maximum, sizes)
        total = jnp.zeros((GROUP, 1), F32)
        joined = jnp.zeros((GROUP, HD), F32)
        for z in range(Z):
            weight = jnp.exp2(sizes[z] - top)
            total = total + weight
            joined = joined + got_ref[z, :, h * HD : (h + 1) * HD] * weight
        picked.append((joined / total).astype(BF16))
    picked = jnp.concatenate(picked, axis=1)
    for k, pack in enumerate(packs):
        part = jnp.dot(picked, pack[:BLOCK, :], preferred_element_type=F32)
        out_ref[:, k * 256 : (k + 1) * 256] = part


def inner_kernel(me_ref, total_ref, *refs):
    packs, weights, out_ref = refs[:PLANE], refs[PLANE : 2 * PLANE], refs[-1]
    place = me_ref[0] % PLANE
    slot = lax.broadcasted_iota(jnp.int32, (GROUP, TRACES * STEPS), 0)
    at = lax.broadcasted_iota(jnp.int32, (GROUP, TRACES * STEPS), 1)
    trace = slot & (PAD - 1)
    wanted = trace * STEPS + PLANE * (slot >> 3) + place
    chosen = jnp.where((at == wanted) & (trace < TRACES), 1.0, 0.0).astype(BF16)
    inner = jnp.zeros((GROUP, WIDE), F32)
    for k, (pack, weight) in enumerate(zip(packs, weights)):
        base = jnp.dot(chosen, pack[BLOCK:, :], preferred_element_type=F32)
        stream = (base + total_ref[:, k * 256 : (k + 1) * 256]).astype(BF16)
        inner = inner + jnp.dot(stream, weight[...], preferred_element_type=F32)
    out_ref[...] = inner


def hidden_kernel(me_ref, inner_ref, class_ref, out_ref):
    hidden = jnp.maximum(inner_ref[...], 0.0).astype(BF16)
    logits = jnp.dot(hidden, class_ref[...], preferred_element_type=F32)
    gap = logits[:, 1:2] - logits[:, 0:1]
    lane = lax.broadcasted_iota(jnp.int32, (PAD, HD), 1)
    mine = jnp.where(lane == me_ref[0], gap, 0.0)
    for k in range(out_ref.shape[0]):
        out_ref[k] = mine


def vote_kernel(prompts, clusters, got_ref, scores_ref, votes_ref):
    gap = jnp.sum(got_ref[...], axis=0)
    scores = 1.0 / (1.0 + jnp.exp(-gap))
    scores_ref[...] = scores[:TRACES, :STEPS]
    lane = lax.broadcasted_iota(jnp.int32, (PAD, HD), 1)
    chain = jnp.min(jnp.where(lane < STEPS, scores, 2.0), axis=1, keepdims=True)
    prompt = lax.broadcasted_iota(jnp.int32, (PROMPTS, CLUSTERS), 0)
    cluster = lax.broadcasted_iota(jnp.int32, (PROMPTS, CLUSTERS), 1)
    votes = jnp.zeros((PROMPTS, CLUSTERS), F32)
    for t in range(TRACES):
        here = (prompt == prompts[t]) & (cluster == clusters[t])
        votes = votes + jnp.where(here, chain[t : t + 1, :], 0.0)
    votes_ref[...] = votes


def swapped(value, axis, bit):
    count = lax.axis_size(axis)
    return lax.ppermute(value, axis, [(s, s ^ bit) for s in range(count)])


def raised(value):
    count = lax.axis_size("ctx")
    return lax.ppermute(value, "ctx", [(s, (s + PLANE) % count) for s in range(count)])


def per_device(
    queries,
    keys_values,
    trace_lengths,
    step_rows,
    prompt_ids,
    cluster_ids,
    step_stream,
    out_weight,
    score_weight,
    class_weight,
):
    me = lax.axis_index("ctx").astype(jnp.int32).reshape(1)
    columns = [[PLANE * z + j for z in range(Z)] for j in range(PLANE)]
    tie = lambda *values: lax.optimization_barrier(values)
    add = functools.partial(attend, me=me, lengths=trace_lengths, queries=queries)

    kv0 = keys_values
    core0 = swapped(kv0, "ctx", 1)
    kv1 = raised(kv0)

    half = PER_GROUP * HD
    keep, passed, sent = small_call(
        pick_kernel,
        tuple(jax.ShapeDtypeStruct((n * GROUP, half), BF16) for n in (1, 1, 2)),
        [me, step_rows, queries],
        [SMEM, VMEM, VMEM],
        scratch_shapes=[pltpu.VMEM((PLANE * GROUP, half), BF16)],
        name="pick",
    )
    arrived = swapped(sent, "ctx", 1)
    arrived, own_kv = tie(arrived, kv0)
    state = add([(0, 0)], kvs=[own_kv], state=None)
    across = swapped(passed + arrived[GROUP:], "ctx", 2)
    wanted = keep + arrived[:GROUP] + across
    wanted, state, kv0y = tie(wanted, state, kv0)
    across0 = swapped(kv0y, "ctx", 2)
    core0y = swapped(across0, "ctx", 1)
    wanted = jnp.broadcast_to(wanted[None], (Z, GROUP, half))
    wanted = lax.all_to_all(wanted, "ctx", 0, 0, axis_index_groups=columns)

    pack = jnp.concatenate([out_weight, step_stream], axis=0)
    pack, across0 = tie(pack, across0)
    packs = [pack, swapped(pack, "ctx", 1), swapped(pack, "ctx", 2)]
    packs.append(swapped(packs[2], "ctx", 1))

    parts = small_call(
        picked_kernel,
        jax.ShapeDtypeStruct((GROUP, half + HD), F32),
        [me, trace_lengths, step_rows, wanted, kv0, core0, across0, core0y],
        [SMEM, SMEM] + [VMEM] * 6,
        name="picked",
    )
    parts, state, kv1, core0, packs[2] = tie(parts, state, kv1, core0, packs[2])
    weight, _ = tie(score_weight, packs[2])
    weights = [weight, swapped(weight, "ctx", 1), swapped(weight, "ctx", 2)]
    weights.append(swapped(weights[2], "ctx", 1))
    core1 = swapped(kv1, "ctx", 1)
    state = add([(0, 1)], kvs=[core0], state=state)
    state = add([(0, 2), (0, 3)], kvs=[across0, core0y], state=state)
    parts = jnp.broadcast_to(parts.astype(jnp.float16)[None], (Z, GROUP, half + HD))
    parts = lax.all_to_all(parts, "ctx", 0, 0, axis_index_groups=columns).astype(F32)
    parts, state, kv1, weights[2] = tie(parts, state, kv1, weights[2])

    projected = small_call(
        project_kernel, jax.ShapeDtypeStruct((GROUP, WIDE), F32), [parts, *packs], name="project"
    )
    projected, kv1 = tie((projected * 0.25).astype(jnp.float16), kv1)
    kv2 = raised(kv1)
    across1 = swapped(kv1, "ctx", 2)
    core1y = swapped(across1, "ctx", 1)
    state = add([(1, 0)], kvs=[kv1], state=state)
    other = swapped(projected, "head", 2)
    other, state, core1 = tie(other, state, core1)
    projected = projected + other
    state = add([(1, 1)], kvs=[core1], state=state)
    other = swapped(projected, "head", 4)
    other, state, across1, kv2 = tie(other, state, across1, kv2)
    projected = projected + other
    across2 = swapped(kv2, "ctx", 2)
    core2 = swapped(kv2, "ctx", 1)
    core2y = swapped(across2, "ctx", 1)
    state = add([(1, 2)], kvs=[across1], state=state)
    other = swapped(projected, "head", 1)
    other, state, core1y = tie(other, state, core1y)
    projected = (projected.astype(F32) + other.astype(F32)) * 4.0

    inner = small_call(
        inner_kernel,
        jax.ShapeDtypeStruct((GROUP, WIDE), F32),
        [me, projected, *packs, *weights],
        [SMEM] + [VMEM] * 9,
        name="inner",
    )
    inner, state = tie(inner, state)
    inner = (inner * 2.0**-10).astype(jnp.float16).reshape(Z, PAD, WIDE)
    state = add([(1, 3), (2, 0)], kvs=[core1y, kv2], state=state)
    inner = lax.all_to_all(inner, "ctx", 0, 0, axis_index_groups=columns)
    inner, state, core2 = tie(inner, state, core2)
    inner = jnp.sum(inner.astype(F32), axis=0) * 2.0**10
    heads, count = lax.axis_size("head"), lax.axis_size("ctx")
    gap = small_call(
        hidden_kernel,
        jax.ShapeDtypeStruct((heads, PAD, HD), F32),
        [me, inner, class_weight],
        [SMEM, VMEM, VMEM],
        name="hidden",
    )
    gap, state, across2 = tie(gap, state, across2)
    state = add([(2, 1), (2, 2)], kvs=[core2, across2], state=state)
    gap = lax.all_to_all(gap, "head", 0, 0)
    gap, state, core2y = tie(gap, state, core2y)
    gap = jnp.sum(gap, axis=0)
    attended = add([(2, 3)], kvs=[core2y], state=state, last=True)
    gap = lax.all_to_all(jnp.broadcast_to(gap[None], (count, PAD, HD)), "ctx", 0, 0)
    step_scores, votes = small_call(
        vote_kernel,
        (
            jax.ShapeDtypeStruct((TRACES, STEPS), F32),
            jax.ShapeDtypeStruct((PROMPTS, CLUSTERS), F32),
        ),
        [prompt_ids, cluster_ids, gap],
        [SMEM, SMEM, VMEM],
        name="vote",
    )
    return (attended, step_scores, votes)


def solution(mesh):
    placed = (
        P("ctx", "head"),
        P(None, "ctx", "head"),
        P(),
        P(),
        P(),
        P(),
        P(None, "ctx"),
        P("head", "ctx"),
        P("ctx", "head"),
        P("head", None),
    )
    return jax.shard_map(
        per_device,
        mesh=mesh,
        in_specs=placed,
        out_specs=(P("ctx", "head"), P(), P()),
        check_vma=False,
    )
```

```python
import functools
import math

import jax
import jax.numpy as jnp
from jax import lax
from jax.experimental import pallas as pl
from jax.experimental.pallas import tpu as pltpu
from jax.sharding import PartitionSpec as P

HD = 128
PROMPTS = 2
CLUSTERS = 4
TRACES = 7
STEPS = 32
PER_GROUP = 4
BLOCK = 512
TILE = 256
Z = 8
PLANE = 4
PAD = 8
GROUP = Z * PAD
WIDE = 1024
COEF = HD**-0.5 * math.log2(math.e)
LOW = -1e30
NONE = -60000.0
VMEM = pl.BlockSpec(memory_space=pltpu.VMEM)
SMEM = pl.BlockSpec(memory_space=pltpu.SMEM)
ANY = pl.BlockSpec(memory_space=pl.ANY)
BF16 = jnp.bfloat16
F32 = jnp.float32


def first_key(row, lengths):
    start = row * 0
    end = jnp.int32(0)
    for t in range(TRACES):
        end = end + lengths[t]
        start = jnp.where(row >= end, end, start)
    return start


def pick_kernel(me_ref, steps_ref, q_ref, keep_ref, pass_ref, send_ref, all_ref):
    me = me_ref[0]
    core, side = me % 2, (me // 2) % 2
    at = lax.broadcasted_iota(jnp.int32, (TRACES, BLOCK), 1) + me * BLOCK
    none = jnp.zeros((PAD - TRACES, BLOCK), F32)
    steps = steps_ref[...]
    for c in range(2):
        for y in range(2):
            parts = []
            for z in range(Z):
                step = PLANE * z + 2 * y + c
                parts.append(jnp.where(steps[:, step : step + 1] == at, 1.0, 0.0))
                parts.append(none)
            chosen = jnp.concatenate(parts, axis=0).astype(BF16)
            got = jnp.dot(chosen, q_ref[...], preferred_element_type=F32)
            all_ref[pl.ds((2 * c + y) * GROUP, GROUP), :] = got.astype(BF16)

    def group(c, y):
        return all_ref[pl.ds(pl.multiple_of((2 * c + y) * GROUP, GROUP), GROUP), :]

    keep_ref[...] = group(core, side)
    pass_ref[...] = group(core, 1 - side)
    send_ref[:GROUP] = group(1 - core, side)
    send_ref[GROUP:] = group(1 - core, 1 - side)


def picked_kernel(me_ref, lengths, steps_ref, q_ref, q1_ref, q2_ref, *refs):
    kv_refs, out_ref, kv_s, sems = refs[:PLANE], refs[PLANE], refs[-2], refs[-1]
    copies = [
        pltpu.make_async_copy(kv, kv_s.at[k], sems.at[k]) for k, kv in enumerate(kv_refs)
    ]
    for copy in copies:
        copy.start()
    me = me_ref[0]
    place = me % PLANE
    steps = steps_ref[...]
    lane = lax.broadcasted_iota(jnp.int32, (TRACES, STEPS), 1)
    none = jnp.full((PAD - TRACES, HD), -1, jnp.int32)
    parts = []
    for z in range(Z):
        mine = jnp.where(lane == PLANE * z + place, steps, 0)
        mine = jnp.sum(mine, axis=1, keepdims=True)
        parts.append(jnp.broadcast_to(mine, (TRACES, HD)))
        parts.append(none)
    row = jnp.concatenate(parts, axis=0)
    start = first_key(row, lengths)
    row = jnp.concatenate([row] * (BLOCK // HD), axis=1)
    start = jnp.concatenate([start] * (BLOCK // HD), axis=1)
    k_pos = lax.broadcasted_iota(jnp.int32, (GROUP, BLOCK), 1)
    q = (q_ref[...].astype(F32) + q1_ref[...].astype(F32) + q2_ref[...].astype(F32)).astype(BF16)
    q = jnp.concatenate([q[:, h * HD : (h + 1) * HD] for h in range(PER_GROUP)], axis=0)
    scores = []
    for k in range(PLANE):
        key0 = (me - place + (place ^ k)) * BLOCK
        mask = (k_pos <= row - key0) & (k_pos >= start - key0)
        mask = jnp.concatenate([mask] * PER_GROUP, axis=0)
        copies[k].wait()
        s = lax.dot_general(
            q, kv_s[k, 0], (((1,), (1,)), ((), ())), preferred_element_type=F32
        )
        scores.append(jnp.where(mask, s, LOW))
    top = jnp.maximum(jnp.maximum(scores[0], scores[1]), jnp.maximum(scores[2], scores[3]))
    top = jnp.maximum(jnp.max(top, axis=1, keepdims=True), 0.1 * LOW)
    ones = jnp.ones((BLOCK, HD), BF16)
    pv = jnp.zeros((PER_GROUP * GROUP, 2 * HD), F32)
    for k, s in enumerate(scores):
        p = jnp.exp2((s - top) * COEF).astype(BF16)
        ext = jnp.concatenate([kv_s[k, 1], ones], axis=1)
        pv = pv + jnp.dot(p, ext, preferred_element_type=F32)
    total = pv[:, HD:]
    some = total > 0.0
    total = jnp.where(some, total, 1.0)
    value = pv[:, :HD] / total
    size = jnp.where(some, top * COEF + jnp.log2(total), NONE)
    lanes = lax.broadcasted_iota(jnp.int32, (GROUP, HD), 1)
    stats = jnp.zeros((GROUP, HD), F32)
    for h in range(PER_GROUP):
        rows = slice(h * GROUP, (h + 1) * GROUP)
        out_ref[:, h * HD : (h + 1) * HD] = value[rows]
        rest = size[rows]
        for k in range(3):
            coarse = rest.astype(BF16).astype(F32)
            stats = jnp.where(lanes == PER_GROUP * k + h, coarse, stats)
            rest = rest - coarse
    for z in range(Z):
        packed = jnp.zeros((1, HD), F32)
        for t in range(TRACES):
            at = z * PAD + t
            packed = packed + pltpu.roll(stats[at : at + 1], 16 * t, 1)
        out_ref[z * PAD + TRACES : (z + 1) * PAD, :HD] = packed


def attend_kernel(slots, first, last, *refs):
    n = len(slots)
    me_ref, lengths, q_hbm = refs[:3]
    kv_hbm = refs[3 : 3 + n]
    if last:
        out_hbm = refs[-8]
    else:
        acc_hbm, ml_hbm = refs[-9:-7]
    if not first:
        acc_in, ml_in = refs[3 + n : 5 + n]
    q_ref, kv_ref, acc_ref, m_ref, l_ref, ml_ref, sems = refs[-7:]
    me = me_ref[0]
    place = me % PLANE
    row0 = me * BLOCK
    ones = jnp.ones((BLOCK, HD), BF16)
    blocks = [me - place - back * PLANE + (place ^ flip) for back, flip in slots]
    earliest = first_key(row0, lengths)
    active = [(block < me) & ((block + 1) * BLOCK > earliest) for block in blocks]

    def copy_in(source, target, k):
        return pltpu.make_async_copy(source, target, sems.at[k])

    def weigh(rows, count, keys, ext, mask, fresh):
        q = q_ref[rows, :]
        q = jnp.concatenate([q[:, h * HD : (h + 1) * HD] for h in range(PER_GROUP)], axis=0)
        s = lax.dot_general(q, keys, (((1,), (1,)), ((), ())), preferred_element_type=F32)
        for h in range(PER_GROUP):
            cols = slice(h * HD, (h + 1) * HD)
            mine = s[h * count : (h + 1) * count]
            if mask is not None:
                mine = jnp.where(mask, mine, LOW)
            top = jnp.max(mine, axis=1, keepdims=True)
            if fresh:
                top = jnp.broadcast_to(top, (count, HD))
            else:
                before = m_ref[rows, cols]
                top = jnp.maximum(before, top)
            wide = jnp.concatenate([top] * (mine.shape[1] // HD), axis=1)
            p = jnp.exp2((mine - wide) * COEF).astype(BF16)
            pv = jnp.dot(p, ext, preferred_element_type=F32)
            m_ref[rows, cols] = top
            if fresh:
                acc_ref[rows, cols] = pv[:, :HD]
                l_ref[rows, cols] = pv[:, HD:]
            else:
                scale = jnp.exp2((before - top) * COEF)
                acc_ref[rows, cols] = acc_ref[rows, cols] * scale + pv[:, :HD]
                l_ref[rows, cols] = l_ref[rows, cols] * scale + pv[:, HD:]

    def own_block(kv):
        for tile in range(BLOCK // TILE):
            width = (tile + 1) * TILE
            rows = slice(tile * TILE, width)
            keys = kv[0, :width, :]
            ext = jnp.concatenate([kv[1, :width, :], ones[:width]], axis=1)
            q_pos = row0 + tile * TILE + lax.broadcasted_iota(jnp.int32, (TILE, width), 0)
            k_pos = row0 + lax.broadcasted_iota(jnp.int32, (TILE, width), 1)
            starts = first_key(
                row0 + tile * TILE + lax.broadcasted_iota(jnp.int32, (TILE, HD), 0), lengths
            )
            starts = jnp.concatenate([starts] * (width // HD), axis=1)
            mask = (k_pos <= q_pos) & (k_pos >= starts)
            weigh(rows, TILE, keys, ext, mask, True)

    def other_block(kv, block):
        key0 = block * BLOCK

        def one_tile(tile, carry):
            begin = pl.multiple_of(tile * TILE, TILE)
            rows = pl.ds(begin, TILE)
            low = first_key(row0 + begin, lengths)
            high = first_key(row0 + begin + TILE - 1, lengths)
            some = (block < me) & (key0 + BLOCK > low)
            every = key0 >= high

            def run(masked):
                keys = kv[0]
                ext = jnp.concatenate([kv[1], ones], axis=1)
                mask = None
                if masked:
                    starts = first_key(
                        row0 + begin + lax.broadcasted_iota(jnp.int32, (TILE, HD), 0), lengths
                    )
                    starts = jnp.concatenate([starts] * (BLOCK // HD), axis=1)
                    k_pos = key0 + lax.broadcasted_iota(jnp.int32, (TILE, BLOCK), 1)
                    mask = k_pos >= starts
                weigh(rows, TILE, keys, ext, mask, False)

            pl.when(some & every)(functools.partial(run, False))
            pl.when(some & jnp.logical_not(every))(functools.partial(run, True))
            return carry

        lax.fori_loop(0, BLOCK // TILE, one_tile, 0)

    def load_state():
        copies = [copy_in(acc_in, acc_ref, n), copy_in(ml_in, ml_ref, n + 1)]
        for copy in copies:
            copy.start()
        return copies

    def spread_state(copies):
        for copy in copies:
            copy.wait()
        for h in range(PER_GROUP):
            cols = slice(h * HD, (h + 1) * HD)
            m_ref[:, cols] = jnp.broadcast_to(ml_ref[:, h : h + 1], (BLOCK, HD))
            at = PER_GROUP + h
            l_ref[:, cols] = jnp.broadcast_to(ml_ref[:, at : at + 1], (BLOCK, HD))

    def store_state():
        lanes = lax.broadcasted_iota(jnp.int32, (BLOCK, HD), 1)
        ml = jnp.zeros((BLOCK, HD), F32)
        for h in range(PER_GROUP):
            cols = slice(h * HD, (h + 1) * HD)
            ml = jnp.where(lanes == h, m_ref[:, cols], ml)
            ml = jnp.where(lanes == PER_GROUP + h, l_ref[:, cols], ml)
        ml_ref[...] = ml
        copies = [copy_in(acc_ref, acc_hbm, n), copy_in(ml_ref, ml_hbm, n + 1)]
        for copy in copies:
            copy.start()
        for copy in copies:
            copy.wait()

    def work(loaded):
        q_copy = copy_in(q_hbm, q_ref, n + 2)
        q_copy.start()
        copies = [copy_in(kv, kv_ref.at[k], k) for k, kv in enumerate(kv_hbm)]
        for copy in copies:
            copy.start()
        if loaded:
            spread_state(loaded)
        q_copy.wait()
        for k, slot in enumerate(slots):
            copies[k].wait()
            if slot == (0, 0):
                own_block(kv_ref.at[k])
            else:
                other_block(kv_ref.at[k], blocks[k])

    some = functools.reduce(jnp.logical_or, active)
    if first:
        work(None)
        store_state()
    elif last:
        loaded = load_state()

        @pl.when(some)
        def _():
            work(loaded)

        @pl.when(jnp.logical_not(some))
        def _():
            spread_state(loaded)

        acc_ref[...] = acc_ref[...] / l_ref[...]
        copy = copy_in(acc_ref, out_hbm, n)
        copy.start()
        copy.wait()
    else:

        @pl.when(some)
        def _():
            work(load_state())
            store_state()


def attend(slots, me, lengths, queries, kvs, state, last=False):
    heads = jax.ShapeDtypeStruct((BLOCK, PER_GROUP * HD), F32)
    sizes = jax.ShapeDtypeStruct((BLOCK, HD), F32)
    operands = [me, lengths, queries, *kvs]
    aliases = {}
    if state is not None:
        if not last:
            aliases = {len(operands): 0, len(operands) + 1: 1}
        operands += state
    shapes = (heads,) if last else (heads, sizes)
    work = PER_GROUP * BLOCK * BLOCK * len(slots)
    got = pl.pallas_call(
        functools.partial(attend_kernel, slots, state is None, last),
        out_shape=shapes,
        in_specs=[SMEM, SMEM] + [ANY] * (len(operands) - 2),
        out_specs=[ANY] * len(shapes),
        scratch_shapes=[
            pltpu.VMEM((BLOCK, PER_GROUP * HD), BF16),
            pltpu.VMEM((len(slots), 2, BLOCK, HD), BF16),
            pltpu.VMEM((BLOCK, PER_GROUP * HD), F32),
            pltpu.VMEM((BLOCK, PER_GROUP * HD), F32),
            pltpu.VMEM((BLOCK, PER_GROUP * HD), F32),
            pltpu.VMEM((BLOCK, HD), F32),
            pltpu.SemaphoreType.DMA((len(slots) + 3,)),
        ],
        input_output_aliases=aliases,
        compiler_params=pltpu.CompilerParams(vmem_limit_bytes=32 << 20),
        cost_estimate=pl.CostEstimate(
            flops=4 * HD * work, bytes_accessed=4 << 20, transcendentals=work
        ),
        name="attend_%d_%d" % slots[0],
    )(*operands)
    return got[0] if last else got


def small_call(kernel, shape, operands, specs=None, **kw):
    return pl.pallas_call(
        kernel,
        out_shape=shape,
        in_specs=specs or [VMEM] * len(operands),
        out_specs=jax.tree.map(lambda _: VMEM, shape),
        compiler_params=pltpu.CompilerParams(vmem_limit_bytes=24 << 20),
        **kw,
    )(*operands)


def project_kernel(got_ref, *refs):
    packs, out_ref, weight_s, sems = refs[:PLANE], refs[PLANE], refs[-2], refs[-1]
    copies = [
        pltpu.make_async_copy(pack.at[pl.ds(0, BLOCK)], weight_s.at[k], sems.at[k])
        for k, pack in enumerate(packs)
    ]
    for copy in copies:
        copy.start()
    sizes = []
    for z in range(Z):
        stats = []
        for step in range(Z):
            packed = got_ref[z, step * PAD + TRACES : (step + 1) * PAD, :HD]
            for t in range(PAD):
                stats.append(pltpu.roll(packed, (HD - 16 * t) % HD, 1))
        sizes.append(jnp.concatenate(stats, axis=0))
    sizes = [
        size
        + pltpu.roll(size, HD - PER_GROUP, 1)
        + pltpu.roll(size, HD - 2 * PER_GROUP, 1)
        for size in sizes
    ]
    top = functools.reduce(jnp.maximum, sizes)
    weights = [jnp.exp2(size - top) for size in sizes]
    total = functools.reduce(jnp.add, weights)
    weights = [weight / total for weight in weights]
    slot = lax.broadcasted_iota(jnp.int32, (GROUP, HD), 0)
    picked = []
    for h in range(PER_GROUP):
        joined = jnp.zeros((GROUP, HD), F32)
        for z in range(Z):
            joined = joined + got_ref[z, :, h * HD : (h + 1) * HD] * weights[z][:, h : h + 1]
        joined = jnp.where((slot & (PAD - 1)) < TRACES, joined, 0.0)
        picked.append(joined.astype(BF16))
    picked = jnp.concatenate(picked, axis=1)
    for k in range(PLANE):
        copies[k].wait()
        part = jnp.dot(picked, weight_s[k], preferred_element_type=F32)
        out_ref[:, k * 256 : (k + 1) * 256] = part


def inner_kernel(me_ref, total_ref, *refs):
    packs, out_ref, pack_s, sems = refs[:PLANE], refs[PLANE], refs[-2], refs[-1]
    rest = pack_s.shape[1]
    copies = [
        pltpu.make_async_copy(pack.at[pl.ds(BLOCK, rest)], pack_s.at[k], sems.at[k])
        for k, pack in enumerate(packs)
    ]
    for copy in copies:
        copy.start()
    place = me_ref[0] % PLANE
    slot = lax.broadcasted_iota(jnp.int32, (GROUP, TRACES * STEPS), 0)
    at = lax.broadcasted_iota(jnp.int32, (GROUP, TRACES * STEPS), 1)
    trace = slot & (PAD - 1)
    wanted = trace * STEPS + PLANE * (slot >> 3) + place
    chosen = jnp.where((at == wanted) & (trace < TRACES), 1.0, 0.0).astype(BF16)
    for k in range(PLANE):
        copies[k].wait()
        base = jnp.dot(chosen, pack_s[k, WIDE:], preferred_element_type=F32)
        stream = (base + total_ref[:, k * 256 : (k + 1) * 256]).astype(BF16)
        for n in range(4):
            weight = pack_s[k, n * 256 : (n + 1) * 256]
            part = jnp.dot(stream, weight, preferred_element_type=F32)
            cols = slice(n * 256, (n + 1) * 256)
            out_ref[:, cols] = part if k == 0 else out_ref[:, cols] + part


def hidden_kernel(me_ref, inner_ref, class_ref, out_ref):
    hidden = jnp.maximum(inner_ref[...], 0.0).astype(BF16)
    logits = jnp.dot(hidden, class_ref[...], preferred_element_type=F32)
    gap = logits[:, 1:2] - logits[:, 0:1]
    lane = lax.broadcasted_iota(jnp.int32, (PAD, HD), 1)
    mine = jnp.where(lane == me_ref[0], gap, 0.0)
    for k in range(out_ref.shape[0]):
        out_ref[k] = mine


def vote_kernel(prompts, clusters, got_ref, scores_ref, votes_ref):
    gap = jnp.sum(got_ref[...], axis=0)
    scores = 1.0 / (1.0 + jnp.exp(-gap))
    scores_ref[...] = scores[:TRACES, :STEPS]
    lane = lax.broadcasted_iota(jnp.int32, (PAD, HD), 1)
    chain = jnp.min(jnp.where(lane < STEPS, scores, 2.0), axis=1, keepdims=True)
    prompt = lax.broadcasted_iota(jnp.int32, (PROMPTS, CLUSTERS), 0)
    cluster = lax.broadcasted_iota(jnp.int32, (PROMPTS, CLUSTERS), 1)
    votes = jnp.zeros((PROMPTS, CLUSTERS), F32)
    for t in range(TRACES):
        here = (prompt == prompts[t]) & (cluster == clusters[t])
        votes = votes + jnp.where(here, chain[t : t + 1, :], 0.0)
    votes_ref[...] = votes


def swapped(value, axis, bit):
    count = lax.axis_size(axis)
    return lax.ppermute(value, axis, [(s, s ^ bit) for s in range(count)])


def raised(value, planes):
    count = lax.axis_size("ctx")
    steps = planes * PLANE
    return lax.ppermute(value, "ctx", [(s, (s + steps) % count) for s in range(count)])


def per_device(
    queries,
    keys_values,
    trace_lengths,
    step_rows,
    prompt_ids,
    cluster_ids,
    step_stream,
    out_weight,
    score_weight,
    class_weight,
):
    me = lax.axis_index("ctx").astype(jnp.int32).reshape(1)
    columns = [[PLANE * z + j for z in range(Z)] for j in range(PLANE)]
    tie = lambda *values: lax.optimization_barrier(values)
    add = functools.partial(attend, me=me, lengths=trace_lengths, queries=queries)

    kv0 = keys_values
    core0 = swapped(kv0, "ctx", 1)
    kv1 = raised(kv0, 1)

    half = PER_GROUP * HD
    keep, passed, sent = small_call(
        pick_kernel,
        tuple(jax.ShapeDtypeStruct((n * GROUP, half), BF16) for n in (1, 1, 2)),
        [me, step_rows, queries],
        [SMEM, VMEM, VMEM],
        scratch_shapes=[pltpu.VMEM((PLANE * GROUP, half), BF16)],
        name="pick",
    )
    arrived = swapped(sent, "ctx", 1)
    across = swapped(passed + arrived[GROUP:], "ctx", 2)
    wanted = keep + arrived[:GROUP] + across
    wanted, kv0y = tie(wanted, kv0)
    wanted1, wanted2 = raised(wanted, -1), raised(wanted, -2)
    across0 = swapped(kv0y, "ctx", 2)
    core0y = swapped(across0, "ctx", 1)
    wanted, core0 = tie(wanted, core0)
    state = add([(0, 0), (0, 1)], kvs=[kv0, core0], state=None)
    wanted, wanted1, wanted2, state = tie(wanted, wanted1, wanted2, state)

    pack = jnp.concatenate(
        [out_weight]
        + [score_weight[:, n * 256 : (n + 1) * 256] for n in range(4)]
        + [step_stream],
        axis=0,
    )
    pack, across0 = tie(pack, across0)
    packs = [pack, swapped(pack, "ctx", 1), swapped(pack, "ctx", 2)]
    packs.append(swapped(packs[2], "ctx", 1))

    parts = small_call(
        picked_kernel,
        jax.ShapeDtypeStruct((GROUP, half), F32),
        [me, trace_lengths, step_rows, wanted, wanted1, wanted2, kv0, core0, across0, core0y],
        [SMEM, SMEM] + [VMEM] * 4 + [ANY] * 4,
        scratch_shapes=[
            pltpu.VMEM((PLANE, 2, BLOCK, HD), BF16),
            pltpu.SemaphoreType.DMA((PLANE,)),
        ],
        name="picked",
    )
    parts, state, kv1, across0, core0y = tie(parts, state, kv1, across0, core0y)
    core1 = swapped(kv1, "ctx", 1)
    state = add(
        [(0, 2), (0, 3), (1, 0), (1, 1)], kvs=[across0, core0y, kv1, core1], state=state
    )
    parts = jnp.broadcast_to(parts.astype(jnp.float16)[None], (Z, GROUP, half))
    parts = lax.all_to_all(parts, "ctx", 0, 0, axis_index_groups=columns).astype(F32)
    parts, state, kv1, packs[2] = tie(parts, state, kv1, packs[2])
    across1 = swapped(kv1, "ctx", 2)

    projected = small_call(
        project_kernel,
        jax.ShapeDtypeStruct((GROUP, WIDE), F32),
        [parts, *packs],
        [VMEM] + [ANY] * 4,
        scratch_shapes=[
            pltpu.VMEM((PLANE, BLOCK, 256), BF16),
            pltpu.SemaphoreType.DMA((PLANE,)),
        ],
        name="project",
    )
    projected, kv1 = tie((projected * 0.25).astype(jnp.float16), kv1)
    kv2 = raised(kv1, 1)
    projected = projected + swapped(projected, "head", 2)
    projected, across1 = tie(projected, across1)
    core1y = swapped(across1, "ctx", 1)
    projected = projected + swapped(projected, "head", 4)
    projected, kv2 = tie(projected, kv2)
    core2 = swapped(kv2, "ctx", 1)
    other = swapped(projected, "head", 1)
    projected = (projected.astype(F32) + other.astype(F32)) * 4.0

    inner = small_call(
        inner_kernel,
        jax.ShapeDtypeStruct((GROUP, WIDE), F32),
        [me, projected, *packs],
        [SMEM, VMEM] + [ANY] * 4,
        scratch_shapes=[
            pltpu.VMEM((PLANE, WIDE + TRACES * STEPS, 256), BF16),
            pltpu.SemaphoreType.DMA((PLANE,)),
        ],
        name="inner",
    )
    inner, state, kv2 = tie(inner, state, kv2)
    across2 = swapped(kv2, "ctx", 2)
    inner = (inner * 2.0**-10).astype(jnp.float16).reshape(Z, PAD, WIDE)
    state = add(
        [(1, 2), (1, 3), (2, 0), (2, 1)], kvs=[across1, core1y, kv2, core2], state=state
    )
    inner = lax.all_to_all(inner, "ctx", 0, 0, axis_index_groups=columns)
    inner, state = tie(inner, state)
    inner = jnp.sum(inner.astype(F32), axis=0) * 2.0**10
    heads, count = lax.axis_size("head"), lax.axis_size("ctx")
    gap = small_call(
        hidden_kernel,
        jax.ShapeDtypeStruct((heads, PAD, HD), F32),
        [me, inner, class_weight],
        [SMEM, VMEM, VMEM],
        name="hidden",
    )
    gap, across2 = tie(gap, across2)
    core2y = swapped(across2, "ctx", 1)
    gap = lax.all_to_all(gap, "head", 0, 0)
    gap, state, core2y = tie(gap, state, core2y)
    gap = jnp.sum(gap, axis=0)
    attended = add([(2, 2), (2, 3)], kvs=[across2, core2y], state=state, last=True)
    gap = lax.all_to_all(jnp.broadcast_to(gap[None], (count, PAD, HD)), "ctx", 0, 0)
    step_scores, votes = small_call(
        vote_kernel,
        (
            jax.ShapeDtypeStruct((TRACES, STEPS), F32),
            jax.ShapeDtypeStruct((PROMPTS, CLUSTERS), F32),
        ),
        [prompt_ids, cluster_ids, gap],
        [SMEM, SMEM, VMEM],
        name="vote",
    )
    return (attended, step_scores, votes)


def solution(mesh):
    placed = (
        P("ctx", "head"),
        P(None, "ctx", "head"),
        P(),
        P(),
        P(),
        P(),
        P(None, "ctx"),
        P("head", "ctx"),
        P("ctx", "head"),
        P("head", None),
    )
    return jax.shard_map(
        per_device,
        mesh=mesh,
        in_specs=placed,
        out_specs=(P("ctx", "head"), P(), P()),
        check_vma=False,
    )
```

```python
import functools
import math

import jax
import jax.numpy as jnp
from jax import lax
from jax.experimental import pallas as pl
from jax.experimental.pallas import tpu as pltpu
from jax.sharding import PartitionSpec as P

HD = 128
PROMPTS = 2
CLUSTERS = 4
TRACES = 7
STEPS = 32
PER_GROUP = 4
BLOCK = 512
TILE = 256
Z = 8
PLANE = 4
PAD = 8
GROUP = Z * PAD
WIDE = 1024
COEF = HD**-0.5 * math.log2(math.e)
LOW = -1e30
NONE = -60000.0
VMEM = pl.BlockSpec(memory_space=pltpu.VMEM)
SMEM = pl.BlockSpec(memory_space=pltpu.SMEM)
HBM = pl.BlockSpec(memory_space=pltpu.HBM)
BF16 = jnp.bfloat16
F32 = jnp.float32


def first_key(row, lengths):
    start = row * 0
    end = jnp.int32(0)
    for t in range(TRACES):
        end = end + lengths[t]
        start = jnp.where(row >= end, end, start)
    return start


def pick_kernel(me_ref, steps_hbm, q_hbm, keep_ref, pass_ref, send_ref, all_ref, steps_ref, q_ref, sems):
    steps_copy = pltpu.make_async_copy(steps_hbm, steps_ref, sems.at[0])
    q_copy = pltpu.make_async_copy(q_hbm, q_ref, sems.at[1])
    steps_copy.start()
    q_copy.start()
    steps_copy.wait()
    q_copy.wait()
    me = me_ref[0]
    core, side = me % 2, (me // 2) % 2
    at = lax.broadcasted_iota(jnp.int32, (TRACES, BLOCK), 1) + me * BLOCK
    none = jnp.zeros((PAD - TRACES, BLOCK), F32)
    steps = steps_ref[...]
    for c in range(2):
        for y in range(2):
            parts = []
            for z in range(Z):
                step = PLANE * z + 2 * y + c
                parts.append(jnp.where(steps[:, step : step + 1] == at, 1.0, 0.0))
                parts.append(none)
            chosen = jnp.concatenate(parts, axis=0).astype(BF16)
            got = jnp.dot(chosen, q_ref[...], preferred_element_type=F32)
            all_ref[pl.ds((2 * c + y) * GROUP, GROUP), :] = got.astype(BF16)

    def group(c, y):
        return all_ref[pl.ds(pl.multiple_of((2 * c + y) * GROUP, GROUP), GROUP), :]

    keep_ref[...] = group(core, side)
    pass_ref[...] = group(core, 1 - side)
    send_ref[:GROUP] = group(1 - core, side)
    send_ref[GROUP:] = group(1 - core, 1 - side)


def picked_kernel(me_ref, lengths_hbm, steps_hbm, q_ref, q1_ref, q2_ref, *refs):
    kv_refs, out_ref = refs[:PLANE], refs[PLANE]
    kv_s, lengths, steps_ref, sems = refs[-4:]
    lengths_copy = pltpu.make_async_copy(lengths_hbm, lengths, sems.at[PLANE])
    steps_copy = pltpu.make_async_copy(steps_hbm, steps_ref, sems.at[PLANE + 1])
    copies = [
        pltpu.make_async_copy(kv, kv_s.at[k], sems.at[k]) for k, kv in enumerate(kv_refs)
    ]
    for copy in [lengths_copy, steps_copy] + copies:
        copy.start()
    lengths_copy.wait()
    steps_copy.wait()
    me = me_ref[0]
    place = me % PLANE
    steps = steps_ref[...]
    lane = lax.broadcasted_iota(jnp.int32, (TRACES, STEPS), 1)
    none = jnp.full((PAD - TRACES, HD), -1, jnp.int32)
    parts = []
    for z in range(Z):
        mine = jnp.where(lane == PLANE * z + place, steps, 0)
        mine = jnp.sum(mine, axis=1, keepdims=True)
        parts.append(jnp.broadcast_to(mine, (TRACES, HD)))
        parts.append(none)
    row = jnp.concatenate(parts, axis=0)
    start = first_key(row, lengths)
    row = jnp.concatenate([row] * (BLOCK // HD), axis=1)
    start = jnp.concatenate([start] * (BLOCK // HD), axis=1)
    k_pos = lax.broadcasted_iota(jnp.int32, (GROUP, BLOCK), 1)
    q = (q_ref[...].astype(F32) + q1_ref[...].astype(F32) + q2_ref[...].astype(F32)).astype(BF16)
    q = jnp.concatenate([q[:, h * HD : (h + 1) * HD] for h in range(PER_GROUP)], axis=0)
    scores = []
    for k in range(PLANE):
        key0 = (me - place + (place ^ k)) * BLOCK
        mask = (k_pos <= row - key0) & (k_pos >= start - key0)
        mask = jnp.concatenate([mask] * PER_GROUP, axis=0)
        copies[k].wait()
        s = lax.dot_general(
            q, kv_s[k, 0], (((1,), (1,)), ((), ())), preferred_element_type=F32
        )
        scores.append(jnp.where(mask, s, LOW))
    top = jnp.maximum(jnp.maximum(scores[0], scores[1]), jnp.maximum(scores[2], scores[3]))
    top = jnp.maximum(jnp.max(top, axis=1, keepdims=True), 0.1 * LOW)
    ones = jnp.ones((BLOCK, HD), BF16)
    pv = jnp.zeros((PER_GROUP * GROUP, 2 * HD), F32)
    for k, s in enumerate(scores):
        p = jnp.exp2((s - top) * COEF).astype(BF16)
        ext = jnp.concatenate([kv_s[k, 1], ones], axis=1)
        pv = pv + jnp.dot(p, ext, preferred_element_type=F32)
    total = pv[:, HD:]
    some = total > 0.0
    total = jnp.where(some, total, 1.0)
    value = pv[:, :HD] / total
    size = jnp.where(some, top * COEF + jnp.log2(total), NONE)
    lanes = lax.broadcasted_iota(jnp.int32, (GROUP, HD), 1)
    stats = jnp.zeros((GROUP, HD), F32)
    for h in range(PER_GROUP):
        rows = slice(h * GROUP, (h + 1) * GROUP)
        out_ref[:, h * HD : (h + 1) * HD] = value[rows]
        rest = size[rows]
        for k in range(3):
            coarse = rest.astype(BF16).astype(F32)
            stats = jnp.where(lanes == PER_GROUP * k + h, coarse, stats)
            rest = rest - coarse
    for z in range(Z):
        packed = jnp.zeros((1, HD), F32)
        for t in range(TRACES):
            at = z * PAD + t
            packed = packed + pltpu.roll(stats[at : at + 1], 16 * t, 1)
        out_ref[z * PAD + TRACES : (z + 1) * PAD, :HD] = packed


def attend_kernel(slots, first, last, *refs):
    n = len(slots)
    me_ref, lengths_hbm, q_hbm = refs[:3]
    kv_hbm = refs[3 : 3 + n]
    if last:
        out_hbm = refs[-9]
    else:
        acc_hbm, ml_hbm = refs[-10:-8]
    if not first:
        acc_in, ml_in = refs[3 + n : 5 + n]
    q_ref, kv_ref, acc_ref, m_ref, l_ref, ml_ref, lengths, sems = refs[-8:]
    lengths_copy = pltpu.make_async_copy(lengths_hbm, lengths, sems.at[0])
    lengths_copy.start()
    lengths_copy.wait()
    me = me_ref[0]
    place = me % PLANE
    row0 = me * BLOCK
    ones = jnp.ones((BLOCK, HD), BF16)
    blocks = [me - place - back * PLANE + (place ^ flip) for back, flip in slots]
    earliest = first_key(row0, lengths)
    active = [(block < me) & ((block + 1) * BLOCK > earliest) for block in blocks]

    def copy_in(source, target, k):
        return pltpu.make_async_copy(source, target, sems.at[k])

    def weigh(rows, count, keys, ext, mask, fresh):
        q = q_ref[rows, :]
        q = jnp.concatenate([q[:, h * HD : (h + 1) * HD] for h in range(PER_GROUP)], axis=0)
        s = lax.dot_general(q, keys, (((1,), (1,)), ((), ())), preferred_element_type=F32)
        for h in range(PER_GROUP):
            cols = slice(h * HD, (h + 1) * HD)
            mine = s[h * count : (h + 1) * count]
            if mask is not None:
                mine = jnp.where(mask, mine, LOW)
            top = jnp.max(mine, axis=1, keepdims=True)
            if fresh:
                top = jnp.broadcast_to(top, (count, HD))
            else:
                before = m_ref[rows, cols]
                top = jnp.maximum(before, top)
            wide = jnp.concatenate([top] * (mine.shape[1] // HD), axis=1)
            p = jnp.exp2((mine - wide) * COEF).astype(BF16)
            pv = jnp.dot(p, ext, preferred_element_type=F32)
            m_ref[rows, cols] = top
            if fresh:
                acc_ref[rows, cols] = pv[:, :HD]
                l_ref[rows, cols] = pv[:, HD:]
            else:
                scale = jnp.exp2((before - top) * COEF)
                acc_ref[rows, cols] = acc_ref[rows, cols] * scale + pv[:, :HD]
                l_ref[rows, cols] = l_ref[rows, cols] * scale + pv[:, HD:]

    def own_block(kv):
        for tile in range(BLOCK // TILE):
            width = (tile + 1) * TILE
            rows = slice(tile * TILE, width)
            keys = kv[0, :width, :]
            ext = jnp.concatenate([kv[1, :width, :], ones[:width]], axis=1)
            q_pos = row0 + tile * TILE + lax.broadcasted_iota(jnp.int32, (TILE, width), 0)
            k_pos = row0 + lax.broadcasted_iota(jnp.int32, (TILE, width), 1)
            starts = first_key(
                row0 + tile * TILE + lax.broadcasted_iota(jnp.int32, (TILE, HD), 0), lengths
            )
            starts = jnp.concatenate([starts] * (width // HD), axis=1)
            mask = (k_pos <= q_pos) & (k_pos >= starts)
            weigh(rows, TILE, keys, ext, mask, True)

    def other_block(kv, block):
        key0 = block * BLOCK

        def one_tile(tile, carry):
            begin = pl.multiple_of(tile * TILE, TILE)
            rows = pl.ds(begin, TILE)
            low = first_key(row0 + begin, lengths)
            high = first_key(row0 + begin + TILE - 1, lengths)
            some = (block < me) & (key0 + BLOCK > low)
            every = key0 >= high

            def run(masked):
                keys = kv[0]
                ext = jnp.concatenate([kv[1], ones], axis=1)
                mask = None
                if masked:
                    starts = first_key(
                        row0 + begin + lax.broadcasted_iota(jnp.int32, (TILE, HD), 0), lengths
                    )
                    starts = jnp.concatenate([starts] * (BLOCK // HD), axis=1)
                    k_pos = key0 + lax.broadcasted_iota(jnp.int32, (TILE, BLOCK), 1)
                    mask = k_pos >= starts
                weigh(rows, TILE, keys, ext, mask, False)

            pl.when(some & every)(functools.partial(run, False))
            pl.when(some & jnp.logical_not(every))(functools.partial(run, True))
            return carry

        lax.fori_loop(0, BLOCK // TILE, one_tile, 0)

    def load_state():
        copies = [copy_in(acc_in, acc_ref, n), copy_in(ml_in, ml_ref, n + 1)]
        for copy in copies:
            copy.start()
        return copies

    def spread_state(copies):
        for copy in copies:
            copy.wait()
        for h in range(PER_GROUP):
            cols = slice(h * HD, (h + 1) * HD)
            m_ref[:, cols] = jnp.broadcast_to(ml_ref[:, h : h + 1], (BLOCK, HD))
            at = PER_GROUP + h
            l_ref[:, cols] = jnp.broadcast_to(ml_ref[:, at : at + 1], (BLOCK, HD))

    def store_state():
        lanes = lax.broadcasted_iota(jnp.int32, (BLOCK, HD), 1)
        ml = jnp.zeros((BLOCK, HD), F32)
        for h in range(PER_GROUP):
            cols = slice(h * HD, (h + 1) * HD)
            ml = jnp.where(lanes == h, m_ref[:, cols], ml)
            ml = jnp.where(lanes == PER_GROUP + h, l_ref[:, cols], ml)
        ml_ref[...] = ml
        copies = [copy_in(acc_ref, acc_hbm, n), copy_in(ml_ref, ml_hbm, n + 1)]
        for copy in copies:
            copy.start()
        for copy in copies:
            copy.wait()

    def work(loaded):
        q_copy = copy_in(q_hbm, q_ref, n + 2)
        q_copy.start()
        copies = [copy_in(kv, kv_ref.at[k], k) for k, kv in enumerate(kv_hbm)]
        for copy in copies:
            copy.start()
        if loaded:
            spread_state(loaded)
        q_copy.wait()
        for k, slot in enumerate(slots):
            copies[k].wait()
            if slot == (0, 0):
                own_block(kv_ref.at[k])
            else:
                other_block(kv_ref.at[k], blocks[k])

    some = functools.reduce(jnp.logical_or, active)
    if first:
        work(None)
        store_state()
    elif last:
        loaded = load_state()

        @pl.when(some)
        def _():
            work(loaded)

        @pl.when(jnp.logical_not(some))
        def _():
            spread_state(loaded)

        acc_ref[...] = acc_ref[...] / l_ref[...]
        copy = copy_in(acc_ref, out_hbm, n)
        copy.start()
        copy.wait()
    else:

        @pl.when(some)
        def _():
            work(load_state())
            store_state()


def attend(slots, me, lengths, queries, kvs, state, last=False):
    heads = pltpu.HBM((BLOCK, PER_GROUP * HD), F32)
    sizes = pltpu.HBM((BLOCK, HD), F32)
    operands = [me, *pinned([lengths, queries]), *kvs]
    aliases = {}
    if state is not None:
        if not last:
            aliases = {len(operands): 0, len(operands) + 1: 1}
        operands += pinned(state)
    shapes = (heads,) if last else (heads, sizes)
    work = PER_GROUP * BLOCK * BLOCK * len(slots)
    got = pl.pallas_call(
        functools.partial(attend_kernel, slots, state is None, last),
        out_shape=shapes,
        in_specs=[SMEM] + [HBM] * (len(operands) - 1),
        out_specs=[HBM] * len(shapes),
        scratch_shapes=[
            pltpu.VMEM((BLOCK, PER_GROUP * HD), BF16),
            pltpu.VMEM((len(slots), 2, BLOCK, HD), BF16),
            pltpu.VMEM((BLOCK, PER_GROUP * HD), F32),
            pltpu.VMEM((BLOCK, PER_GROUP * HD), F32),
            pltpu.VMEM((BLOCK, PER_GROUP * HD), F32),
            pltpu.VMEM((BLOCK, HD), F32),
            pltpu.SMEM((TRACES,), jnp.int32),
            pltpu.SemaphoreType.DMA((len(slots) + 3,)),
        ],
        input_output_aliases=aliases,
        compiler_params=pltpu.CompilerParams(vmem_limit_bytes=32 << 20),
        cost_estimate=pl.CostEstimate(
            flops=4 * HD * work, bytes_accessed=4 << 20, transcendentals=work
        ),
        name="attend_%d_%d" % slots[0],
    )(*operands)
    return got[0] if last else got


def pinned(values):
    return [pltpu.with_memory_space_constraint(value, pltpu.HBM) for value in values]


def small_call(kernel, shape, operands, specs=None, **kw):
    return pl.pallas_call(
        kernel,
        out_shape=shape,
        in_specs=specs or [VMEM] * len(operands),
        out_specs=jax.tree.map(lambda _: VMEM, shape),
        compiler_params=pltpu.CompilerParams(vmem_limit_bytes=24 << 20),
        **kw,
    )(*operands)


def project_kernel(got_ref, *refs):
    packs, out_ref, weight_s, sems = refs[:PLANE], refs[PLANE], refs[-2], refs[-1]
    copies = [
        pltpu.make_async_copy(pack.at[pl.ds(0, BLOCK)], weight_s.at[k], sems.at[k])
        for k, pack in enumerate(packs)
    ]
    for copy in copies:
        copy.start()
    sizes = []
    for z in range(Z):
        stats = []
        for step in range(Z):
            packed = got_ref[z, step * PAD + TRACES : (step + 1) * PAD, :HD]
            for t in range(PAD):
                stats.append(pltpu.roll(packed, (HD - 16 * t) % HD, 1))
        sizes.append(jnp.concatenate(stats, axis=0))
    sizes = [
        size
        + pltpu.roll(size, HD - PER_GROUP, 1)
        + pltpu.roll(size, HD - 2 * PER_GROUP, 1)
        for size in sizes
    ]
    top = functools.reduce(jnp.maximum, sizes)
    weights = [jnp.exp2(size - top) for size in sizes]
    total = functools.reduce(jnp.add, weights)
    weights = [weight / total for weight in weights]
    slot = lax.broadcasted_iota(jnp.int32, (GROUP, HD), 0)
    picked = []
    for h in range(PER_GROUP):
        joined = jnp.zeros((GROUP, HD), F32)
        for z in range(Z):
            joined = joined + got_ref[z, :, h * HD : (h + 1) * HD] * weights[z][:, h : h + 1]
        joined = jnp.where((slot & (PAD - 1)) < TRACES, joined, 0.0)
        picked.append(joined.astype(BF16))
    picked = jnp.concatenate(picked, axis=1)
    for k in range(PLANE):
        copies[k].wait()
        part = jnp.dot(picked, weight_s[k], preferred_element_type=F32)
        out_ref[:, k * 256 : (k + 1) * 256] = part


def inner_kernel(me_ref, total_ref, *refs):
    packs, out_ref, pack_s, sems = refs[:PLANE], refs[PLANE], refs[-2], refs[-1]
    rest = pack_s.shape[1]
    copies = [
        pltpu.make_async_copy(pack.at[pl.ds(BLOCK, rest)], pack_s.at[k], sems.at[k])
        for k, pack in enumerate(packs)
    ]
    for copy in copies:
        copy.start()
    place = me_ref[0] % PLANE
    slot = lax.broadcasted_iota(jnp.int32, (GROUP, TRACES * STEPS), 0)
    at = lax.broadcasted_iota(jnp.int32, (GROUP, TRACES * STEPS), 1)
    trace = slot & (PAD - 1)
    wanted = trace * STEPS + PLANE * (slot >> 3) + place
    chosen = jnp.where((at == wanted) & (trace < TRACES), 1.0, 0.0).astype(BF16)
    for k in range(PLANE):
        copies[k].wait()
        base = jnp.dot(chosen, pack_s[k, WIDE:], preferred_element_type=F32)
        stream = (base + total_ref[:, k * 256 : (k + 1) * 256]).astype(BF16)
        for n in range(4):
            weight = pack_s[k, n * 256 : (n + 1) * 256]
            part = jnp.dot(stream, weight, preferred_element_type=F32)
            cols = slice(n * 256, (n + 1) * 256)
            out_ref[:, cols] = part if k == 0 else out_ref[:, cols] + part


def hidden_kernel(me_ref, inner_ref, class_ref, out_ref):
    hidden = jnp.maximum(inner_ref[...], 0.0).astype(BF16)
    logits = jnp.dot(hidden, class_ref[...], preferred_element_type=F32)
    gap = logits[:, 1:2] - logits[:, 0:1]
    lane = lax.broadcasted_iota(jnp.int32, (PAD, HD), 1)
    mine = jnp.where(lane == me_ref[0], gap, 0.0)
    for k in range(out_ref.shape[0]):
        out_ref[k] = mine


def vote_kernel(prompts, clusters, got_ref, scores_ref, votes_ref):
    gap = jnp.sum(got_ref[...], axis=0)
    scores = 1.0 / (1.0 + jnp.exp(-gap))
    scores_ref[...] = scores[:TRACES, :STEPS]
    lane = lax.broadcasted_iota(jnp.int32, (PAD, HD), 1)
    chain = jnp.min(jnp.where(lane < STEPS, scores, 2.0), axis=1, keepdims=True)
    prompt = lax.broadcasted_iota(jnp.int32, (PROMPTS, CLUSTERS), 0)
    cluster = lax.broadcasted_iota(jnp.int32, (PROMPTS, CLUSTERS), 1)
    votes = jnp.zeros((PROMPTS, CLUSTERS), F32)
    for t in range(TRACES):
        here = (prompt == prompts[t]) & (cluster == clusters[t])
        votes = votes + jnp.where(here, chain[t : t + 1, :], 0.0)
    votes_ref[...] = votes


def swapped(value, axis, bit):
    count = lax.axis_size(axis)
    return lax.ppermute(value, axis, [(s, s ^ bit) for s in range(count)])


def raised(value, planes):
    count = lax.axis_size("ctx")
    steps = planes * PLANE
    return lax.ppermute(value, "ctx", [(s, (s + steps) % count) for s in range(count)])


def per_device(
    queries,
    keys_values,
    trace_lengths,
    step_rows,
    prompt_ids,
    cluster_ids,
    step_stream,
    out_weight,
    score_weight,
    class_weight,
):
    me = lax.axis_index("ctx").astype(jnp.int32).reshape(1)
    columns = [[PLANE * z + j for z in range(Z)] for j in range(PLANE)]
    tie = lambda *values: lax.optimization_barrier(values)
    add = functools.partial(attend, me=me, lengths=trace_lengths, queries=queries)

    kv0 = keys_values
    core0 = swapped(kv0, "ctx", 1)
    kv1 = raised(kv0, 1)

    half = PER_GROUP * HD
    keep, passed, sent = small_call(
        pick_kernel,
        tuple(jax.ShapeDtypeStruct((n * GROUP, half), BF16) for n in (1, 1, 2)),
        [me, *pinned([step_rows, queries])],
        [SMEM, HBM, HBM],
        scratch_shapes=[
            pltpu.VMEM((PLANE * GROUP, half), BF16),
            pltpu.VMEM((TRACES, STEPS), jnp.int32),
            pltpu.VMEM((BLOCK, half), BF16),
            pltpu.SemaphoreType.DMA((2,)),
        ],
        name="pick",
    )
    arrived = swapped(sent, "ctx", 1)
    across = swapped(passed + arrived[GROUP:], "ctx", 2)
    wanted = keep + arrived[:GROUP] + across
    wanted, kv0y, core0, kv1 = tie(wanted, kv0, core0, kv1)
    wanted1, wanted2 = raised(wanted, -1), raised(wanted, -2)
    across0 = swapped(kv0y, "ctx", 2)
    core0y = swapped(core0, "ctx", 2)
    state = add([(0, 0), (0, 1)], kvs=[pinned([kv0y])[0], core0], state=None)
    wanted, wanted1, wanted2, state = tie(wanted, wanted1, wanted2, state)

    pack = jnp.concatenate(
        [out_weight]
        + [score_weight[:, n * 256 : (n + 1) * 256] for n in range(4)]
        + [step_stream],
        axis=0,
    )
    pack, wanted1, wanted2 = tie(pack, wanted1, wanted2)
    packs = [pack, swapped(pack, "ctx", 1), swapped(pack, "ctx", 2)]
    packs.append(swapped(packs[2], "ctx", 1))

    parts = small_call(
        picked_kernel,
        jax.ShapeDtypeStruct((GROUP, half), F32),
        [
            me,
            *pinned([trace_lengths, step_rows]),
            wanted,
            wanted1,
            wanted2,
            *pinned([kv0]),
            core0,
            across0,
            core0y,
        ],
        [SMEM, HBM, HBM] + [VMEM] * 3 + [HBM] * 4,
        scratch_shapes=[
            pltpu.VMEM((PLANE, 2, BLOCK, HD), BF16),
            pltpu.SMEM((TRACES,), jnp.int32),
            pltpu.VMEM((TRACES, STEPS), jnp.int32),
            pltpu.SemaphoreType.DMA((PLANE + 2,)),
        ],
        name="picked",
    )
    parts, state, kv1, across0, core0y = tie(parts, state, kv1, across0, core0y)
    core1 = swapped(kv1, "ctx", 1)
    state = add(
        [(0, 2), (0, 3), (1, 0), (1, 1)], kvs=[across0, core0y, kv1, core1], state=state
    )
    parts = jnp.broadcast_to(parts.astype(jnp.float16)[None], (Z, GROUP, half))
    parts = lax.all_to_all(parts, "ctx", 0, 0, axis_index_groups=columns).astype(F32)
    parts, state, kv1, core1, packs[2] = tie(parts, state, kv1, core1, packs[2])

    projected = small_call(
        project_kernel,
        jax.ShapeDtypeStruct((GROUP, WIDE), F32),
        [parts, *packs],
        [VMEM] + [HBM] * 4,
        scratch_shapes=[
            pltpu.VMEM((PLANE, BLOCK, 256), BF16),
            pltpu.SemaphoreType.DMA((PLANE,)),
        ],
        name="project",
    )
    projected, kv1 = tie((projected * 0.25).astype(jnp.float16), kv1)
    kv2 = raised(kv1, 1)
    other = swapped(projected, "head", 1)
    other, kv2, kv1 = tie(other, kv2, kv1)
    projected = projected + other
    across1, across2 = swapped(kv1, "ctx", 2), swapped(kv2, "ctx", 2)
    core2 = swapped(kv2, "ctx", 1)
    projected = projected + swapped(projected, "head", 2)
    projected, across1 = tie(projected, across1)
    core1y = swapped(across1, "ctx", 1)
    other = swapped(projected, "head", 4)
    state = add([(2, 0), (2, 1)], kvs=[kv2, core2], state=state)
    other, state, across2 = tie(other, state, across2)
    core2y = swapped(across2, "ctx", 1)
    projected = (projected.astype(F32) + other.astype(F32)) * 4.0

    inner = small_call(
        inner_kernel,
        jax.ShapeDtypeStruct((GROUP, WIDE), F32),
        [me, projected, *packs],
        [SMEM, VMEM] + [HBM] * 4,
        scratch_shapes=[
            pltpu.VMEM((PLANE, WIDE + TRACES * STEPS, 256), BF16),
            pltpu.SemaphoreType.DMA((PLANE,)),
        ],
        name="inner",
    )
    inner, state, core1y = tie(inner, state, core1y)
    inner = (inner * 2.0**-10).astype(jnp.float16).reshape(Z, PAD, WIDE)
    state = add([(1, 2), (1, 3)], kvs=[across1, core1y], state=state)
    inner = lax.all_to_all(inner, "ctx", 0, 0, axis_index_groups=columns)
    inner, state = tie(inner, state)
    inner = jnp.sum(inner.astype(F32), axis=0) * 2.0**10
    heads, count = lax.axis_size("head"), lax.axis_size("ctx")
    gap = small_call(
        hidden_kernel,
        jax.ShapeDtypeStruct((heads, PAD, HD), F32),
        [me, inner, class_weight],
        [SMEM, VMEM, VMEM],
        name="hidden",
    )
    gap, state, core2y = tie(gap, state, core2y)
    attended = add([(2, 2), (2, 3)], kvs=[across2, core2y], state=state, last=True)
    gap = lax.all_to_all(gap, "head", 0, 0)
    gap, attended = tie(gap, attended)
    gap = jnp.sum(gap, axis=0)
    gap = lax.all_to_all(jnp.broadcast_to(gap[None], (count, PAD, HD)), "ctx", 0, 0)
    step_scores, votes = small_call(
        vote_kernel,
        (
            jax.ShapeDtypeStruct((TRACES, STEPS), F32),
            jax.ShapeDtypeStruct((PROMPTS, CLUSTERS), F32),
        ),
        [prompt_ids, cluster_ids, gap],
        [SMEM, SMEM, VMEM],
        name="vote",
    )
    return (attended, step_scores, votes)


def solution(mesh):
    placed = (
        P("ctx", "head"),
        P(None, "ctx", "head"),
        P(),
        P(),
        P(),
        P(),
        P(None, "ctx"),
        P("head", "ctx"),
        P("ctx", "head"),
        P("head", None),
    )
    return jax.shard_map(
        per_device,
        mesh=mesh,
        in_specs=placed,
        out_specs=(P("ctx", "head"), P(), P()),
        check_vma=False,
    )
```

```python
import functools
import math

import jax
import jax.numpy as jnp
from jax import lax
from jax.experimental import pallas as pl
from jax.experimental.pallas import tpu as pltpu
from jax.sharding import PartitionSpec as P

HD = 128
PROMPTS = 2
CLUSTERS = 4
TRACES = 7
STEPS = 32
PER_GROUP = 4
BLOCK = 512
TILE = 256
Z = 8
PLANE = 4
PAD = 8
GROUP = Z * PAD
WIDE = 1024
COEF = HD**-0.5 * math.log2(math.e)
LOW = -1e30
NONE = -60000.0
VMEM = pl.BlockSpec(memory_space=pltpu.VMEM)
SMEM = pl.BlockSpec(memory_space=pltpu.SMEM)
HBM = pl.BlockSpec(memory_space=pltpu.HBM)
BF16 = jnp.bfloat16
F32 = jnp.float32


def first_key(row, lengths):
    start = row * 0
    end = jnp.int32(0)
    for t in range(TRACES):
        end = end + lengths[t]
        start = jnp.where(row >= end, end, start)
    return start


def pick_kernel(me_ref, steps_hbm, q_hbm, keep_ref, pass_ref, send_ref, all_ref, steps_ref, q_ref, sems):
    steps_copy = pltpu.make_async_copy(steps_hbm, steps_ref, sems.at[0])
    q_copy = pltpu.make_async_copy(q_hbm, q_ref, sems.at[1])
    steps_copy.start()
    q_copy.start()
    steps_copy.wait()
    q_copy.wait()
    me = me_ref[0]
    core, side = me % 2, (me // 2) % 2
    at = lax.broadcasted_iota(jnp.int32, (TRACES, BLOCK), 1) + me * BLOCK
    none = jnp.zeros((PAD - TRACES, BLOCK), F32)
    steps = steps_ref[...]
    for c in range(2):
        for y in range(2):
            parts = []
            for z in range(Z):
                step = PLANE * z + 2 * y + c
                parts.append(jnp.where(steps[:, step : step + 1] == at, 1.0, 0.0))
                parts.append(none)
            chosen = jnp.concatenate(parts, axis=0).astype(BF16)
            got = jnp.dot(chosen, q_ref[...], preferred_element_type=F32)
            all_ref[pl.ds((2 * c + y) * GROUP, GROUP), :] = got.astype(BF16)

    def group(c, y):
        return all_ref[pl.ds(pl.multiple_of((2 * c + y) * GROUP, GROUP), GROUP), :]

    keep_ref[...] = group(core, side)
    pass_ref[...] = group(core, 1 - side)
    send_ref[:GROUP] = group(1 - core, side)
    send_ref[GROUP:] = group(1 - core, 1 - side)


def picked_kernel(me_ref, lengths_hbm, steps_hbm, q_ref, q1_ref, q2_ref, *refs):
    kv_refs, out_ref = refs[:PLANE], refs[PLANE]
    kv_s, lengths, steps_ref, sems = refs[-4:]
    lengths_copy = pltpu.make_async_copy(lengths_hbm, lengths, sems.at[PLANE])
    steps_copy = pltpu.make_async_copy(steps_hbm, steps_ref, sems.at[PLANE + 1])
    copies = [
        pltpu.make_async_copy(kv, kv_s.at[k], sems.at[k]) for k, kv in enumerate(kv_refs)
    ]
    for copy in [lengths_copy, steps_copy] + copies:
        copy.start()
    lengths_copy.wait()
    steps_copy.wait()
    me = me_ref[0]
    place = me % PLANE
    steps = steps_ref[...]
    lane = lax.broadcasted_iota(jnp.int32, (TRACES, STEPS), 1)
    none = jnp.full((PAD - TRACES, HD), -1, jnp.int32)
    parts = []
    for z in range(Z):
        mine = jnp.where(lane == PLANE * z + place, steps, 0)
        mine = jnp.sum(mine, axis=1, keepdims=True)
        parts.append(jnp.broadcast_to(mine, (TRACES, HD)))
        parts.append(none)
    row = jnp.concatenate(parts, axis=0)
    start = first_key(row, lengths)
    row = jnp.concatenate([row] * (BLOCK // HD), axis=1)
    start = jnp.concatenate([start] * (BLOCK // HD), axis=1)
    k_pos = lax.broadcasted_iota(jnp.int32, (GROUP, BLOCK), 1)
    q = (q_ref[...].astype(F32) + q1_ref[...].astype(F32) + q2_ref[...].astype(F32)).astype(BF16)
    q = jnp.concatenate([q[:, h * HD : (h + 1) * HD] for h in range(PER_GROUP)], axis=0)
    scores = []
    for k in range(PLANE):
        key0 = (me - place + (place ^ k)) * BLOCK
        mask = (k_pos <= row - key0) & (k_pos >= start - key0)
        mask = jnp.concatenate([mask] * PER_GROUP, axis=0)
        copies[k].wait()
        s = lax.dot_general(
            q, kv_s[k, 0], (((1,), (1,)), ((), ())), preferred_element_type=F32
        )
        scores.append(jnp.where(mask, s, LOW))
    top = jnp.maximum(jnp.maximum(scores[0], scores[1]), jnp.maximum(scores[2], scores[3]))
    top = jnp.maximum(jnp.max(top, axis=1, keepdims=True), 0.1 * LOW)
    ones = jnp.ones((BLOCK, HD), BF16)
    pv = jnp.zeros((PER_GROUP * GROUP, 2 * HD), F32)
    for k, s in enumerate(scores):
        p = jnp.exp2((s - top) * COEF).astype(BF16)
        ext = jnp.concatenate([kv_s[k, 1], ones], axis=1)
        pv = pv + jnp.dot(p, ext, preferred_element_type=F32)
    total = pv[:, HD:]
    some = total > 0.0
    total = jnp.where(some, total, 1.0)
    value = pv[:, :HD] / total
    size = jnp.where(some, top * COEF + jnp.log2(total), NONE)
    lanes = lax.broadcasted_iota(jnp.int32, (GROUP, HD), 1)
    stats = jnp.zeros((GROUP, HD), F32)
    for h in range(PER_GROUP):
        rows = slice(h * GROUP, (h + 1) * GROUP)
        out_ref[:, h * HD : (h + 1) * HD] = value[rows]
        rest = size[rows]
        for k in range(3):
            coarse = rest.astype(BF16).astype(F32)
            stats = jnp.where(lanes == PER_GROUP * k + h, coarse, stats)
            rest = rest - coarse
    for z in range(Z):
        packed = jnp.zeros((1, HD), F32)
        for t in range(TRACES):
            at = z * PAD + t
            packed = packed + pltpu.roll(stats[at : at + 1], 16 * t, 1)
        out_ref[z * PAD + TRACES : (z + 1) * PAD, :HD] = packed


def attend_kernel(slots, first, last, *refs):
    n = len(slots)
    arrays = 1 + max(slot[2] for slot in slots)
    me_ref, lengths_hbm, q_hbm = refs[:3]
    kv_hbm = [refs[3 + array].at[pl.ds(2 * at, 2)] for _, _, array, at in slots]
    if last:
        out_hbm = refs[-9]
    else:
        acc_hbm, ml_hbm = refs[-10:-8]
    if not first:
        acc_in, ml_in = refs[3 + arrays : 5 + arrays]
    q_ref, kv_ref, acc_ref, m_ref, l_ref, ml_ref, lengths, sems = refs[-8:]
    lengths_copy = pltpu.make_async_copy(lengths_hbm, lengths, sems.at[0])
    lengths_copy.start()
    lengths_copy.wait()
    me = me_ref[0]
    place = me % PLANE
    row0 = me * BLOCK
    ones = jnp.ones((BLOCK, HD), BF16)
    blocks = [me - place - back * PLANE + (place ^ flip) for back, flip, _, _ in slots]
    earliest = first_key(row0, lengths)
    active = [(block < me) & ((block + 1) * BLOCK > earliest) for block in blocks]

    def copy_in(source, target, k):
        return pltpu.make_async_copy(source, target, sems.at[k])

    def weigh(rows, count, keys, ext, mask, fresh):
        q = q_ref[rows, :]
        q = jnp.concatenate([q[:, h * HD : (h + 1) * HD] for h in range(PER_GROUP)], axis=0)
        s = lax.dot_general(q, keys, (((1,), (1,)), ((), ())), preferred_element_type=F32)
        for h in range(PER_GROUP):
            cols = slice(h * HD, (h + 1) * HD)
            mine = s[h * count : (h + 1) * count]
            if mask is not None:
                mine = jnp.where(mask, mine, LOW)
            top = jnp.max(mine, axis=1, keepdims=True)
            if fresh:
                top = jnp.broadcast_to(top, (count, HD))
            else:
                before = m_ref[rows, cols]
                top = jnp.maximum(before, top)
            wide = jnp.concatenate([top] * (mine.shape[1] // HD), axis=1)
            p = jnp.exp2((mine - wide) * COEF).astype(BF16)
            pv = jnp.dot(p, ext, preferred_element_type=F32)
            m_ref[rows, cols] = top
            if fresh:
                acc_ref[rows, cols] = pv[:, :HD]
                l_ref[rows, cols] = pv[:, HD:]
            else:
                scale = jnp.exp2((before - top) * COEF)
                acc_ref[rows, cols] = acc_ref[rows, cols] * scale + pv[:, :HD]
                l_ref[rows, cols] = l_ref[rows, cols] * scale + pv[:, HD:]

    def own_block(kv):
        for tile in range(BLOCK // TILE):
            width = (tile + 1) * TILE
            rows = slice(tile * TILE, width)
            keys = kv[0, :width, :]
            ext = jnp.concatenate([kv[1, :width, :], ones[:width]], axis=1)
            q_pos = row0 + tile * TILE + lax.broadcasted_iota(jnp.int32, (TILE, width), 0)
            k_pos = row0 + lax.broadcasted_iota(jnp.int32, (TILE, width), 1)
            starts = first_key(
                row0 + tile * TILE + lax.broadcasted_iota(jnp.int32, (TILE, HD), 0), lengths
            )
            starts = jnp.concatenate([starts] * (width // HD), axis=1)
            mask = (k_pos <= q_pos) & (k_pos >= starts)
            weigh(rows, TILE, keys, ext, mask, True)

    def other_tile(index, carry):
        tile, k = index % (BLOCK // TILE), index // (BLOCK // TILE)
        block = blocks[-1]
        for other in range(n - 1):
            block = jnp.where(k == other, blocks[other], block)
        key0 = block * BLOCK
        begin = pl.multiple_of(tile * TILE, TILE)
        rows = pl.ds(begin, TILE)
        low = first_key(row0 + begin, lengths)
        high = first_key(row0 + begin + TILE - 1, lengths)
        some = (block < me) & (key0 + BLOCK > low)
        every = key0 >= high

        def run(masked):
            keys = kv_ref[k, 0]
            ext = jnp.concatenate([kv_ref[k, 1], ones], axis=1)
            mask = None
            if masked:
                starts = first_key(
                    row0 + begin + lax.broadcasted_iota(jnp.int32, (TILE, HD), 0), lengths
                )
                starts = jnp.concatenate([starts] * (BLOCK // HD), axis=1)
                k_pos = key0 + lax.broadcasted_iota(jnp.int32, (TILE, BLOCK), 1)
                mask = k_pos >= starts
            weigh(rows, TILE, keys, ext, mask, False)

        pl.when(some & every)(functools.partial(run, False))
        pl.when(some & jnp.logical_not(every))(functools.partial(run, True))
        return carry

    def load_state():
        copies = [copy_in(acc_in, acc_ref, n), copy_in(ml_in, ml_ref, n + 1)]
        for copy in copies:
            copy.start()
        return copies

    def spread_state(copies):
        for copy in copies:
            copy.wait()
        for h in range(PER_GROUP):
            cols = slice(h * HD, (h + 1) * HD)
            m_ref[:, cols] = jnp.broadcast_to(ml_ref[:, h : h + 1], (BLOCK, HD))
            at = PER_GROUP + h
            l_ref[:, cols] = jnp.broadcast_to(ml_ref[:, at : at + 1], (BLOCK, HD))

    def store_state():
        lanes = lax.broadcasted_iota(jnp.int32, (BLOCK, HD), 1)
        ml = jnp.zeros((BLOCK, HD), F32)
        for h in range(PER_GROUP):
            cols = slice(h * HD, (h + 1) * HD)
            ml = jnp.where(lanes == h, m_ref[:, cols], ml)
            ml = jnp.where(lanes == PER_GROUP + h, l_ref[:, cols], ml)
        ml_ref[...] = ml
        copies = [copy_in(acc_ref, acc_hbm, n), copy_in(ml_ref, ml_hbm, n + 1)]
        for copy in copies:
            copy.start()
        for copy in copies:
            copy.wait()

    def work(loaded):
        q_copy = copy_in(q_hbm, q_ref, n + 2)
        q_copy.start()
        copies = [copy_in(kv, kv_ref.at[k], k) for k, kv in enumerate(kv_hbm)]
        for copy in copies:
            copy.start()
        if loaded:
            spread_state(loaded)
        q_copy.wait()
        for copy in copies:
            copy.wait()
        if first:
            own_block(kv_ref.at[0])
        lax.fori_loop((BLOCK // TILE) * int(first), (BLOCK // TILE) * n, other_tile, 0)

    some = functools.reduce(jnp.logical_or, active)
    if first:
        work(None)
        store_state()
    elif last:
        loaded = load_state()

        @pl.when(some)
        def _():
            work(loaded)

        @pl.when(jnp.logical_not(some))
        def _():
            spread_state(loaded)

        acc_ref[...] = acc_ref[...] / l_ref[...]
        copy = copy_in(acc_ref, out_hbm, n)
        copy.start()
        copy.wait()
    else:

        @pl.when(some)
        def _():
            work(load_state())
            store_state()


def attend(slots, me, lengths, queries, kvs, state, last=False):
    heads = pltpu.HBM((BLOCK, PER_GROUP * HD), F32)
    sizes = pltpu.HBM((BLOCK, HD), F32)
    operands = [me, *pinned([lengths, queries]), *kvs]
    aliases = {}
    if state is not None:
        if not last:
            aliases = {len(operands): 0, len(operands) + 1: 1}
        operands += pinned(state)
    shapes = (heads,) if last else (heads, sizes)
    work = PER_GROUP * BLOCK * BLOCK * len(slots)
    got = pl.pallas_call(
        functools.partial(attend_kernel, slots, state is None, last),
        out_shape=shapes,
        in_specs=[SMEM] + [HBM] * (len(operands) - 1),
        out_specs=[HBM] * len(shapes),
        scratch_shapes=[
            pltpu.VMEM((BLOCK, PER_GROUP * HD), BF16),
            pltpu.VMEM((len(slots), 2, BLOCK, HD), BF16),
            pltpu.VMEM((BLOCK, PER_GROUP * HD), F32),
            pltpu.VMEM((BLOCK, PER_GROUP * HD), F32),
            pltpu.VMEM((BLOCK, PER_GROUP * HD), F32),
            pltpu.VMEM((BLOCK, HD), F32),
            pltpu.SMEM((TRACES,), jnp.int32),
            pltpu.SemaphoreType.DMA((len(slots) + 3,)),
        ],
        input_output_aliases=aliases,
        compiler_params=pltpu.CompilerParams(vmem_limit_bytes=32 << 20),
        cost_estimate=pl.CostEstimate(
            flops=4 * HD * work, bytes_accessed=4 << 20, transcendentals=work
        ),
        name="attend_%d_%d" % slots[0][:2],
    )(*operands)
    return got[0] if last else got


def pinned(values):
    return [pltpu.with_memory_space_constraint(value, pltpu.HBM) for value in values]


def small_call(kernel, shape, operands, specs=None, **kw):
    return pl.pallas_call(
        kernel,
        out_shape=shape,
        in_specs=specs or [VMEM] * len(operands),
        out_specs=jax.tree.map(lambda _: VMEM, shape),
        compiler_params=pltpu.CompilerParams(vmem_limit_bytes=24 << 20),
        **kw,
    )(*operands)


def project_kernel(got_ref, *refs):
    packs, out_ref, weight_s, sems = refs[:PLANE], refs[PLANE], refs[-2], refs[-1]
    copies = [
        pltpu.make_async_copy(pack, weight_s.at[k], sems.at[k])
        for k, pack in enumerate(packs)
    ]
    for copy in copies:
        copy.start()
    sizes = []
    for z in range(Z):
        stats = []
        for step in range(Z):
            packed = got_ref[z, step * PAD + TRACES : (step + 1) * PAD, :HD]
            for t in range(PAD):
                stats.append(pltpu.roll(packed, (HD - 16 * t) % HD, 1))
        sizes.append(jnp.concatenate(stats, axis=0))
    sizes = [
        size
        + pltpu.roll(size, HD - PER_GROUP, 1)
        + pltpu.roll(size, HD - 2 * PER_GROUP, 1)
        for size in sizes
    ]
    top = functools.reduce(jnp.maximum, sizes)
    weights = [jnp.exp2(size - top) for size in sizes]
    total = functools.reduce(jnp.add, weights)
    weights = [weight / total for weight in weights]
    slot = lax.broadcasted_iota(jnp.int32, (GROUP, HD), 0)
    picked = []
    for h in range(PER_GROUP):
        joined = jnp.zeros((GROUP, HD), F32)
        for z in range(Z):
            joined = joined + got_ref[z, :, h * HD : (h + 1) * HD] * weights[z][:, h : h + 1]
        joined = jnp.where((slot & (PAD - 1)) < TRACES, joined, 0.0)
        picked.append(joined.astype(BF16))
    picked = jnp.concatenate(picked, axis=1)
    for k in range(PLANE):
        copies[k].wait()
        part = jnp.dot(picked, weight_s[k], preferred_element_type=F32)
        out_ref[:, k * 256 : (k + 1) * 256] = part


def inner_kernel(me_ref, total_ref, *refs):
    packs, out_ref, pack_s, sems = refs[:PLANE], refs[PLANE], refs[-2], refs[-1]
    copies = [
        pltpu.make_async_copy(pack, pack_s.at[k], sems.at[k])
        for k, pack in enumerate(packs)
    ]
    for copy in copies:
        copy.start()
    place = me_ref[0] % PLANE
    slot = lax.broadcasted_iota(jnp.int32, (GROUP, TRACES * STEPS), 0)
    at = lax.broadcasted_iota(jnp.int32, (GROUP, TRACES * STEPS), 1)
    trace = slot & (PAD - 1)
    wanted = trace * STEPS + PLANE * (slot >> 3) + place
    chosen = jnp.where((at == wanted) & (trace < TRACES), 1.0, 0.0).astype(BF16)
    for k in range(PLANE):
        copies[k].wait()
        base = jnp.dot(chosen, pack_s[k, WIDE:], preferred_element_type=F32)
        stream = (base + total_ref[:, k * 256 : (k + 1) * 256]).astype(BF16)
        for n in range(4):
            weight = pack_s[k, n * 256 : (n + 1) * 256]
            part = jnp.dot(stream, weight, preferred_element_type=F32)
            cols = slice(n * 256, (n + 1) * 256)
            out_ref[:, cols] = part if k == 0 else out_ref[:, cols] + part


def hidden_kernel(me_ref, inner_ref, class_ref, out_ref):
    hidden = jnp.maximum(inner_ref[...], 0.0).astype(BF16)
    logits = jnp.dot(hidden, class_ref[...], preferred_element_type=F32)
    gap = logits[:, 1:2] - logits[:, 0:1]
    lane = lax.broadcasted_iota(jnp.int32, (PAD, HD), 1)
    mine = jnp.where(lane == me_ref[0], gap, 0.0)
    for k in range(out_ref.shape[0]):
        out_ref[k] = mine


def vote_kernel(prompts, clusters, got_ref, scores_ref, votes_ref):
    gap = jnp.sum(got_ref[...], axis=0)
    scores = 1.0 / (1.0 + jnp.exp(-gap))
    scores_ref[...] = scores[:TRACES, :STEPS]
    lane = lax.broadcasted_iota(jnp.int32, (PAD, HD), 1)
    chain = jnp.min(jnp.where(lane < STEPS, scores, 2.0), axis=1, keepdims=True)
    prompt = lax.broadcasted_iota(jnp.int32, (PROMPTS, CLUSTERS), 0)
    cluster = lax.broadcasted_iota(jnp.int32, (PROMPTS, CLUSTERS), 1)
    votes = jnp.zeros((PROMPTS, CLUSTERS), F32)
    for t in range(TRACES):
        here = (prompt == prompts[t]) & (cluster == clusters[t])
        votes = votes + jnp.where(here, chain[t : t + 1, :], 0.0)
    votes_ref[...] = votes


def swapped(value, axis, bit):
    count = lax.axis_size(axis)
    return lax.ppermute(value, axis, [(s, s ^ bit) for s in range(count)])


def raised(value, planes):
    count = lax.axis_size("ctx")
    steps = planes * PLANE
    return lax.ppermute(value, "ctx", [(s, (s + steps) % count) for s in range(count)])


def per_device(
    queries,
    keys_values,
    trace_lengths,
    step_rows,
    prompt_ids,
    cluster_ids,
    step_stream,
    out_weight,
    score_weight,
    class_weight,
):
    me = lax.axis_index("ctx").astype(jnp.int32).reshape(1)
    columns = [[PLANE * z + j for z in range(Z)] for j in range(PLANE)]
    tie = lambda *values: lax.optimization_barrier(values)
    add = functools.partial(attend, me=me, lengths=trace_lengths, queries=queries)

    kv0 = keys_values
    core0 = swapped(kv0, "ctx", 1)
    kv1 = raised(kv0, 1)

    half = PER_GROUP * HD
    keep, passed, sent = small_call(
        pick_kernel,
        tuple(jax.ShapeDtypeStruct((n * GROUP, half), BF16) for n in (1, 1, 2)),
        [me, *pinned([step_rows, queries])],
        [SMEM, HBM, HBM],
        scratch_shapes=[
            pltpu.VMEM((PLANE * GROUP, half), BF16),
            pltpu.VMEM((TRACES, STEPS), jnp.int32),
            pltpu.VMEM((BLOCK, half), BF16),
            pltpu.SemaphoreType.DMA((2,)),
        ],
        name="pick",
    )
    arrived = swapped(sent, "ctx", 1)
    across = swapped(passed + arrived[GROUP:], "ctx", 2)
    wanted = keep + arrived[:GROUP] + across
    wanted, kv0y, core0, kv1 = tie(wanted, kv0, core0, kv1)
    wanted1, wanted2 = raised(wanted, -1), raised(wanted, -2)
    across0 = swapped(kv0y, "ctx", 2)
    core0y = swapped(core0, "ctx", 2)
    state = add([(0, 0, 0, 0), (0, 1, 1, 0)], kvs=[pinned([kv0y])[0], core0], state=None)
    wanted, wanted1, wanted2, state = tie(wanted, wanted1, wanted2, state)

    parts = small_call(
        picked_kernel,
        jax.ShapeDtypeStruct((GROUP, half), F32),
        [
            me,
            *pinned([trace_lengths, step_rows]),
            wanted,
            wanted1,
            wanted2,
            *pinned([kv0]),
            core0,
            across0,
            core0y,
        ],
        [SMEM, HBM, HBM] + [VMEM] * 3 + [HBM] * 4,
        scratch_shapes=[
            pltpu.VMEM((PLANE, 2, BLOCK, HD), BF16),
            pltpu.SMEM((TRACES,), jnp.int32),
            pltpu.VMEM((TRACES, STEPS), jnp.int32),
            pltpu.SemaphoreType.DMA((PLANE + 2,)),
        ],
        name="picked",
    )
    parts, state, kv1, across0, core0y, weight = tie(
        parts, state, kv1, across0, core0y, out_weight
    )
    across1 = swapped(kv1, "ctx", 2)

    firsts = [weight, swapped(weight, "ctx", 1), swapped(weight, "ctx", 2)]
    firsts.append(swapped(firsts[2], "ctx", 1))
    pack = jnp.concatenate(
        [score_weight[:, n * 256 : (n + 1) * 256] for n in range(4)] + [step_stream], axis=0
    )
    parts = jnp.broadcast_to(parts.astype(jnp.float16)[None], (Z, GROUP, half))
    parts = lax.all_to_all(parts, "ctx", 0, 0, axis_index_groups=columns).astype(F32)
    pair1 = jnp.concatenate([kv1, across1], axis=0)
    cores1 = swapped(pair1, "ctx", 1)
    state = add(
        [(0, 2, 0, 0), (0, 3, 1, 0), (1, 0, 2, 0), (1, 2, 2, 1)],
        kvs=[across0, core0y, pair1],
        state=state,
    )
    parts, state, pair1, cores1, pack = tie(parts, state, pair1, cores1, pack)
    packs = [pack, swapped(pack, "ctx", 1), swapped(pack, "ctx", 2)]
    packs.append(swapped(packs[2], "ctx", 1))

    projected = small_call(
        project_kernel,
        jax.ShapeDtypeStruct((GROUP, WIDE), F32),
        [parts, *firsts],
        [VMEM] + [HBM] * 4,
        scratch_shapes=[
            pltpu.VMEM((PLANE, BLOCK, 256), BF16),
            pltpu.SemaphoreType.DMA((PLANE,)),
        ],
        name="project",
    )
    projected, pair1 = tie((projected * 0.25).astype(jnp.float16), pair1)
    pair2 = raised(pair1, 1)
    projected = projected + swapped(projected, "head", 2)
    projected = projected + swapped(projected, "head", 4)
    projected, cores1 = tie(projected, cores1)
    other = swapped(projected, "head", 1)
    state = add([(1, 1, 0, 0), (1, 3, 0, 1)], kvs=[cores1], state=state)
    other, state, pair2 = tie(other, state, pair2)
    cores2 = swapped(pair2, "ctx", 1)
    projected = (projected.astype(F32) + other.astype(F32)) * 4.0

    inner = small_call(
        inner_kernel,
        jax.ShapeDtypeStruct((GROUP, WIDE), F32),
        [me, projected, *packs],
        [SMEM, VMEM] + [HBM] * 4,
        scratch_shapes=[
            pltpu.VMEM((PLANE, WIDE + TRACES * STEPS, 256), BF16),
            pltpu.SemaphoreType.DMA((PLANE,)),
        ],
        name="inner",
    )
    inner, state, pair2 = tie(inner, state, pair2)
    inner = (inner * 2.0**-10).astype(jnp.float16).reshape(Z, PAD, WIDE)
    state = add([(2, 0, 0, 0), (2, 2, 0, 1)], kvs=[pair2], state=state)
    inner = lax.all_to_all(inner, "ctx", 0, 0, axis_index_groups=columns)
    inner, state = tie(inner, state)
    inner = jnp.sum(inner.astype(F32), axis=0) * 2.0**10
    heads, count = lax.axis_size("head"), lax.axis_size("ctx")
    gap = small_call(
        hidden_kernel,
        jax.ShapeDtypeStruct((heads, PAD, HD), F32),
        [me, inner, class_weight],
        [SMEM, VMEM, VMEM],
        name="hidden",
    )
    gap, state, cores2 = tie(gap, state, cores2)
    attended = add([(2, 1, 0, 0), (2, 3, 0, 1)], kvs=[cores2], state=state, last=True)
    gap = lax.all_to_all(gap, "head", 0, 0)
    gap, attended = tie(gap, attended)
    gap = jnp.sum(gap, axis=0)
    gap = lax.all_to_all(jnp.broadcast_to(gap[None], (count, PAD, HD)), "ctx", 0, 0)
    step_scores, votes = small_call(
        vote_kernel,
        (
            jax.ShapeDtypeStruct((TRACES, STEPS), F32),
            jax.ShapeDtypeStruct((PROMPTS, CLUSTERS), F32),
        ),
        [prompt_ids, cluster_ids, gap],
        [SMEM, SMEM, VMEM],
        name="vote",
    )
    return (attended, step_scores, votes)


def solution(mesh):
    placed = (
        P("ctx", "head"),
        P(None, "ctx", "head"),
        P(),
        P(),
        P(),
        P(),
        P(None, "ctx"),
        P("head", "ctx"),
        P("ctx", "head"),
        P("head", None),
    )
    return jax.shard_map(
        per_device,
        mesh=mesh,
        in_specs=placed,
        out_specs=(P("ctx", "head"), P(), P()),
        check_vma=False,
    )
```

```python
import functools
import math

import jax
import jax.numpy as jnp
from jax import lax
from jax.experimental import pallas as pl
from jax.experimental.pallas import tpu as pltpu
from jax.sharding import PartitionSpec as P

HD = 128
PROMPTS = 2
CLUSTERS = 4
TRACES = 7
STEPS = 32
PER_GROUP = 4
BLOCK = 512
TILE = 256
Z = 8
PLANE = 4
PAD = 8
GROUP = Z * PAD
WIDE = 1024
COEF = HD**-0.5 * math.log2(math.e)
LOW = -1e30
NONE = -60000.0
VMEM = pl.BlockSpec(memory_space=pltpu.VMEM)
SMEM = pl.BlockSpec(memory_space=pltpu.SMEM)
HBM = pl.BlockSpec(memory_space=pltpu.HBM)
BF16 = jnp.bfloat16
F32 = jnp.float32


def first_key(row, lengths):
    start = row * 0
    end = jnp.int32(0)
    for t in range(TRACES):
        end = end + lengths[t]
        start = jnp.where(row >= end, end, start)
    return start


def pick_kernel(me_ref, steps_hbm, q_hbm, keep_ref, pass_ref, send_ref, all_ref, steps_ref, q_ref, sems):
    steps_copy = pltpu.make_async_copy(steps_hbm, steps_ref, sems.at[0])
    q_copy = pltpu.make_async_copy(q_hbm, q_ref, sems.at[1])
    steps_copy.start()
    q_copy.start()
    steps_copy.wait()
    q_copy.wait()
    me = me_ref[0]
    core, side = me % 2, (me // 2) % 2
    at = lax.broadcasted_iota(jnp.int32, (TRACES, BLOCK), 1) + me * BLOCK
    none = jnp.zeros((PAD - TRACES, BLOCK), F32)
    steps = steps_ref[...]
    for c in range(2):
        for y in range(2):
            parts = []
            for z in range(Z):
                step = PLANE * z + 2 * y + c
                parts.append(jnp.where(steps[:, step : step + 1] == at, 1.0, 0.0))
                parts.append(none)
            chosen = jnp.concatenate(parts, axis=0).astype(BF16)
            got = jnp.dot(chosen, q_ref[...], preferred_element_type=F32)
            all_ref[pl.ds((2 * c + y) * GROUP, GROUP), :] = got.astype(BF16)

    def group(c, y):
        return all_ref[pl.ds(pl.multiple_of((2 * c + y) * GROUP, GROUP), GROUP), :]

    keep_ref[...] = group(core, side)
    pass_ref[...] = group(core, 1 - side)
    send_ref[:GROUP] = group(1 - core, side)
    send_ref[GROUP:] = group(1 - core, 1 - side)


def picked_kernel(me_ref, lengths_hbm, steps_hbm, q_ref, q1_ref, q2_ref, *refs):
    kv_refs, out_ref = refs[:PLANE], refs[PLANE]
    kv_s, lengths, steps_ref, sems = refs[-4:]
    lengths_copy = pltpu.make_async_copy(lengths_hbm, lengths, sems.at[PLANE])
    steps_copy = pltpu.make_async_copy(steps_hbm, steps_ref, sems.at[PLANE + 1])
    copies = [
        pltpu.make_async_copy(kv, kv_s.at[k], sems.at[k]) for k, kv in enumerate(kv_refs)
    ]
    for copy in [lengths_copy, steps_copy] + copies:
        copy.start()
    lengths_copy.wait()
    steps_copy.wait()
    me = me_ref[0]
    place = me % PLANE
    steps = steps_ref[...]
    lane = lax.broadcasted_iota(jnp.int32, (TRACES, STEPS), 1)
    none = jnp.full((PAD - TRACES, HD), -1, jnp.int32)
    parts = []
    for z in range(Z):
        mine = jnp.where(lane == PLANE * z + place, steps, 0)
        mine = jnp.sum(mine, axis=1, keepdims=True)
        parts.append(jnp.broadcast_to(mine, (TRACES, HD)))
        parts.append(none)
    row = jnp.concatenate(parts, axis=0)
    start = first_key(row, lengths)
    row = jnp.concatenate([row] * (BLOCK // HD), axis=1)
    start = jnp.concatenate([start] * (BLOCK // HD), axis=1)
    k_pos = lax.broadcasted_iota(jnp.int32, (GROUP, BLOCK), 1)
    q = (q_ref[...].astype(F32) + q1_ref[...].astype(F32) + q2_ref[...].astype(F32)).astype(BF16)
    q = jnp.concatenate([q[:, h * HD : (h + 1) * HD] for h in range(PER_GROUP)], axis=0)
    scores = []
    for k in range(PLANE):
        key0 = (me - place + (place ^ k)) * BLOCK
        mask = (k_pos <= row - key0) & (k_pos >= start - key0)
        mask = jnp.concatenate([mask] * PER_GROUP, axis=0)
        copies[k].wait()
        s = lax.dot_general(
            q, kv_s[k, 0], (((1,), (1,)), ((), ())), preferred_element_type=F32
        )
        scores.append(jnp.where(mask, s, LOW))
    top = jnp.maximum(jnp.maximum(scores[0], scores[1]), jnp.maximum(scores[2], scores[3]))
    top = jnp.maximum(jnp.max(top, axis=1, keepdims=True), 0.1 * LOW)
    ones = jnp.ones((BLOCK, HD), BF16)
    pv = jnp.zeros((PER_GROUP * GROUP, 2 * HD), F32)
    for k, s in enumerate(scores):
        p = jnp.exp2((s - top) * COEF).astype(BF16)
        ext = jnp.concatenate([kv_s[k, 1], ones], axis=1)
        pv = pv + jnp.dot(p, ext, preferred_element_type=F32)
    total = pv[:, HD:]
    some = total > 0.0
    total = jnp.where(some, total, 1.0)
    value = pv[:, :HD] / total
    size = jnp.where(some, top * COEF + jnp.log2(total), NONE)
    lanes = lax.broadcasted_iota(jnp.int32, (GROUP, HD), 1)
    stats = jnp.zeros((GROUP, HD), F32)
    for h in range(PER_GROUP):
        rows = slice(h * GROUP, (h + 1) * GROUP)
        out_ref[:, h * HD : (h + 1) * HD] = value[rows]
        rest = size[rows]
        for k in range(3):
            coarse = rest.astype(BF16).astype(F32)
            stats = jnp.where(lanes == PER_GROUP * k + h, coarse, stats)
            rest = rest - coarse
    for z in range(Z):
        packed = jnp.zeros((1, HD), F32)
        for t in range(TRACES):
            at = z * PAD + t
            packed = packed + pltpu.roll(stats[at : at + 1], 16 * t, 1)
        out_ref[z * PAD + TRACES : (z + 1) * PAD, :HD] = packed


def attend_kernel(slots, first, last, *refs):
    n = len(slots)
    arrays = 1 + max(slot[2] for slot in slots)
    me_ref, lengths_hbm, q_hbm = refs[:3]
    kv_hbm = [refs[3 + array].at[pl.ds(2 * at, 2)] for _, _, array, at in slots]
    if last:
        out_hbm = refs[-9]
    else:
        acc_hbm, ml_hbm = refs[-10:-8]
    if not first:
        acc_in, ml_in = refs[3 + arrays : 5 + arrays]
    q_ref, kv_ref, acc_ref, m_ref, l_ref, ml_ref, lengths, sems = refs[-8:]
    lengths_copy = pltpu.make_async_copy(lengths_hbm, lengths, sems.at[0])
    lengths_copy.start()
    lengths_copy.wait()
    me = me_ref[0]
    place = me % PLANE
    row0 = me * BLOCK
    ones = jnp.ones((BLOCK, HD), BF16)
    blocks = [me - place - back * PLANE + (place ^ flip) for back, flip, _, _ in slots]
    earliest = first_key(row0, lengths)
    active = [(block < me) & ((block + 1) * BLOCK > earliest) for block in blocks]

    def copy_in(source, target, k):
        return pltpu.make_async_copy(source, target, sems.at[k])

    def weigh(rows, count, keys, ext, mask, fresh):
        q = q_ref[rows, :]
        q = jnp.concatenate([q[:, h * HD : (h + 1) * HD] for h in range(PER_GROUP)], axis=0)
        s = lax.dot_general(q, keys, (((1,), (1,)), ((), ())), preferred_element_type=F32)
        for h in range(PER_GROUP):
            cols = slice(h * HD, (h + 1) * HD)
            mine = s[h * count : (h + 1) * count]
            if mask is not None:
                mine = jnp.where(mask, mine, LOW)
            top = jnp.max(mine, axis=1, keepdims=True)
            if fresh:
                top = jnp.broadcast_to(top, (count, HD))
            else:
                before = m_ref[rows, cols]
                top = jnp.maximum(before, top)
            wide = jnp.concatenate([top] * (mine.shape[1] // HD), axis=1)
            p = jnp.exp2((mine - wide) * COEF).astype(BF16)
            pv = jnp.dot(p, ext, preferred_element_type=F32)
            m_ref[rows, cols] = top
            if fresh:
                acc_ref[rows, cols] = pv[:, :HD]
                l_ref[rows, cols] = pv[:, HD:]
            else:
                scale = jnp.exp2((before - top) * COEF)
                acc_ref[rows, cols] = acc_ref[rows, cols] * scale + pv[:, :HD]
                l_ref[rows, cols] = l_ref[rows, cols] * scale + pv[:, HD:]

    def own_block(kv):
        for tile in range(BLOCK // TILE):
            width = (tile + 1) * TILE
            rows = slice(tile * TILE, width)
            keys = kv[0, :width, :]
            ext = jnp.concatenate([kv[1, :width, :], ones[:width]], axis=1)
            q_pos = row0 + tile * TILE + lax.broadcasted_iota(jnp.int32, (TILE, width), 0)
            k_pos = row0 + lax.broadcasted_iota(jnp.int32, (TILE, width), 1)
            starts = first_key(
                row0 + tile * TILE + lax.broadcasted_iota(jnp.int32, (TILE, HD), 0), lengths
            )
            starts = jnp.concatenate([starts] * (width // HD), axis=1)
            mask = (k_pos <= q_pos) & (k_pos >= starts)
            weigh(rows, TILE, keys, ext, mask, True)

    def other_tile(index, carry):
        tile, k = index % (BLOCK // TILE), index // (BLOCK // TILE)
        block = blocks[-1]
        for other in range(n - 1):
            block = jnp.where(k == other, blocks[other], block)
        key0 = block * BLOCK
        begin = pl.multiple_of(tile * TILE, TILE)
        rows = pl.ds(begin, TILE)
        low = first_key(row0 + begin, lengths)
        high = first_key(row0 + begin + TILE - 1, lengths)
        some = (block < me) & (key0 + BLOCK > low)
        every = key0 >= high

        def run(masked):
            keys = kv_ref[k, 0]
            ext = jnp.concatenate([kv_ref[k, 1], ones], axis=1)
            mask = None
            if masked:
                starts = first_key(
                    row0 + begin + lax.broadcasted_iota(jnp.int32, (TILE, HD), 0), lengths
                )
                starts = jnp.concatenate([starts] * (BLOCK // HD), axis=1)
                k_pos = key0 + lax.broadcasted_iota(jnp.int32, (TILE, BLOCK), 1)
                mask = k_pos >= starts
            weigh(rows, TILE, keys, ext, mask, False)

        pl.when(some & every)(functools.partial(run, False))
        pl.when(some & jnp.logical_not(every))(functools.partial(run, True))
        return carry

    def load_state():
        copies = [copy_in(acc_in, acc_ref, n), copy_in(ml_in, ml_ref, n + 1)]
        for copy in copies:
            copy.start()
        return copies

    def spread_state(copies):
        for copy in copies:
            copy.wait()
        for h in range(PER_GROUP):
            cols = slice(h * HD, (h + 1) * HD)
            m_ref[:, cols] = jnp.broadcast_to(ml_ref[:, h : h + 1], (BLOCK, HD))
            at = PER_GROUP + h
            l_ref[:, cols] = jnp.broadcast_to(ml_ref[:, at : at + 1], (BLOCK, HD))

    def store_state():
        lanes = lax.broadcasted_iota(jnp.int32, (BLOCK, HD), 1)
        ml = jnp.zeros((BLOCK, HD), F32)
        for h in range(PER_GROUP):
            cols = slice(h * HD, (h + 1) * HD)
            ml = jnp.where(lanes == h, m_ref[:, cols], ml)
            ml = jnp.where(lanes == PER_GROUP + h, l_ref[:, cols], ml)
        ml_ref[...] = ml
        copies = [copy_in(acc_ref, acc_hbm, n), copy_in(ml_ref, ml_hbm, n + 1)]
        for copy in copies:
            copy.start()
        for copy in copies:
            copy.wait()

    def work(loaded):
        q_copy = copy_in(q_hbm, q_ref, n + 2)
        q_copy.start()
        copies = [copy_in(kv, kv_ref.at[k], k) for k, kv in enumerate(kv_hbm)]
        for copy in copies:
            copy.start()
        if loaded:
            spread_state(loaded)
        q_copy.wait()
        for copy in copies:
            copy.wait()
        if first:
            own_block(kv_ref.at[0])
        lax.fori_loop((BLOCK // TILE) * int(first), (BLOCK // TILE) * n, other_tile, 0)

    some = functools.reduce(jnp.logical_or, active)
    if first:
        work(None)
        store_state()
    elif last:
        loaded = load_state()

        @pl.when(some)
        def _():
            work(loaded)

        @pl.when(jnp.logical_not(some))
        def _():
            spread_state(loaded)

        acc_ref[...] = acc_ref[...] / l_ref[...]
        copy = copy_in(acc_ref, out_hbm, n)
        copy.start()
        copy.wait()
    else:

        @pl.when(some)
        def _():
            work(load_state())
            store_state()


def attend(slots, me, lengths, queries, kvs, state, last=False):
    heads = pltpu.HBM((BLOCK, PER_GROUP * HD), F32)
    sizes = pltpu.HBM((BLOCK, HD), F32)
    operands = [me, *pinned([lengths, queries]), *kvs]
    aliases = {}
    if state is not None:
        if not last:
            aliases = {len(operands): 0, len(operands) + 1: 1}
        operands += pinned(state)
    shapes = (heads,) if last else (heads, sizes)
    work = PER_GROUP * BLOCK * BLOCK * len(slots)
    got = pl.pallas_call(
        functools.partial(attend_kernel, slots, state is None, last),
        out_shape=shapes,
        in_specs=[SMEM] + [HBM] * (len(operands) - 1),
        out_specs=[HBM] * len(shapes),
        scratch_shapes=[
            pltpu.VMEM((BLOCK, PER_GROUP * HD), BF16),
            pltpu.VMEM((len(slots), 2, BLOCK, HD), BF16),
            pltpu.VMEM((BLOCK, PER_GROUP * HD), F32),
            pltpu.VMEM((BLOCK, PER_GROUP * HD), F32),
            pltpu.VMEM((BLOCK, PER_GROUP * HD), F32),
            pltpu.VMEM((BLOCK, HD), F32),
            pltpu.SMEM((TRACES,), jnp.int32),
            pltpu.SemaphoreType.DMA((len(slots) + 3,)),
        ],
        input_output_aliases=aliases,
        compiler_params=pltpu.CompilerParams(vmem_limit_bytes=32 << 20),
        cost_estimate=pl.CostEstimate(
            flops=4 * HD * work, bytes_accessed=4 << 20, transcendentals=work
        ),
        name="attend_%d_%d" % slots[0][:2],
    )(*operands)
    return got[0] if last else got


def pinned(values):
    return [pltpu.with_memory_space_constraint(value, pltpu.HBM) for value in values]


def small_call(kernel, shape, operands, specs=None, **kw):
    return pl.pallas_call(
        kernel,
        out_shape=shape,
        in_specs=specs or [VMEM] * len(operands),
        out_specs=jax.tree.map(lambda _: VMEM, shape),
        compiler_params=pltpu.CompilerParams(vmem_limit_bytes=24 << 20),
        **kw,
    )(*operands)


def project_kernel(got_ref, *refs):
    packs, out_ref, weight_s, sems = refs[:PLANE], refs[PLANE], refs[-2], refs[-1]
    copies = [
        pltpu.make_async_copy(pack, weight_s.at[k], sems.at[k])
        for k, pack in enumerate(packs)
    ]
    for copy in copies:
        copy.start()
    sizes = []
    for z in range(Z):
        stats = []
        for step in range(Z):
            packed = got_ref[z, step * PAD + TRACES : (step + 1) * PAD, :HD]
            for t in range(PAD):
                stats.append(pltpu.roll(packed, (HD - 16 * t) % HD, 1))
        sizes.append(jnp.concatenate(stats, axis=0))
    sizes = [
        size
        + pltpu.roll(size, HD - PER_GROUP, 1)
        + pltpu.roll(size, HD - 2 * PER_GROUP, 1)
        for size in sizes
    ]
    top = functools.reduce(jnp.maximum, sizes)
    weights = [jnp.exp2(size - top) for size in sizes]
    total = functools.reduce(jnp.add, weights)
    weights = [weight / total for weight in weights]
    slot = lax.broadcasted_iota(jnp.int32, (GROUP, HD), 0)
    picked = []
    for h in range(PER_GROUP):
        joined = jnp.zeros((GROUP, HD), F32)
        for z in range(Z):
            joined = joined + got_ref[z, :, h * HD : (h + 1) * HD] * weights[z][:, h : h + 1]
        joined = jnp.where((slot & (PAD - 1)) < TRACES, joined, 0.0)
        picked.append(joined.astype(BF16))
    picked = jnp.concatenate(picked, axis=1)
    for k in range(PLANE):
        copies[k].wait()
        part = jnp.dot(picked, weight_s[k], preferred_element_type=F32)
        out_ref[:, k * 256 : (k + 1) * 256] = part


def inner_kernel(me_ref, total_ref, *refs):
    packs, out_ref, pack_s, sems = refs[:PLANE], refs[PLANE], refs[-2], refs[-1]
    copies = [
        pltpu.make_async_copy(pack, pack_s.at[k], sems.at[k])
        for k, pack in enumerate(packs)
    ]
    for copy in copies:
        copy.start()
    place = me_ref[0] % PLANE
    slot = lax.broadcasted_iota(jnp.int32, (GROUP, TRACES * STEPS), 0)
    at = lax.broadcasted_iota(jnp.int32, (GROUP, TRACES * STEPS), 1)
    trace = slot & (PAD - 1)
    wanted = trace * STEPS + PLANE * (slot >> 3) + place
    chosen = jnp.where((at == wanted) & (trace < TRACES), 1.0, 0.0).astype(BF16)
    for k in range(PLANE):
        copies[k].wait()
        base = jnp.dot(chosen, pack_s[k, WIDE:], preferred_element_type=F32)
        stream = (base + total_ref[:, k * 256 : (k + 1) * 256]).astype(BF16)
        for n in range(4):
            weight = pack_s[k, n * 256 : (n + 1) * 256]
            part = jnp.dot(stream, weight, preferred_element_type=F32)
            cols = slice(n * 256, (n + 1) * 256)
            out_ref[:, cols] = part if k == 0 else out_ref[:, cols] + part


def hidden_kernel(inner_ref, class_ref, out_ref):
    hidden = jnp.maximum(inner_ref[...], 0.0).astype(BF16)
    logits = jnp.dot(hidden, class_ref[...], preferred_element_type=F32)
    gap = logits[:, 1:2] - logits[:, 0:1]
    lane = lax.broadcasted_iota(jnp.int32, (PAD, HD), 1)
    row = lax.broadcasted_iota(jnp.int32, (PAD, HD), 0)
    mine = jnp.sum(jnp.where(lane == row, gap, 0.0), axis=0, keepdims=True)
    for k in range(out_ref.shape[0]):
        out_ref[k] = mine


def vote_kernel(prompts, clusters, got_ref, scores_ref, votes_ref):
    gap = jnp.concatenate([got_ref[k] for k in range(STEPS)], axis=0)
    scores = 1.0 / (1.0 + jnp.exp(-gap.T[:PAD]))
    scores_ref[...] = scores[:TRACES]
    chain = jnp.min(scores, axis=1, keepdims=True)
    prompt = lax.broadcasted_iota(jnp.int32, (PROMPTS, CLUSTERS), 0)
    cluster = lax.broadcasted_iota(jnp.int32, (PROMPTS, CLUSTERS), 1)
    votes = jnp.zeros((PROMPTS, CLUSTERS), F32)
    for t in range(TRACES):
        here = (prompt == prompts[t]) & (cluster == clusters[t])
        votes = votes + jnp.where(here, chain[t : t + 1, :], 0.0)
    votes_ref[...] = votes


def swapped(value, axis, bit):
    count = lax.axis_size(axis)
    return lax.ppermute(value, axis, [(s, s ^ bit) for s in range(count)])


def raised(value, planes):
    count = lax.axis_size("ctx")
    steps = planes * PLANE
    return lax.ppermute(value, "ctx", [(s, (s + steps) % count) for s in range(count)])


def per_device(
    queries,
    keys_values,
    trace_lengths,
    step_rows,
    prompt_ids,
    cluster_ids,
    step_stream,
    out_weight,
    score_weight,
    class_weight,
):
    me = lax.axis_index("ctx").astype(jnp.int32).reshape(1)
    columns = [[PLANE * z + j for z in range(Z)] for j in range(PLANE)]
    tie = lambda *values: lax.optimization_barrier(values)
    add = functools.partial(attend, me=me, lengths=trace_lengths, queries=queries)

    kv0 = keys_values
    core0 = swapped(kv0, "ctx", 1)

    half = PER_GROUP * HD
    keep, passed, sent = small_call(
        pick_kernel,
        tuple(jax.ShapeDtypeStruct((n * GROUP, half), BF16) for n in (1, 1, 2)),
        [me, *pinned([step_rows, queries])],
        [SMEM, HBM, HBM],
        scratch_shapes=[
            pltpu.VMEM((PLANE * GROUP, half), BF16),
            pltpu.VMEM((TRACES, STEPS), jnp.int32),
            pltpu.VMEM((BLOCK, half), BF16),
            pltpu.SemaphoreType.DMA((2,)),
        ],
        name="pick",
    )
    arrived = swapped(sent, "ctx", 1)
    across0 = swapped(kv0, "ctx", 2)
    core0y = swapped(core0, "ctx", 2)
    across = swapped(passed + arrived[GROUP:], "ctx", 2)
    wanted = keep + arrived[:GROUP] + across
    wanted1, wanted2 = raised(wanted, -1), raised(wanted, -2)
    wanted, own_kv, core0, across0 = tie(wanted, kv0, core0, across0)
    state = add([(0, 0, 0, 0), (0, 1, 1, 0)], kvs=[pinned([own_kv])[0], core0], state=None)
    wanted, wanted1, wanted2, state = tie(wanted, wanted1, wanted2, state)

    weight, wanted = tie(out_weight, wanted)
    firsts = [weight, swapped(weight, "ctx", 1), swapped(weight, "ctx", 2)]
    firsts.append(swapped(firsts[2], "ctx", 1))
    pack = jnp.concatenate(
        [score_weight[:, n * 256 : (n + 1) * 256] for n in range(4)] + [step_stream], axis=0
    )
    kv1, _ = tie(raised(kv0, 1), wanted)

    parts = small_call(
        picked_kernel,
        jax.ShapeDtypeStruct((GROUP, half), F32),
        [
            me,
            *pinned([trace_lengths, step_rows]),
            wanted,
            wanted1,
            wanted2,
            *pinned([kv0]),
            core0,
            across0,
            core0y,
        ],
        [SMEM, HBM, HBM] + [VMEM] * 3 + [HBM] * 4,
        scratch_shapes=[
            pltpu.VMEM((PLANE, 2, BLOCK, HD), BF16),
            pltpu.SMEM((TRACES,), jnp.int32),
            pltpu.VMEM((TRACES, STEPS), jnp.int32),
            pltpu.SemaphoreType.DMA((PLANE + 2,)),
        ],
        name="picked",
    )
    parts, state, kv1, across0, core0y = tie(parts, state, kv1, across0, core0y)
    across1 = swapped(kv1, "ctx", 2)
    parts = jnp.broadcast_to(parts.astype(jnp.float16)[None], (Z, GROUP, half))
    parts = lax.all_to_all(parts, "ctx", 0, 0, axis_index_groups=columns).astype(F32)
    pair1 = jnp.concatenate([kv1, across1], axis=0)
    *firsts, pair1, pack = tie(*firsts, pair1, pack)
    cores1 = swapped(pair1, "ctx", 1)
    state = add(
        [(0, 2, 0, 0), (0, 3, 1, 0), (1, 0, 2, 0), (1, 2, 2, 1)],
        kvs=[across0, core0y, pair1],
        state=state,
    )
    parts, state, pair1, cores1, pack = tie(parts, state, pair1, cores1, pack)
    packs = [pack, swapped(pack, "ctx", 1), swapped(pack, "ctx", 2)]

    projected = small_call(
        project_kernel,
        jax.ShapeDtypeStruct((GROUP, WIDE), F32),
        [parts, *firsts],
        [VMEM] + [HBM] * 4,
        scratch_shapes=[
            pltpu.VMEM((PLANE, BLOCK, 256), BF16),
            pltpu.SemaphoreType.DMA((PLANE,)),
        ],
        name="project",
    )
    projected, pair1 = tie((projected * 0.25).astype(jnp.float16), pair1)
    pair2 = raised(pair1, 1)
    projected = projected + swapped(projected, "head", 2)
    projected = projected + swapped(projected, "head", 4)
    projected, cores1, packs[2] = tie(projected, cores1, packs[2])
    packs.append(swapped(packs[2], "ctx", 1))
    other = swapped(projected, "head", 1)
    state = add([(1, 1, 0, 0), (1, 3, 0, 1)], kvs=[cores1], state=state)
    other, state, pair2 = tie(other, state, pair2)
    cores2 = swapped(pair2, "ctx", 1)
    projected = (projected.astype(F32) + other.astype(F32)) * 4.0

    inner = small_call(
        inner_kernel,
        jax.ShapeDtypeStruct((GROUP, WIDE), F32),
        [me, projected, *packs],
        [SMEM, VMEM] + [HBM] * 4,
        scratch_shapes=[
            pltpu.VMEM((PLANE, WIDE + TRACES * STEPS, 256), BF16),
            pltpu.SemaphoreType.DMA((PLANE,)),
        ],
        name="inner",
    )
    inner, state, pair2 = tie(inner, state, pair2)
    inner = (inner * 2.0**-10).astype(jnp.float16).reshape(Z, PAD, WIDE)
    state = add([(2, 0, 0, 0), (2, 2, 0, 1)], kvs=[pair2], state=state)
    inner = lax.all_to_all(inner, "ctx", 0, 0, axis_index_groups=columns)
    inner, state = tie(inner, state)
    inner = jnp.sum(inner.astype(F32), axis=0) * 2.0**10
    heads, count = lax.axis_size("head"), lax.axis_size("ctx")
    gap = small_call(
        hidden_kernel,
        jax.ShapeDtypeStruct((heads, 1, HD), F32),
        [inner, class_weight],
        name="hidden",
    )
    gap, state, cores2 = tie(gap, state, cores2)
    attended = add([(2, 1, 0, 0), (2, 3, 0, 1)], kvs=[cores2], state=state, last=True)
    gap = lax.all_to_all(gap, "head", 0, 0)
    gap, attended = tie(gap, attended)
    gap = jnp.sum(gap, axis=0)
    gap = lax.all_to_all(jnp.broadcast_to(gap[None], (count, 1, HD)), "ctx", 0, 0)
    step_scores, votes = small_call(
        vote_kernel,
        (
            jax.ShapeDtypeStruct((TRACES, STEPS), F32),
            jax.ShapeDtypeStruct((PROMPTS, CLUSTERS), F32),
        ),
        [prompt_ids, cluster_ids, gap],
        [SMEM, SMEM, VMEM],
        name="vote",
    )
    return (attended, step_scores, votes)


def solution(mesh):
    placed = (
        P("ctx", "head"),
        P(None, "ctx", "head"),
        P(),
        P(),
        P(),
        P(),
        P(None, "ctx"),
        P("head", "ctx"),
        P("ctx", "head"),
        P("head", None),
    )
    return jax.shard_map(
        per_device,
        mesh=mesh,
        in_specs=placed,
        out_specs=(P("ctx", "head"), P(), P()),
        check_vma=False,
    )
```

```python
import functools
import math

import jax
import jax.numpy as jnp
from jax import lax
from jax.experimental import pallas as pl
from jax.experimental.pallas import tpu as pltpu
from jax.sharding import PartitionSpec as P

HD = 128
PROMPTS = 2
CLUSTERS = 4
TRACES = 7
STEPS = 32
PER_GROUP = 4
BLOCK = 512
TILE = 512
OWN_TILE = 256
Z = 8
PLANE = 4
PAD = 8
GROUP = Z * PAD
WIDE = 1024
COEF = HD**-0.5 * math.log2(math.e)
LOW = -1e30
NONE = -60000.0
VMEM = pl.BlockSpec(memory_space=pltpu.VMEM)
SMEM = pl.BlockSpec(memory_space=pltpu.SMEM)
HBM = pl.BlockSpec(memory_space=pltpu.HBM)
BF16 = jnp.bfloat16
F32 = jnp.float32


def first_key(row, lengths):
    start = row * 0
    end = jnp.int32(0)
    for t in range(TRACES):
        end = end + lengths[t]
        start = jnp.where(row >= end, end, start)
    return start


def pick_kernel(me_ref, steps_hbm, q_hbm, keep_ref, pass_ref, send_ref, all_ref, steps_ref, q_ref, sems):
    steps_copy = pltpu.make_async_copy(steps_hbm, steps_ref, sems.at[0])
    q_copy = pltpu.make_async_copy(q_hbm, q_ref, sems.at[1])
    steps_copy.start()
    q_copy.start()
    steps_copy.wait()
    q_copy.wait()
    me = me_ref[0]
    core, side = me % 2, (me // 2) % 2
    at = lax.broadcasted_iota(jnp.int32, (TRACES, BLOCK), 1) + me * BLOCK
    none = jnp.zeros((PAD - TRACES, BLOCK), F32)
    steps = steps_ref[...]
    for c in range(2):
        for y in range(2):
            parts = []
            for z in range(Z):
                step = PLANE * z + 2 * y + c
                parts.append(jnp.where(steps[:, step : step + 1] == at, 1.0, 0.0))
                parts.append(none)
            chosen = jnp.concatenate(parts, axis=0).astype(BF16)
            got = jnp.dot(chosen, q_ref[...], preferred_element_type=F32)
            all_ref[pl.ds((2 * c + y) * GROUP, GROUP), :] = got.astype(BF16)

    def group(c, y):
        return all_ref[pl.ds(pl.multiple_of((2 * c + y) * GROUP, GROUP), GROUP), :]

    keep_ref[...] = group(core, side)
    pass_ref[...] = group(core, 1 - side)
    send_ref[:GROUP] = group(1 - core, side)
    send_ref[GROUP:] = group(1 - core, 1 - side)


def picked_kernel(me_ref, lengths_hbm, steps_hbm, q_ref, q1_ref, q2_ref, *refs):
    kv_refs, out_ref = refs[:PLANE], refs[PLANE]
    kv_s, lengths, steps_ref, sems = refs[-4:]
    lengths_copy = pltpu.make_async_copy(lengths_hbm, lengths, sems.at[PLANE])
    steps_copy = pltpu.make_async_copy(steps_hbm, steps_ref, sems.at[PLANE + 1])
    copies = [
        pltpu.make_async_copy(kv, kv_s.at[k], sems.at[k]) for k, kv in enumerate(kv_refs)
    ]
    for copy in [lengths_copy, steps_copy] + copies:
        copy.start()
    lengths_copy.wait()
    steps_copy.wait()
    me = me_ref[0]
    place = me % PLANE
    steps = steps_ref[...]
    lane = lax.broadcasted_iota(jnp.int32, (TRACES, STEPS), 1)
    none = jnp.full((PAD - TRACES, HD), -1, jnp.int32)
    parts = []
    for z in range(Z):
        mine = jnp.where(lane == PLANE * z + place, steps, 0)
        mine = jnp.sum(mine, axis=1, keepdims=True)
        parts.append(jnp.broadcast_to(mine, (TRACES, HD)))
        parts.append(none)
    row = jnp.concatenate(parts, axis=0)
    start = first_key(row, lengths)
    row = jnp.concatenate([row] * (BLOCK // HD), axis=1)
    start = jnp.concatenate([start] * (BLOCK // HD), axis=1)
    k_pos = lax.broadcasted_iota(jnp.int32, (GROUP, BLOCK), 1)
    q = (q_ref[...].astype(F32) + q1_ref[...].astype(F32) + q2_ref[...].astype(F32)).astype(BF16)
    q = jnp.concatenate([q[:, h * HD : (h + 1) * HD] for h in range(PER_GROUP)], axis=0)
    scores = []
    for k in range(PLANE):
        key0 = (me - place + (place ^ k)) * BLOCK
        mask = (k_pos <= row - key0) & (k_pos >= start - key0)
        mask = jnp.concatenate([mask] * PER_GROUP, axis=0)
        copies[k].wait()
        s = lax.dot_general(
            q, kv_s[k, 0], (((1,), (1,)), ((), ())), preferred_element_type=F32
        )
        scores.append(jnp.where(mask, s, LOW))
    top = jnp.maximum(jnp.maximum(scores[0], scores[1]), jnp.maximum(scores[2], scores[3]))
    top = jnp.maximum(jnp.max(top, axis=1, keepdims=True), 0.1 * LOW)
    ones = jnp.ones((BLOCK, HD), BF16)
    pv = jnp.zeros((PER_GROUP * GROUP, 2 * HD), F32)
    for k, s in enumerate(scores):
        p = jnp.exp2((s - top) * COEF).astype(BF16)
        ext = jnp.concatenate([kv_s[k, 1], ones], axis=1)
        pv = pv + jnp.dot(p, ext, preferred_element_type=F32)
    total = pv[:, HD:]
    some = total > 0.0
    total = jnp.where(some, total, 1.0)
    value = pv[:, :HD] / total
    size = jnp.where(some, top * COEF + jnp.log2(total), NONE)
    lanes = lax.broadcasted_iota(jnp.int32, (GROUP, HD), 1)
    stats = jnp.zeros((GROUP, HD), F32)
    for h in range(PER_GROUP):
        rows = slice(h * GROUP, (h + 1) * GROUP)
        out_ref[:, h * HD : (h + 1) * HD] = value[rows]
        rest = size[rows]
        for k in range(3):
            coarse = rest.astype(BF16).astype(F32)
            stats = jnp.where(lanes == PER_GROUP * k + h, coarse, stats)
            rest = rest - coarse
    for z in range(Z):
        packed = jnp.zeros((1, HD), F32)
        for t in range(TRACES):
            at = z * PAD + t
            packed = packed + pltpu.roll(stats[at : at + 1], 16 * t, 1)
        out_ref[z * PAD + TRACES : (z + 1) * PAD, :HD] = packed


def attend_kernel(slots, first, last, *refs):
    n = len(slots)
    arrays = 1 + max(slot[2] for slot in slots)
    me_ref, lengths_hbm, q_ref = refs[:3]
    kv_hbm = [refs[3 + array].at[pl.ds(2 * at, 2)] for _, _, array, at in slots]
    kv_ref, lengths, sems = refs[-3:]
    if first:
        q_hbm = q_ref
        q_ref, m_ref, l_ref, acc_ref = refs[3 + arrays : 7 + arrays]
    else:
        m_ref, l_ref, acc_ref = refs[3 + arrays : 6 + arrays]
    copies = [
        pltpu.make_async_copy(kv, kv_ref.at[k], sems.at[k]) for k, kv in enumerate(kv_hbm)
    ]
    copies.append(pltpu.make_async_copy(lengths_hbm, lengths, sems.at[n]))
    if first:
        copies.append(pltpu.make_async_copy(q_hbm, q_ref, sems.at[n + 1]))
    for copy in copies:
        copy.start()
    for copy in copies:
        copy.wait()
    me = me_ref[0]
    place = me % PLANE
    row0 = me * BLOCK
    ones = jnp.ones((BLOCK, HD), BF16)
    blocks = [me - place - back * PLANE + (place ^ flip) for back, flip, _, _ in slots]

    def weigh(rows, count, keys, ext, mask, fresh):
        q = q_ref[rows, :]
        q = jnp.concatenate([q[:, h * HD : (h + 1) * HD] for h in range(PER_GROUP)], axis=0)
        s = lax.dot_general(q, keys, (((1,), (1,)), ((), ())), preferred_element_type=F32)
        for h in range(PER_GROUP):
            cols = slice(h * HD, (h + 1) * HD)
            mine = s[h * count : (h + 1) * count]
            if mask is not None:
                mine = jnp.where(mask, mine, LOW)
            top = jnp.max(mine, axis=1, keepdims=True)
            if fresh:
                top = jnp.broadcast_to(top, (count, HD))
            else:
                before = m_ref[rows, cols]
                top = jnp.maximum(before, top)
            wide = jnp.concatenate([top] * (mine.shape[1] // HD), axis=1)
            p = jnp.exp2((mine - wide) * COEF).astype(BF16)
            pv = jnp.dot(p, ext, preferred_element_type=F32)
            m_ref[rows, cols] = top
            if fresh:
                acc_ref[rows, cols] = pv[:, :HD]
                l_ref[rows, cols] = pv[:, HD:]
            else:
                scale = jnp.exp2((before - top) * COEF)
                acc_ref[rows, cols] = acc_ref[rows, cols] * scale + pv[:, :HD]
                l_ref[rows, cols] = l_ref[rows, cols] * scale + pv[:, HD:]

    def own_block():
        for tile in range(BLOCK // OWN_TILE):
            width = (tile + 1) * OWN_TILE
            rows = slice(tile * OWN_TILE, width)
            keys = kv_ref[0, 0, :width, :]
            ext = jnp.concatenate([kv_ref[0, 1, :width, :], ones[:width]], axis=1)
            shape = (OWN_TILE, width)
            q_pos = row0 + tile * OWN_TILE + lax.broadcasted_iota(jnp.int32, shape, 0)
            k_pos = row0 + lax.broadcasted_iota(jnp.int32, shape, 1)
            starts = first_key(q_pos[:, :HD], lengths)
            starts = jnp.concatenate([starts] * (width // HD), axis=1)
            mask = (k_pos <= q_pos) & (k_pos >= starts)
            weigh(rows, OWN_TILE, keys, ext, mask, True)

    def other_tile(index, carry):
        tile, k = index % (BLOCK // TILE), index // (BLOCK // TILE)
        block = blocks[-1]
        for other in range(n - 1):
            block = jnp.where(k == other, blocks[other], block)
        key0 = block * BLOCK
        begin = pl.multiple_of(tile * TILE, TILE)
        rows = pl.ds(begin, TILE)
        low = first_key(row0 + begin, lengths)
        high = first_key(row0 + begin + TILE - 1, lengths)
        some = (block < me) & (key0 + BLOCK > low)
        every = key0 >= high

        def run(masked):
            keys = kv_ref[k, 0]
            ext = jnp.concatenate([kv_ref[k, 1], ones], axis=1)
            mask = None
            if masked:
                starts = first_key(
                    row0 + begin + lax.broadcasted_iota(jnp.int32, (TILE, HD), 0), lengths
                )
                starts = jnp.concatenate([starts] * (BLOCK // HD), axis=1)
                k_pos = key0 + lax.broadcasted_iota(jnp.int32, (TILE, BLOCK), 1)
                mask = k_pos >= starts
            weigh(rows, TILE, keys, ext, mask, False)

        pl.when(some & every)(functools.partial(run, False))
        pl.when(some & jnp.logical_not(every))(functools.partial(run, True))
        return carry

    if first:
        own_block()
    tiles = BLOCK // TILE
    lax.fori_loop(tiles * int(first), tiles * n, other_tile, 0)
    if last:
        out_ref = refs[-4]
        out_ref[...] = acc_ref[...] / l_ref[...]


def attend(slots, me, lengths, queries, kvs, state, last=False):
    shape = (BLOCK, PER_GROUP * HD)
    first = state is None
    operands = [me, *pinned([lengths, queries] if first else [lengths]), *kvs]
    specs = [SMEM] + [HBM] * (len(operands) - 1)
    if not first:
        q, *sums = [pltpu.with_memory_space_constraint(x, pltpu.VMEM) for x in state]
        operands[2:2] = [q]
        specs[2:2] = [VMEM]
        at = len(operands)
        operands += sums
        specs += [VMEM] * 3
    if last:
        shapes, aliases = (jax.ShapeDtypeStruct(shape, F32),), {}
    elif first:
        shapes, aliases = (pltpu.VMEM(shape, BF16),) + (pltpu.VMEM(shape, F32),) * 3, {}
    else:
        shapes, aliases = (pltpu.VMEM(shape, F32),) * 3, {at + k: k for k in range(3)}
    work = PER_GROUP * BLOCK * BLOCK * len(slots)
    got = pl.pallas_call(
        functools.partial(attend_kernel, slots, first, last),
        out_shape=shapes,
        in_specs=specs,
        out_specs=[VMEM] * len(shapes),
        scratch_shapes=[
            pltpu.VMEM((len(slots), 2, BLOCK, HD), BF16),
            pltpu.SMEM((TRACES,), jnp.int32),
            pltpu.SemaphoreType.DMA((len(slots) + 2,)),
        ],
        input_output_aliases=aliases,
        compiler_params=pltpu.CompilerParams(vmem_limit_bytes=32 << 20),
        cost_estimate=pl.CostEstimate(
            flops=4 * HD * work, bytes_accessed=1 << 20, transcendentals=work
        ),
        name="attend_%d_%d" % slots[0][:2],
    )(*operands)
    if last:
        return got[0]
    return list(got) if first else [q, *got]


def pinned(values):
    return [pltpu.with_memory_space_constraint(value, pltpu.HBM) for value in values]


def small_call(kernel, shape, operands, specs=None, **kw):
    return pl.pallas_call(
        kernel,
        out_shape=shape,
        in_specs=specs or [VMEM] * len(operands),
        out_specs=jax.tree.map(lambda _: VMEM, shape),
        compiler_params=pltpu.CompilerParams(vmem_limit_bytes=24 << 20),
        **kw,
    )(*operands)


def project_kernel(got_ref, *refs):
    packs, out_ref, weight_s, sems = refs[:PLANE], refs[PLANE], refs[-2], refs[-1]
    copies = [
        pltpu.make_async_copy(pack, weight_s.at[k], sems.at[k])
        for k, pack in enumerate(packs)
    ]
    for copy in copies:
        copy.start()
    sizes = []
    for z in range(Z):
        stats = []
        for step in range(Z):
            packed = got_ref[z, step * PAD + TRACES : (step + 1) * PAD, :HD]
            for t in range(PAD):
                stats.append(pltpu.roll(packed, (HD - 16 * t) % HD, 1))
        sizes.append(jnp.concatenate(stats, axis=0))
    sizes = [
        size
        + pltpu.roll(size, HD - PER_GROUP, 1)
        + pltpu.roll(size, HD - 2 * PER_GROUP, 1)
        for size in sizes
    ]
    top = functools.reduce(jnp.maximum, sizes)
    weights = [jnp.exp2(size - top) for size in sizes]
    total = functools.reduce(jnp.add, weights)
    weights = [weight / total for weight in weights]
    slot = lax.broadcasted_iota(jnp.int32, (GROUP, HD), 0)
    picked = []
    for h in range(PER_GROUP):
        joined = jnp.zeros((GROUP, HD), F32)
        for z in range(Z):
            joined = joined + got_ref[z, :, h * HD : (h + 1) * HD] * weights[z][:, h : h + 1]
        joined = jnp.where((slot & (PAD - 1)) < TRACES, joined, 0.0)
        picked.append(joined.astype(BF16))
    picked = jnp.concatenate(picked, axis=1)
    for k in range(PLANE):
        copies[k].wait()
        part = jnp.dot(picked, weight_s[k], preferred_element_type=F32)
        out_ref[:, k * 256 : (k + 1) * 256] = part


def inner_kernel(me_ref, total_ref, *refs):
    packs, out_ref, pack_s, sems = refs[:PLANE], refs[PLANE], refs[-2], refs[-1]
    copies = [
        pltpu.make_async_copy(pack, pack_s.at[k], sems.at[k])
        for k, pack in enumerate(packs)
    ]
    for copy in copies:
        copy.start()
    place = me_ref[0] % PLANE
    slot = lax.broadcasted_iota(jnp.int32, (GROUP, TRACES * STEPS), 0)
    at = lax.broadcasted_iota(jnp.int32, (GROUP, TRACES * STEPS), 1)
    trace = slot & (PAD - 1)
    wanted = trace * STEPS + PLANE * (slot >> 3) + place
    chosen = jnp.where((at == wanted) & (trace < TRACES), 1.0, 0.0).astype(BF16)
    for k in range(PLANE):
        copies[k].wait()
        base = jnp.dot(chosen, pack_s[k, WIDE:], preferred_element_type=F32)
        stream = (base + total_ref[:, k * 256 : (k + 1) * 256]).astype(BF16)
        for n in range(4):
            weight = pack_s[k, n * 256 : (n + 1) * 256]
            part = jnp.dot(stream, weight, preferred_element_type=F32)
            cols = slice(n * 256, (n + 1) * 256)
            out_ref[:, cols] = part if k == 0 else out_ref[:, cols] + part


def hidden_kernel(inner_ref, class_ref, out_ref):
    hidden = jnp.maximum(inner_ref[...], 0.0).astype(BF16)
    logits = jnp.dot(hidden, class_ref[...], preferred_element_type=F32)
    gap = logits[:, 1:2] - logits[:, 0:1]
    lane = lax.broadcasted_iota(jnp.int32, (PAD, HD), 1)
    row = lax.broadcasted_iota(jnp.int32, (PAD, HD), 0)
    mine = jnp.sum(jnp.where(lane == row, gap, 0.0), axis=0, keepdims=True)
    for k in range(out_ref.shape[0]):
        out_ref[k] = mine


def vote_kernel(prompts, clusters, got_ref, scores_ref, votes_ref):
    gap = jnp.concatenate([got_ref[k] for k in range(STEPS)], axis=0)
    scores = 1.0 / (1.0 + jnp.exp(-gap.T[:PAD]))
    scores_ref[...] = scores[:TRACES]
    chain = jnp.min(scores, axis=1, keepdims=True)
    prompt = lax.broadcasted_iota(jnp.int32, (PROMPTS, CLUSTERS), 0)
    cluster = lax.broadcasted_iota(jnp.int32, (PROMPTS, CLUSTERS), 1)
    votes = jnp.zeros((PROMPTS, CLUSTERS), F32)
    for t in range(TRACES):
        here = (prompt == prompts[t]) & (cluster == clusters[t])
        votes = votes + jnp.where(here, chain[t : t + 1, :], 0.0)
    votes_ref[...] = votes


def swapped(value, axis, bit):
    count = lax.axis_size(axis)
    return lax.ppermute(value, axis, [(s, s ^ bit) for s in range(count)])


def raised(value, planes):
    count = lax.axis_size("ctx")
    steps = planes * PLANE
    return lax.ppermute(value, "ctx", [(s, (s + steps) % count) for s in range(count)])


def per_device(
    queries,
    keys_values,
    trace_lengths,
    step_rows,
    prompt_ids,
    cluster_ids,
    step_stream,
    out_weight,
    score_weight,
    class_weight,
):
    me = lax.axis_index("ctx").astype(jnp.int32).reshape(1)
    columns = [[PLANE * z + j for z in range(Z)] for j in range(PLANE)]
    tie = lambda *values: lax.optimization_barrier(values)
    add = functools.partial(attend, me=me, lengths=trace_lengths, queries=queries)

    kv0 = keys_values
    core0 = swapped(kv0, "ctx", 1)

    half = PER_GROUP * HD
    keep, passed, sent = small_call(
        pick_kernel,
        tuple(jax.ShapeDtypeStruct((n * GROUP, half), BF16) for n in (1, 1, 2)),
        [me, *pinned([step_rows, queries])],
        [SMEM, HBM, HBM],
        scratch_shapes=[
            pltpu.VMEM((PLANE * GROUP, half), BF16),
            pltpu.VMEM((TRACES, STEPS), jnp.int32),
            pltpu.VMEM((BLOCK, half), BF16),
            pltpu.SemaphoreType.DMA((2,)),
        ],
        name="pick",
    )
    arrived = swapped(sent, "ctx", 1)
    across = swapped(passed + arrived[GROUP:], "ctx", 2)
    wanted = keep + arrived[:GROUP] + across
    wanted, kv0y, core0 = tie(wanted, kv0, core0)
    wanted1, wanted2 = raised(wanted, -1), raised(wanted, -2)
    across0 = swapped(kv0y, "ctx", 2)
    across0, wanted1 = tie(across0, wanted1)
    core0y = swapped(across0, "ctx", 1)
    state = add([(0, 0, 0, 0), (0, 1, 1, 0)], kvs=[pinned([kv0y])[0], core0], state=None)
    wanted, wanted1, wanted2, *state = tie(wanted, wanted1, wanted2, *state)

    weight, wanted = tie(out_weight, wanted)
    firsts = [weight, swapped(weight, "ctx", 1), swapped(weight, "ctx", 2)]
    firsts.append(swapped(firsts[2], "ctx", 1))
    pack = jnp.concatenate(
        [score_weight[:, n * 256 : (n + 1) * 256] for n in range(4)] + [step_stream], axis=0
    )
    kv1, _ = tie(raised(kv0, 1), wanted)

    parts = small_call(
        picked_kernel,
        jax.ShapeDtypeStruct((GROUP, half), F32),
        [
            me,
            *pinned([trace_lengths, step_rows]),
            wanted,
            wanted1,
            wanted2,
            *pinned([kv0]),
            core0,
            across0,
            core0y,
        ],
        [SMEM, HBM, HBM] + [VMEM] * 3 + [HBM] * 4,
        scratch_shapes=[
            pltpu.VMEM((PLANE, 2, BLOCK, HD), BF16),
            pltpu.SMEM((TRACES,), jnp.int32),
            pltpu.VMEM((TRACES, STEPS), jnp.int32),
            pltpu.SemaphoreType.DMA((PLANE + 2,)),
        ],
        name="picked",
    )
    parts, kv1, across0, core0y, *state = tie(parts, kv1, across0, core0y, *state)
    across1 = swapped(kv1, "ctx", 2)
    parts = jnp.broadcast_to(parts.astype(jnp.float16)[None], (Z, GROUP, half))
    parts = lax.all_to_all(parts, "ctx", 0, 0, axis_index_groups=columns).astype(F32)
    pair1 = jnp.concatenate([kv1, across1], axis=0)
    *firsts, pair1, pack = tie(*firsts, pair1, pack)
    cores1 = swapped(pair1, "ctx", 1)
    state = add(
        [(0, 2, 0, 0), (0, 3, 1, 0), (1, 0, 2, 0), (1, 2, 2, 1)],
        kvs=[across0, core0y, pair1],
        state=state,
    )
    parts, pair1, cores1, pack, *state = tie(parts, pair1, cores1, pack, *state)
    packs = [pack, swapped(pack, "ctx", 1), swapped(pack, "ctx", 2)]

    projected = small_call(
        project_kernel,
        jax.ShapeDtypeStruct((GROUP, WIDE), F32),
        [parts, *firsts],
        [VMEM] + [HBM] * 4,
        scratch_shapes=[
            pltpu.VMEM((PLANE, BLOCK, 256), BF16),
            pltpu.SemaphoreType.DMA((PLANE,)),
        ],
        name="project",
    )
    projected, pair1 = tie((projected * 0.25).astype(jnp.float16), pair1)
    pair2 = raised(pair1, 1)
    projected = projected + swapped(projected, "head", 2)
    projected = projected + swapped(projected, "head", 4)
    projected, cores1, packs[2] = tie(projected, cores1, packs[2])
    packs.append(swapped(packs[2], "ctx", 1))
    other = swapped(projected, "head", 1)
    state = add([(1, 1, 0, 0), (1, 3, 0, 1)], kvs=[cores1], state=state)
    other, pair2, *state = tie(other, pair2, *state)
    cores2 = swapped(pair2, "ctx", 1)
    projected = (projected.astype(F32) + other.astype(F32)) * 4.0

    inner = small_call(
        inner_kernel,
        jax.ShapeDtypeStruct((GROUP, WIDE), F32),
        [me, projected, *packs],
        [SMEM, VMEM] + [HBM] * 4,
        scratch_shapes=[
            pltpu.VMEM((PLANE, WIDE + TRACES * STEPS, 256), BF16),
            pltpu.SemaphoreType.DMA((PLANE,)),
        ],
        name="inner",
    )
    inner, pair2, *state = tie(inner, pair2, *state)
    inner = (inner * 2.0**-10).astype(jnp.float16).reshape(Z, PAD, WIDE)
    state = add([(2, 0, 0, 0), (2, 2, 0, 1)], kvs=[pair2], state=state)
    inner = lax.all_to_all(inner, "ctx", 0, 0, axis_index_groups=columns)
    inner, *state = tie(inner, *state)
    inner = jnp.sum(inner.astype(F32), axis=0) * 2.0**10
    heads, count = lax.axis_size("head"), lax.axis_size("ctx")
    gap = small_call(
        hidden_kernel,
        jax.ShapeDtypeStruct((heads, 1, HD), F32),
        [inner, class_weight],
        name="hidden",
    )
    gap, cores2, *state = tie(gap, cores2, *state)
    attended = add([(2, 1, 0, 0), (2, 3, 0, 1)], kvs=[cores2], state=state, last=True)
    gap = lax.all_to_all(gap, "head", 0, 0)
    gap, attended = tie(gap, attended)
    gap = jnp.sum(gap, axis=0)
    gap = lax.all_to_all(jnp.broadcast_to(gap[None], (count, 1, HD)), "ctx", 0, 0)
    step_scores, votes = small_call(
        vote_kernel,
        (
            jax.ShapeDtypeStruct((TRACES, STEPS), F32),
            jax.ShapeDtypeStruct((PROMPTS, CLUSTERS), F32),
        ),
        [prompt_ids, cluster_ids, gap],
        [SMEM, SMEM, VMEM],
        name="vote",
    )
    return (attended, step_scores, votes)


def solution(mesh):
    placed = (
        P("ctx", "head"),
        P(None, "ctx", "head"),
        P(),
        P(),
        P(),
        P(),
        P(None, "ctx"),
        P("head", "ctx"),
        P("ctx", "head"),
        P("head", None),
    )
    return jax.shard_map(
        per_device,
        mesh=mesh,
        in_specs=placed,
        out_specs=(P("ctx", "head"), P(), P()),
        check_vma=False,
    )
```

```python
import functools
import math

import jax
import jax.numpy as jnp
from jax import lax
from jax.experimental import pallas as pl
from jax.experimental.pallas import tpu as pltpu
from jax.sharding import PartitionSpec as P

HD = 128
PROMPTS = 2
CLUSTERS = 4
TRACES = 7
STEPS = 32
PER_GROUP = 4
BLOCK = 512
TILE = 512
OWN_TILE = 256
Z = 8
PLANE = 4
PAD = 8
GROUP = Z * PAD
WIDE = 1024
COEF = HD**-0.5 * math.log2(math.e)
LOW = -1e30
NONE = -60000.0
VMEM = pl.BlockSpec(memory_space=pltpu.VMEM)
SMEM = pl.BlockSpec(memory_space=pltpu.SMEM)
HBM = pl.BlockSpec(memory_space=pltpu.HBM)
BF16 = jnp.bfloat16
F32 = jnp.float32


def first_key(row, lengths):
    start = row * 0
    end = jnp.int32(0)
    for t in range(TRACES):
        end = end + lengths[t]
        start = jnp.where(row >= end, end, start)
    return start


def pick_kernel(me_ref, steps_hbm, q_hbm, weight_hbm, stream_hbm, *refs):
    keep_ref, pass_ref, send_ref, pack_hbm, all_ref, steps_ref, q_ref, sems = refs
    copies = [pltpu.make_async_copy(steps_hbm, steps_ref, sems.at[0])]
    for k in range(4):
        part = pl.ds(k * BLOCK // 4, BLOCK // 4)
        copies.append(pltpu.make_async_copy(q_hbm.at[part], q_ref.at[part], sems.at[1 + k]))
    for k, (source, begin) in enumerate([(weight_hbm, 0), (stream_hbm, BLOCK)]):
        target = pack_hbm.at[pl.ds(begin, source.shape[0])]
        copies.append(pltpu.make_async_copy(source, target, sems.at[5 + k]))
    for copy in copies:
        copy.start()
    for copy in copies[:5]:
        copy.wait()
    me = me_ref[0]
    core, side = me % 2, (me // 2) % 2
    at = lax.broadcasted_iota(jnp.int32, (TRACES, BLOCK), 1) + me * BLOCK
    none = jnp.zeros((PAD - TRACES, BLOCK), F32)
    steps = steps_ref[...]
    for c in range(2):
        for y in range(2):
            parts = []
            for z in range(Z):
                step = PLANE * z + 2 * y + c
                parts.append(jnp.where(steps[:, step : step + 1] == at, 1.0, 0.0))
                parts.append(none)
            chosen = jnp.concatenate(parts, axis=0).astype(BF16)
            got = jnp.dot(chosen, q_ref[...], preferred_element_type=F32)
            all_ref[pl.ds((2 * c + y) * GROUP, GROUP), :] = got.astype(BF16)

    def group(c, y):
        return all_ref[pl.ds(pl.multiple_of((2 * c + y) * GROUP, GROUP), GROUP), :]

    keep_ref[...] = group(core, side)
    pass_ref[...] = group(core, 1 - side)
    send_ref[:GROUP] = group(1 - core, side)
    send_ref[GROUP:] = group(1 - core, 1 - side)
    for copy in copies[5:]:
        copy.wait()


def picked_kernel(me_ref, lengths_hbm, steps_hbm, q_ref, q1_ref, q2_ref, *refs):
    kv_refs, out_ref = refs[:PLANE], refs[PLANE]
    plane_ref, lengths, steps_ref, sems = refs[-4:]
    kv_s = plane_ref
    lengths_copy = pltpu.make_async_copy(lengths_hbm, lengths, sems.at[PLANE])
    steps_copy = pltpu.make_async_copy(steps_hbm, steps_ref, sems.at[PLANE + 1])
    copies = [
        pltpu.make_async_copy(kv, kv_s.at[pl.ds(2 * k, 2)], sems.at[k])
        for k, kv in enumerate(kv_refs)
    ]
    for copy in [lengths_copy, steps_copy] + copies:
        copy.start()
    lengths_copy.wait()
    steps_copy.wait()
    me = me_ref[0]
    place = me % PLANE
    steps = steps_ref[...]
    lane = lax.broadcasted_iota(jnp.int32, (TRACES, STEPS), 1)
    none = jnp.full((PAD - TRACES, HD), -1, jnp.int32)
    parts = []
    for z in range(Z):
        mine = jnp.where(lane == PLANE * z + place, steps, 0)
        mine = jnp.sum(mine, axis=1, keepdims=True)
        parts.append(jnp.broadcast_to(mine, (TRACES, HD)))
        parts.append(none)
    row = jnp.concatenate(parts, axis=0)
    start = first_key(row, lengths)
    row = jnp.concatenate([row] * (BLOCK // HD), axis=1)
    start = jnp.concatenate([start] * (BLOCK // HD), axis=1)
    k_pos = lax.broadcasted_iota(jnp.int32, (GROUP, BLOCK), 1)
    q = (q_ref[...].astype(F32) + q1_ref[...].astype(F32) + q2_ref[...].astype(F32)).astype(BF16)
    q = jnp.concatenate([q[:, h * HD : (h + 1) * HD] for h in range(PER_GROUP)], axis=0)
    scores = []
    for k in range(PLANE):
        key0 = (me - place + (place ^ k)) * BLOCK
        mask = (k_pos <= row - key0) & (k_pos >= start - key0)
        mask = jnp.concatenate([mask] * PER_GROUP, axis=0)
        copies[k].wait()
        s = lax.dot_general(
            q, kv_s[2 * k], (((1,), (1,)), ((), ())), preferred_element_type=F32
        )
        scores.append(jnp.where(mask, s, LOW))
    top = jnp.maximum(jnp.maximum(scores[0], scores[1]), jnp.maximum(scores[2], scores[3]))
    top = jnp.maximum(jnp.max(top, axis=1, keepdims=True), 0.1 * LOW)
    ones = jnp.ones((BLOCK, HD), BF16)
    pv = jnp.zeros((PER_GROUP * GROUP, 2 * HD), F32)
    for k, s in enumerate(scores):
        p = jnp.exp2((s - top) * COEF).astype(BF16)
        ext = jnp.concatenate([kv_s[2 * k + 1], ones], axis=1)
        pv = pv + jnp.dot(p, ext, preferred_element_type=F32)
    total = pv[:, HD:]
    some = total > 0.0
    total = jnp.where(some, total, 1.0)
    value = pv[:, :HD] / total
    size = jnp.where(some, top * COEF + jnp.log2(total), NONE)
    lanes = lax.broadcasted_iota(jnp.int32, (GROUP, HD), 1)
    stats = jnp.zeros((GROUP, HD), F32)
    for h in range(PER_GROUP):
        rows = slice(h * GROUP, (h + 1) * GROUP)
        out_ref[:, h * HD : (h + 1) * HD] = value[rows]
        rest = size[rows]
        for k in range(3):
            coarse = rest.astype(BF16).astype(F32)
            stats = jnp.where(lanes == PER_GROUP * k + h, coarse, stats)
            rest = rest - coarse
    for z in range(Z):
        packed = jnp.zeros((1, HD), F32)
        for t in range(TRACES):
            at = z * PAD + t
            packed = packed + pltpu.roll(stats[at : at + 1], 16 * t, 1)
        out_ref[z * PAD + TRACES : (z + 1) * PAD, :HD] = packed


def attend_kernel(slots, first, last, joined, *refs):
    n = len(slots)
    arrays = 1 + max(slot[2] for slot in slots)
    me_ref, lengths_hbm, q_ref = refs[:3]
    kv_hbm = [refs[3 + array].at[pl.ds(2 * at, 2)] for _, _, array, at in slots]
    kv_ref, lengths, sems = refs[-3:]
    if first:
        q_hbm = q_ref
        q_ref, m_ref, l_ref, acc_ref = refs[3 + arrays : 7 + arrays]
    else:
        m_ref, l_ref, acc_ref = refs[3 + arrays : 6 + arrays]
    pair_copies = []
    for k in range(joined):
        source = refs[3 + arrays - joined + k]
        target = refs[-4].at[pl.ds(2 * k, 2)]
        pair_copies.append(pltpu.make_async_copy(source, target, sems.at[n + 2 + k]))
    copies = [
        pltpu.make_async_copy(kv, kv_ref.at[k], sems.at[k]) for k, kv in enumerate(kv_hbm)
    ]
    copies.append(pltpu.make_async_copy(lengths_hbm, lengths, sems.at[n]))
    if first:
        copies.append(pltpu.make_async_copy(q_hbm, q_ref, sems.at[n + 1]))
    for copy in copies + pair_copies:
        copy.start()
    for copy in copies:
        copy.wait()
    me = me_ref[0]
    place = me % PLANE
    row0 = me * BLOCK
    ones = jnp.ones((BLOCK, HD), BF16)
    blocks = [me - place - back * PLANE + (place ^ flip) for back, flip, _, _ in slots]

    def weigh(rows, count, keys, ext, mask, fresh):
        q = q_ref[rows, :]
        q = jnp.concatenate([q[:, h * HD : (h + 1) * HD] for h in range(PER_GROUP)], axis=0)
        s = lax.dot_general(q, keys, (((1,), (1,)), ((), ())), preferred_element_type=F32)
        for h in range(PER_GROUP):
            cols = slice(h * HD, (h + 1) * HD)
            mine = s[h * count : (h + 1) * count]
            if mask is not None:
                mine = jnp.where(mask, mine, LOW)
            top = jnp.max(mine, axis=1, keepdims=True)
            if fresh:
                top = jnp.broadcast_to(top, (count, HD))
            else:
                before = m_ref[rows, cols]
                top = jnp.maximum(before, top)
            wide = jnp.concatenate([top] * (mine.shape[1] // HD), axis=1)
            p = jnp.exp2((mine - wide) * COEF).astype(BF16)
            pv = jnp.dot(p, ext, preferred_element_type=F32)
            m_ref[rows, cols] = top
            if fresh:
                acc_ref[rows, cols] = pv[:, :HD]
                l_ref[rows, cols] = pv[:, HD:]
            else:
                scale = jnp.exp2((before - top) * COEF)
                acc_ref[rows, cols] = acc_ref[rows, cols] * scale + pv[:, :HD]
                l_ref[rows, cols] = l_ref[rows, cols] * scale + pv[:, HD:]

    def own_block():
        for tile in range(BLOCK // OWN_TILE):
            width = (tile + 1) * OWN_TILE
            rows = slice(tile * OWN_TILE, width)
            keys = kv_ref[0, 0, :width, :]
            ext = jnp.concatenate([kv_ref[0, 1, :width, :], ones[:width]], axis=1)
            shape = (OWN_TILE, width)
            q_pos = row0 + tile * OWN_TILE + lax.broadcasted_iota(jnp.int32, shape, 0)
            k_pos = row0 + lax.broadcasted_iota(jnp.int32, shape, 1)
            starts = first_key(q_pos[:, :HD], lengths)
            starts = jnp.concatenate([starts] * (width // HD), axis=1)
            mask = (k_pos <= q_pos) & (k_pos >= starts)
            weigh(rows, OWN_TILE, keys, ext, mask, True)

    def other_tile(index, carry):
        tile, k = index % (BLOCK // TILE), index // (BLOCK // TILE)
        block = blocks[-1]
        for other in range(n - 1):
            block = jnp.where(k == other, blocks[other], block)
        key0 = block * BLOCK
        begin = pl.multiple_of(tile * TILE, TILE)
        rows = pl.ds(begin, TILE)
        low = first_key(row0 + begin, lengths)
        high = first_key(row0 + begin + TILE - 1, lengths)
        some = (block < me) & (key0 + BLOCK > low)
        every = key0 >= high

        def run(masked):
            keys = kv_ref[k, 0]
            ext = jnp.concatenate([kv_ref[k, 1], ones], axis=1)
            mask = None
            if masked:
                starts = first_key(
                    row0 + begin + lax.broadcasted_iota(jnp.int32, (TILE, HD), 0), lengths
                )
                starts = jnp.concatenate([starts] * (BLOCK // HD), axis=1)
                k_pos = key0 + lax.broadcasted_iota(jnp.int32, (TILE, BLOCK), 1)
                mask = k_pos >= starts
            weigh(rows, TILE, keys, ext, mask, False)

        pl.when(some & every)(functools.partial(run, False))
        pl.when(some & jnp.logical_not(every))(functools.partial(run, True))
        return carry

    if first:
        own_block()
    tiles = BLOCK // TILE
    lax.fori_loop(tiles * int(first), tiles * n, other_tile, 0)
    if last:
        out_ref = refs[-4]
        out_ref[...] = acc_ref[...] / l_ref[...]
    for copy in pair_copies:
        copy.wait()


def attend(slots, me, lengths, queries, kvs, state, last=False, in_vmem=0, joined=0):
    shape = (BLOCK, PER_GROUP * HD)
    first = state is None
    kept = [pltpu.with_memory_space_constraint(kv, pltpu.VMEM) for kv in kvs[:in_vmem]]
    operands = [me, *pinned([lengths, queries] if first else [lengths]), *kept, *kvs[in_vmem:]]
    specs = [SMEM] + [HBM] * (len(operands) - 1)
    if not first:
        q, *sums = [pltpu.with_memory_space_constraint(x, pltpu.VMEM) for x in state]
        operands[2:2] = [q]
        specs[2:2] = [VMEM] + [VMEM] * in_vmem
        del specs[3 + in_vmem : 3 + 2 * in_vmem]
        at = len(operands)
        operands += sums
        specs += [VMEM] * 3
    shapes = (pltpu.VMEM(shape, BF16),) + (pltpu.VMEM(shape, F32),) * 3
    out_specs, aliases = [VMEM] * 4, {}
    if last:
        shapes, out_specs = (jax.ShapeDtypeStruct(shape, F32),), [VMEM]
    elif not first:
        aliases = {2: 0, at: 1, at + 1: 2, at + 2: 3}
    if joined:
        shapes += (pltpu.HBM((2 * joined, BLOCK, HD), BF16),)
        out_specs.append(HBM)
    work = PER_GROUP * BLOCK * BLOCK * len(slots)
    got = pl.pallas_call(
        functools.partial(attend_kernel, slots, first, last, joined),
        out_shape=shapes,
        in_specs=specs,
        out_specs=out_specs,
        scratch_shapes=[
            pltpu.VMEM((len(slots), 2, BLOCK, HD), BF16),
            pltpu.SMEM((TRACES,), jnp.int32),
            pltpu.SemaphoreType.DMA((len(slots) + 2 + joined,)),
        ],
        input_output_aliases=aliases,
        compiler_params=pltpu.CompilerParams(vmem_limit_bytes=32 << 20),
        cost_estimate=pl.CostEstimate(
            flops=4 * HD * work, bytes_accessed=1 << 20, transcendentals=work
        ),
        name="attend_%d_%d" % slots[0][:2],
    )(*operands)
    if last:
        return got[0]
    return (list(got[:4]), got[4]) if joined else list(got)


def pinned(values):
    return [pltpu.with_memory_space_constraint(value, pltpu.HBM) for value in values]


def small_call(kernel, shape, operands, specs=None, out_specs=None, **kw):
    return pl.pallas_call(
        kernel,
        out_shape=shape,
        in_specs=specs or [VMEM] * len(operands),
        out_specs=out_specs or ([VMEM] * len(shape) if type(shape) is tuple else VMEM),
        compiler_params=pltpu.CompilerParams(vmem_limit_bytes=24 << 20),
        **kw,
    )(*operands)


def project_kernel(got_ref, *refs):
    packs, out_ref, weight_s, sems = refs[:PLANE], refs[PLANE], refs[-2], refs[-1]
    copies = [
        pltpu.make_async_copy(pack.at[pl.ds(0, BLOCK)], weight_s.at[k], sems.at[k])
        for k, pack in enumerate(packs)
    ]
    for copy in copies:
        copy.start()
    sizes = []
    for z in range(Z):
        stats = []
        for step in range(Z):
            packed = got_ref[z, step * PAD + TRACES : (step + 1) * PAD, :HD]
            for t in range(PAD):
                stats.append(pltpu.roll(packed, (HD - 16 * t) % HD, 1))
        sizes.append(jnp.concatenate(stats, axis=0))
    sizes = [
        size
        + pltpu.roll(size, HD - PER_GROUP, 1)
        + pltpu.roll(size, HD - 2 * PER_GROUP, 1)
        for size in sizes
    ]
    top = functools.reduce(jnp.maximum, sizes)
    weights = [jnp.exp2(size - top) for size in sizes]
    total = functools.reduce(jnp.add, weights)
    weights = [weight / total for weight in weights]
    slot = lax.broadcasted_iota(jnp.int32, (GROUP, HD), 0)
    picked = []
    for h in range(PER_GROUP):
        joined = jnp.zeros((GROUP, HD), F32)
        for z in range(Z):
            joined = joined + got_ref[z, :, h * HD : (h + 1) * HD] * weights[z][:, h : h + 1]
        joined = jnp.where((slot & (PAD - 1)) < TRACES, joined, 0.0)
        picked.append(joined.astype(BF16))
    picked = jnp.concatenate(picked, axis=1)
    for k in range(PLANE):
        copies[k].wait()
        part = jnp.dot(picked, weight_s[k], preferred_element_type=F32)
        out_ref[:, k * 256 : (k + 1) * 256] = part


def inner_kernel(me_ref, total_ref, *refs):
    packs, weights, out_ref = refs[:PLANE], refs[PLANE : 2 * PLANE], refs[2 * PLANE]
    stream_s, weight_s, sems = refs[-3:]
    copies = []
    for k in range(PLANE):
        source = packs[k].at[pl.ds(BLOCK, TRACES * STEPS)]
        copies.append(pltpu.make_async_copy(source, stream_s.at[k], sems.at[2 * k]))
        copies.append(pltpu.make_async_copy(weights[k], weight_s.at[k], sems.at[2 * k + 1]))
    for copy in copies:
        copy.start()
    place = me_ref[0] % PLANE
    slot = lax.broadcasted_iota(jnp.int32, (GROUP, TRACES * STEPS), 0)
    at = lax.broadcasted_iota(jnp.int32, (GROUP, TRACES * STEPS), 1)
    trace = slot & (PAD - 1)
    wanted = trace * STEPS + PLANE * (slot >> 3) + place
    chosen = jnp.where((at == wanted) & (trace < TRACES), 1.0, 0.0).astype(BF16)
    for k in range(PLANE):
        copies[2 * k].wait()
        base = jnp.dot(chosen, stream_s[k], preferred_element_type=F32)
        stream = (base + total_ref[:, k * 256 : (k + 1) * 256]).astype(BF16)
        copies[2 * k + 1].wait()
        part = jnp.dot(stream, weight_s[k], preferred_element_type=F32)
        out_ref[...] = part if k == 0 else out_ref[...] + part


def hidden_kernel(inner_ref, class_ref, out_ref):
    hidden = jnp.maximum(inner_ref[...], 0.0).astype(BF16)
    logits = jnp.dot(hidden, class_ref[...], preferred_element_type=F32)
    gap = logits[:, 1:2] - logits[:, 0:1]
    lane = lax.broadcasted_iota(jnp.int32, (PAD, HD), 1)
    row = lax.broadcasted_iota(jnp.int32, (PAD, HD), 0)
    mine = jnp.sum(jnp.where(lane == row, gap, 0.0), axis=0, keepdims=True)
    for k in range(out_ref.shape[0]):
        out_ref[k] = mine


def vote_kernel(prompts, clusters, got_ref, scores_ref, votes_ref):
    gap = jnp.concatenate([got_ref[k] for k in range(STEPS)], axis=0)
    scores = 1.0 / (1.0 + jnp.exp(-gap.T[:PAD]))
    scores_ref[...] = scores[:TRACES]
    chain = jnp.min(scores, axis=1, keepdims=True)
    prompt = lax.broadcasted_iota(jnp.int32, (PROMPTS, CLUSTERS), 0)
    cluster = lax.broadcasted_iota(jnp.int32, (PROMPTS, CLUSTERS), 1)
    votes = jnp.zeros((PROMPTS, CLUSTERS), F32)
    for t in range(TRACES):
        here = (prompt == prompts[t]) & (cluster == clusters[t])
        votes = votes + jnp.where(here, chain[t : t + 1, :], 0.0)
    votes_ref[...] = votes


def swapped(value, axis, bit):
    count = lax.axis_size(axis)
    return lax.ppermute(value, axis, [(s, s ^ bit) for s in range(count)])


def raised(value, planes):
    count = lax.axis_size("ctx")
    steps = planes * PLANE
    return lax.ppermute(value, "ctx", [(s, (s + steps) % count) for s in range(count)])


def per_device(
    queries,
    keys_values,
    trace_lengths,
    step_rows,
    prompt_ids,
    cluster_ids,
    step_stream,
    out_weight,
    score_weight,
    class_weight,
):
    me = lax.axis_index("ctx").astype(jnp.int32).reshape(1)
    columns = [[PLANE * z + j for z in range(Z)] for j in range(PLANE)]
    tie = lambda *values: lax.optimization_barrier(values)
    add = functools.partial(attend, me=me, lengths=trace_lengths, queries=queries)

    kv0 = keys_values
    core0 = swapped(kv0, "ctx", 1)

    half = PER_GROUP * HD
    packed = (BLOCK + TRACES * STEPS, 256)
    keep, passed, sent, weight = small_call(
        pick_kernel,
        tuple(jax.ShapeDtypeStruct((n * GROUP, half), BF16) for n in (1, 1, 2))
        + (pltpu.HBM(packed, BF16),),
        [me, *pinned([step_rows, queries, out_weight, step_stream])],
        [SMEM] + [HBM] * 4,
        [VMEM] * 3 + [HBM],
        scratch_shapes=[
            pltpu.VMEM((PLANE * GROUP, half), BF16),
            pltpu.VMEM((TRACES, STEPS), jnp.int32),
            pltpu.VMEM((BLOCK, half), BF16),
            pltpu.SemaphoreType.DMA((7,)),
        ],
        name="pick",
    )
    arrived = swapped(sent, "ctx", 1)
    across = swapped(passed + arrived[GROUP:], "ctx", 2)
    wanted = keep + arrived[:GROUP] + across
    wanted, kv0y, core0 = tie(wanted, kv0, core0)
    wanted1, wanted2 = raised(wanted, -1), raised(wanted, -2)
    across0 = swapped(kv0y, "ctx", 2)
    across0, wanted1, wanted2 = tie(across0, wanted1, wanted2)
    core0y = swapped(across0, "ctx", 1)
    state = add([(0, 0, 0, 0), (0, 1, 1, 0)], kvs=[pinned([kv0y])[0], core0], state=None)
    wanted, wanted1, wanted2, *state = tie(wanted, wanted1, wanted2, *state)

    weight, wanted = tie(weight, wanted)
    firsts = [weight, swapped(weight, "ctx", 1), swapped(weight, "ctx", 2)]
    kv1, _ = tie(raised(kv0, 1), wanted)

    parts, plane = small_call(
        picked_kernel,
        (jax.ShapeDtypeStruct((GROUP, half), F32), pltpu.VMEM((2 * PLANE, BLOCK, HD), BF16)),
        [
            me,
            *pinned([trace_lengths, step_rows]),
            wanted,
            wanted1,
            wanted2,
            *pinned([kv0]),
            core0,
            across0,
            core0y,
        ],
        [SMEM, HBM, HBM] + [VMEM] * 3 + [HBM] * 4,
        scratch_shapes=[
            pltpu.SMEM((TRACES,), jnp.int32),
            pltpu.VMEM((TRACES, STEPS), jnp.int32),
            pltpu.SemaphoreType.DMA((PLANE + 2,)),
        ],
        name="picked",
    )
    parts, kv1, plane, *state = tie(parts, kv1, plane, *state)
    across1 = swapped(kv1, "ctx", 2)
    parts = jnp.broadcast_to(parts.astype(jnp.float16)[None], (Z, GROUP, half))
    parts = lax.all_to_all(parts, "ctx", 0, 0, axis_index_groups=columns).astype(F32)
    firsts[2], across1 = tie(firsts[2], across1)
    firsts.append(swapped(firsts[2], "ctx", 1))
    state, pair1 = add(
        [(0, 2, 0, 2), (0, 3, 0, 3), (1, 0, 1, 0), (1, 2, 2, 0)],
        kvs=[plane, kv1, across1],
        state=state,
        in_vmem=1,
        joined=2,
    )
    cores1 = swapped(pair1, "ctx", 1)
    parts, pair1, weight, *state = tie(parts, pair1, score_weight, *state)
    weights = [weight, swapped(weight, "ctx", 1), swapped(weight, "ctx", 2)]

    projected = small_call(
        project_kernel,
        jax.ShapeDtypeStruct((GROUP, WIDE), F32),
        [parts, *firsts],
        [VMEM] + [HBM] * 4,
        scratch_shapes=[
            pltpu.VMEM((PLANE, BLOCK, 256), BF16),
            pltpu.SemaphoreType.DMA((PLANE,)),
        ],
        name="project",
    )
    projected, pair1 = tie((projected * 0.25).astype(jnp.float16), pair1)
    pair2 = raised(pair1, 1)
    projected = projected + swapped(projected, "head", 2)
    projected = projected + swapped(projected, "head", 4)
    projected, cores1, weights[2] = tie(projected, cores1, weights[2])
    weights.append(swapped(weights[2], "ctx", 1))
    other = swapped(projected, "head", 1)
    state = add([(1, 1, 0, 0), (1, 3, 0, 1)], kvs=[cores1], state=state)
    other, pair2, *state = tie(other, pair2, *state)
    cores2 = swapped(pair2, "ctx", 1)
    projected = (projected.astype(F32) + other.astype(F32)) * 4.0

    inner = small_call(
        inner_kernel,
        jax.ShapeDtypeStruct((GROUP, WIDE), F32),
        [me, projected, *firsts, *weights],
        [SMEM, VMEM] + [HBM] * 8,
        scratch_shapes=[
            pltpu.VMEM((PLANE, TRACES * STEPS, 256), BF16),
            pltpu.VMEM((PLANE, 256, WIDE), BF16),
            pltpu.SemaphoreType.DMA((2 * PLANE,)),
        ],
        name="inner",
    )
    inner, pair2, *state = tie(inner, pair2, *state)
    inner = (inner * 2.0**-10).astype(jnp.float16).reshape(Z, PAD, WIDE)
    state = add([(2, 0, 0, 0), (2, 2, 0, 1)], kvs=[pair2], state=state)
    inner = lax.all_to_all(inner, "ctx", 0, 0, axis_index_groups=columns)
    inner, *state = tie(inner, *state)
    inner = jnp.sum(inner.astype(F32), axis=0) * 2.0**10
    heads, count = lax.axis_size("head"), lax.axis_size("ctx")
    gap = small_call(
        hidden_kernel,
        jax.ShapeDtypeStruct((heads, 1, HD), F32),
        [inner, class_weight],
        name="hidden",
    )
    gap, cores2, *state = tie(gap, cores2, *state)
    attended = add([(2, 1, 0, 0), (2, 3, 0, 1)], kvs=[cores2], state=state, last=True)
    gap = lax.all_to_all(gap, "head", 0, 0)
    gap, attended = tie(gap, attended)
    gap = jnp.sum(gap, axis=0)
    gap = lax.all_to_all(jnp.broadcast_to(gap[None], (count, 1, HD)), "ctx", 0, 0)
    step_scores, votes = small_call(
        vote_kernel,
        (
            jax.ShapeDtypeStruct((TRACES, STEPS), F32),
            jax.ShapeDtypeStruct((PROMPTS, CLUSTERS), F32),
        ),
        [prompt_ids, cluster_ids, gap],
        [SMEM, SMEM, VMEM],
        name="vote",
    )
    return (attended, step_scores, votes)


def solution(mesh):
    placed = (
        P("ctx", "head"),
        P(None, "ctx", "head"),
        P(),
        P(),
        P(),
        P(),
        P(None, "ctx"),
        P("head", "ctx"),
        P("ctx", "head"),
        P("head", None),
    )
    return jax.shard_map(
        per_device,
        mesh=mesh,
        in_specs=placed,
        out_specs=(P("ctx", "head"), P(), P()),
        check_vma=False,
    )
```

```python
import functools
import math

import jax
import jax.numpy as jnp
from jax import lax
from jax.experimental import pallas as pl
from jax.experimental.pallas import tpu as pltpu
from jax.sharding import PartitionSpec as P

HD = 128
PROMPTS = 2
CLUSTERS = 4
TRACES = 7
STEPS = 32
PER_GROUP = 4
BLOCK = 512
TILE = 512
OWN_TILE = 256
Z = 8
PLANE = 4
PAD = 8
GROUP = Z * PAD
WIDE = 1024
COEF = HD**-0.5 * math.log2(math.e)
LOW = -1e30
NONE = -60000.0
VMEM = pl.BlockSpec(memory_space=pltpu.VMEM)
SMEM = pl.BlockSpec(memory_space=pltpu.SMEM)
HBM = pl.BlockSpec(memory_space=pltpu.HBM)
BF16 = jnp.bfloat16
F32 = jnp.float32


def first_key(row, lengths):
    start = row * 0
    end = jnp.int32(0)
    for t in range(TRACES):
        end = end + lengths[t]
        start = jnp.where(row >= end, end, start)
    return start


def pick_kernel(me_ref, steps_hbm, q_hbm, weight_hbm, stream_hbm, *refs):
    keep_ref, pass_ref, send_ref, pack_ref, all_ref, steps_ref, q_ref, sems = refs
    copies = [pltpu.make_async_copy(steps_hbm, steps_ref, sems.at[0])]
    for k in range(4):
        part = pl.ds(k * BLOCK // 4, BLOCK // 4)
        copies.append(pltpu.make_async_copy(q_hbm.at[part], q_ref.at[part], sems.at[1 + k]))
    for k, (source, begin) in enumerate([(weight_hbm, 0), (stream_hbm, BLOCK)]):
        target = pack_ref.at[pl.ds(begin, source.shape[0])]
        copies.append(pltpu.make_async_copy(source, target, sems.at[5 + k]))
    for copy in copies:
        copy.start()
    for copy in copies[:5]:
        copy.wait()
    me = me_ref[0]
    core, side = me % 2, (me // 2) % 2
    at = lax.broadcasted_iota(jnp.int32, (TRACES, BLOCK), 1) + me * BLOCK
    none = jnp.zeros((PAD - TRACES, BLOCK), F32)
    steps = steps_ref[...]
    for c in range(2):
        for y in range(2):
            parts = []
            for z in range(Z):
                step = PLANE * z + 2 * y + c
                parts.append(jnp.where(steps[:, step : step + 1] == at, 1.0, 0.0))
                parts.append(none)
            chosen = jnp.concatenate(parts, axis=0).astype(BF16)
            got = jnp.dot(chosen, q_ref[...], preferred_element_type=F32)
            all_ref[pl.ds((2 * c + y) * GROUP, GROUP), :] = got.astype(BF16)

    def group(c, y):
        return all_ref[pl.ds(pl.multiple_of((2 * c + y) * GROUP, GROUP), GROUP), :]

    keep_ref[...] = group(core, side)
    pass_ref[...] = group(core, 1 - side)
    send_ref[:GROUP] = group(1 - core, side)
    send_ref[GROUP:] = group(1 - core, 1 - side)
    for copy in copies[5:]:
        copy.wait()


def picked_kernel(me_ref, lengths_hbm, steps_hbm, q_ref, q1_ref, q2_ref, *refs):
    kv_refs, out_ref, moved_hbm = refs[:PLANE], refs[PLANE], refs[PLANE + 1]
    kv_s, lengths, steps_ref, sems = refs[-4:]
    lengths_copy = pltpu.make_async_copy(lengths_hbm, lengths, sems.at[PLANE])
    steps_copy = pltpu.make_async_copy(steps_hbm, steps_ref, sems.at[PLANE + 1])
    copies = [
        pltpu.make_async_copy(kv, kv_s.at[pl.ds(2 * k, 2)], sems.at[k])
        for k, kv in enumerate(kv_refs)
    ]
    half = pl.ds(PLANE, PLANE)
    moved_copy = pltpu.make_async_copy(kv_s.at[half], moved_hbm, sems.at[PLANE + 2])
    for copy in [lengths_copy, steps_copy] + copies:
        copy.start()
    lengths_copy.wait()
    steps_copy.wait()
    me = me_ref[0]
    place = me % PLANE
    steps = steps_ref[...]
    lane = lax.broadcasted_iota(jnp.int32, (TRACES, STEPS), 1)
    none = jnp.full((PAD - TRACES, HD), -1, jnp.int32)
    parts = []
    for z in range(Z):
        mine = jnp.where(lane == PLANE * z + place, steps, 0)
        mine = jnp.sum(mine, axis=1, keepdims=True)
        parts.append(jnp.broadcast_to(mine, (TRACES, HD)))
        parts.append(none)
    row = jnp.concatenate(parts, axis=0)
    start = first_key(row, lengths)
    row = jnp.concatenate([row] * (BLOCK // HD), axis=1)
    start = jnp.concatenate([start] * (BLOCK // HD), axis=1)
    k_pos = lax.broadcasted_iota(jnp.int32, (GROUP, BLOCK), 1)
    q = (q_ref[...].astype(F32) + q1_ref[...].astype(F32) + q2_ref[...].astype(F32)).astype(BF16)
    q = jnp.concatenate([q[:, h * HD : (h + 1) * HD] for h in range(PER_GROUP)], axis=0)
    scores = []
    for k in range(PLANE):
        key0 = (me - place + (place ^ k)) * BLOCK
        mask = (k_pos <= row - key0) & (k_pos >= start - key0)
        mask = jnp.concatenate([mask] * PER_GROUP, axis=0)
        copies[k].wait()
        s = lax.dot_general(
            q, kv_s[2 * k], (((1,), (1,)), ((), ())), preferred_element_type=F32
        )
        scores.append(jnp.where(mask, s, LOW))
    moved_copy.start()
    top = jnp.maximum(jnp.maximum(scores[0], scores[1]), jnp.maximum(scores[2], scores[3]))
    top = jnp.maximum(jnp.max(top, axis=1, keepdims=True), 0.1 * LOW)
    ones = jnp.ones((BLOCK, HD), BF16)
    pv = jnp.zeros((PER_GROUP * GROUP, 2 * HD), F32)
    for k, s in enumerate(scores):
        p = jnp.exp2((s - top) * COEF).astype(BF16)
        ext = jnp.concatenate([kv_s[2 * k + 1], ones], axis=1)
        pv = pv + jnp.dot(p, ext, preferred_element_type=F32)
    total = pv[:, HD:]
    some = total > 0.0
    total = jnp.where(some, total, 1.0)
    value = pv[:, :HD] / total
    size = jnp.where(some, top * COEF + jnp.log2(total), NONE)
    lanes = lax.broadcasted_iota(jnp.int32, (GROUP, HD), 1)
    stats = jnp.zeros((GROUP, HD), F32)
    for h in range(PER_GROUP):
        rows = slice(h * GROUP, (h + 1) * GROUP)
        out_ref[:, h * HD : (h + 1) * HD] = value[rows]
        rest = size[rows]
        for k in range(3):
            coarse = rest.astype(BF16).astype(F32)
            stats = jnp.where(lanes == PER_GROUP * k + h, coarse, stats)
            rest = rest - coarse
    for z in range(Z):
        packed = jnp.zeros((1, HD), F32)
        for t in range(TRACES):
            at = z * PAD + t
            packed = packed + pltpu.roll(stats[at : at + 1], 16 * t, 1)
        out_ref[z * PAD + TRACES : (z + 1) * PAD, :HD] = packed
    moved_copy.wait()


def attend_kernel(slots, first, last, joined, *refs):
    n = len(slots)
    arrays = 1 + max(slot[2] for slot in slots)
    me_ref, lengths_hbm, q_hbm = refs[:3]
    kv_hbm = [refs[3 + array].at[pl.ds(2 * at, 2)] for _, _, array, at in slots]
    m_ref, l_ref, acc_ref = refs[3 + arrays : 6 + arrays]
    q_ref, kv_ref, lengths, sems = refs[-4:]
    copies = [
        pltpu.make_async_copy(kv, kv_ref.at[k], sems.at[k]) for k, kv in enumerate(kv_hbm)
    ]
    copies.append(pltpu.make_async_copy(lengths_hbm, lengths, sems.at[n]))
    for k in range(4):
        part = pl.ds(k * BLOCK // 4, BLOCK // 4)
        copies.append(
            pltpu.make_async_copy(q_hbm.at[part], q_ref.at[part], sems.at[n + 1 + k])
        )
    pair_copies = []
    for k in range(joined):
        target = refs[-5].at[pl.ds(2 * k, 2)]
        pair_copies.append(
            pltpu.make_async_copy(kv_ref.at[n - joined + k], target, sems.at[n + 5 + k])
        )
    for copy in copies:
        copy.start()
    for copy in copies:
        copy.wait()
    for copy in pair_copies:
        copy.start()
    me = me_ref[0]
    place = me % PLANE
    row0 = me * BLOCK
    ones = jnp.ones((BLOCK, HD), BF16)
    blocks = [me - place - back * PLANE + (place ^ flip) for back, flip, _, _ in slots]

    def weigh(rows, count, keys, ext, mask, fresh):
        q = q_ref[rows, :]
        q = jnp.concatenate([q[:, h * HD : (h + 1) * HD] for h in range(PER_GROUP)], axis=0)
        s = lax.dot_general(q, keys, (((1,), (1,)), ((), ())), preferred_element_type=F32)
        for h in range(PER_GROUP):
            cols = slice(h * HD, (h + 1) * HD)
            mine = s[h * count : (h + 1) * count]
            if mask is not None:
                mine = jnp.where(mask, mine, LOW)
            top = jnp.max(mine, axis=1, keepdims=True)
            if fresh:
                top = jnp.broadcast_to(top, (count, HD))
            else:
                before = m_ref[rows, cols]
                top = jnp.maximum(before, top)
            wide = jnp.concatenate([top] * (mine.shape[1] // HD), axis=1)
            p = jnp.exp2((mine - wide) * COEF).astype(BF16)
            pv = jnp.dot(p, ext, preferred_element_type=F32)
            m_ref[rows, cols] = top
            if fresh:
                acc_ref[rows, cols] = pv[:, :HD]
                l_ref[rows, cols] = pv[:, HD:]
            else:
                scale = jnp.exp2((before - top) * COEF)
                acc_ref[rows, cols] = acc_ref[rows, cols] * scale + pv[:, :HD]
                l_ref[rows, cols] = l_ref[rows, cols] * scale + pv[:, HD:]

    def own_block():
        for tile in range(BLOCK // OWN_TILE):
            width = (tile + 1) * OWN_TILE
            rows = slice(tile * OWN_TILE, width)
            keys = kv_ref[0, 0, :width, :]
            ext = jnp.concatenate([kv_ref[0, 1, :width, :], ones[:width]], axis=1)
            shape = (OWN_TILE, width)
            q_pos = row0 + tile * OWN_TILE + lax.broadcasted_iota(jnp.int32, shape, 0)
            k_pos = row0 + lax.broadcasted_iota(jnp.int32, shape, 1)
            starts = first_key(q_pos[:, :HD], lengths)
            starts = jnp.concatenate([starts] * (width // HD), axis=1)
            mask = (k_pos <= q_pos) & (k_pos >= starts)
            weigh(rows, OWN_TILE, keys, ext, mask, True)

    def other_tile(index, carry):
        tile, k = index % (BLOCK // TILE), index // (BLOCK // TILE)
        block = blocks[-1]
        for other in range(n - 1):
            block = jnp.where(k == other, blocks[other], block)
        key0 = block * BLOCK
        begin = pl.multiple_of(tile * TILE, TILE)
        rows = pl.ds(begin, TILE)
        low = first_key(row0 + begin, lengths)
        high = first_key(row0 + begin + TILE - 1, lengths)
        some = (block < me) & (key0 + BLOCK > low)
        every = key0 >= high

        def run(masked):
            keys = kv_ref[k, 0]
            ext = jnp.concatenate([kv_ref[k, 1], ones], axis=1)
            mask = None
            if masked:
                starts = first_key(
                    row0 + begin + lax.broadcasted_iota(jnp.int32, (TILE, HD), 0), lengths
                )
                starts = jnp.concatenate([starts] * (BLOCK // HD), axis=1)
                k_pos = key0 + lax.broadcasted_iota(jnp.int32, (TILE, BLOCK), 1)
                mask = k_pos >= starts
            weigh(rows, TILE, keys, ext, mask, False)

        pl.when(some & every)(functools.partial(run, False))
        pl.when(some & jnp.logical_not(every))(functools.partial(run, True))
        return carry

    if first:
        own_block()
    tiles = BLOCK // TILE
    lax.fori_loop(tiles * int(first), tiles * n, other_tile, 0)
    if last:
        out_ref = refs[-5]
        out_ref[...] = acc_ref[...] / l_ref[...]
    for copy in pair_copies:
        copy.wait()


def attend(slots, me, lengths, queries, kvs, state, last=False, joined=0):
    shape = (BLOCK, PER_GROUP * HD)
    first = state is None
    operands = [me, *pinned([lengths, queries]), *kvs]
    specs = [SMEM] + [HBM] * (len(operands) - 1)
    shapes, aliases = (pltpu.VMEM(shape, F32),) * 3, {}
    if not first:
        at = len(operands)
        operands += [pltpu.with_memory_space_constraint(x, pltpu.VMEM) for x in state]
        specs += [VMEM] * 3
        aliases = {at + k: k for k in range(3)}
    if last:
        shapes, aliases = (jax.ShapeDtypeStruct(shape, F32),), {}
    if joined:
        shapes += (pltpu.VMEM((2 * joined, BLOCK, HD), BF16),)
    work = PER_GROUP * BLOCK * BLOCK * len(slots)
    got = pl.pallas_call(
        functools.partial(attend_kernel, slots, first, last, joined),
        out_shape=shapes,
        in_specs=specs,
        out_specs=[VMEM] * len(shapes),
        scratch_shapes=[
            pltpu.VMEM(shape, BF16),
            pltpu.VMEM((len(slots), 2, BLOCK, HD), BF16),
            pltpu.SMEM((TRACES,), jnp.int32),
            pltpu.SemaphoreType.DMA((len(slots) + 5 + joined,)),
        ],
        input_output_aliases=aliases,
        compiler_params=pltpu.CompilerParams(vmem_limit_bytes=20 << 20),
        cost_estimate=pl.CostEstimate(
            flops=4 * HD * work, bytes_accessed=1 << 20, transcendentals=work
        ),
        name="attend_%d_%d" % slots[0][:2],
    )(*operands)
    if last:
        return got[0]
    return (list(got[:3]), got[3]) if joined else list(got)


def pinned(values):
    return [pltpu.with_memory_space_constraint(value, pltpu.HBM) for value in values]


def small_call(kernel, shape, operands, specs=None, out_specs=None, **kw):
    return pl.pallas_call(
        kernel,
        out_shape=shape,
        in_specs=specs or [VMEM] * len(operands),
        out_specs=out_specs or ([VMEM] * len(shape) if type(shape) is tuple else VMEM),
        compiler_params=pltpu.CompilerParams(vmem_limit_bytes=16 << 20),
        **kw,
    )(*operands)


def project_kernel(got_ref, *refs):
    packs, out_ref, weight_s, sems = refs[:PLANE], refs[PLANE], refs[-2], refs[-1]
    copies = [
        pltpu.make_async_copy(pack.at[pl.ds(0, BLOCK)], weight_s.at[k], sems.at[k])
        for k, pack in enumerate(packs)
    ]
    for copy in copies:
        copy.start()
    sizes = []
    for z in range(Z):
        stats = []
        for step in range(Z):
            packed = got_ref[z, step * PAD + TRACES : (step + 1) * PAD, :HD]
            for t in range(PAD):
                stats.append(pltpu.roll(packed, (HD - 16 * t) % HD, 1))
        sizes.append(jnp.concatenate(stats, axis=0))
    sizes = [
        size
        + pltpu.roll(size, HD - PER_GROUP, 1)
        + pltpu.roll(size, HD - 2 * PER_GROUP, 1)
        for size in sizes
    ]
    top = functools.reduce(jnp.maximum, sizes)
    weights = [jnp.exp2(size - top) for size in sizes]
    total = functools.reduce(jnp.add, weights)
    weights = [weight / total for weight in weights]
    slot = lax.broadcasted_iota(jnp.int32, (GROUP, HD), 0)
    picked = []
    for h in range(PER_GROUP):
        joined = jnp.zeros((GROUP, HD), F32)
        for z in range(Z):
            joined = joined + got_ref[z, :, h * HD : (h + 1) * HD] * weights[z][:, h : h + 1]
        joined = jnp.where((slot & (PAD - 1)) < TRACES, joined, 0.0)
        picked.append(joined.astype(BF16))
    picked = jnp.concatenate(picked, axis=1)
    for k in range(PLANE):
        copies[k].wait()
        part = jnp.dot(picked, weight_s[k], preferred_element_type=F32)
        out_ref[:, k * 256 : (k + 1) * 256] = part


def inner_kernel(me_ref, total_ref, *refs):
    packs, weights, out_ref = refs[:PLANE], refs[PLANE : 2 * PLANE], refs[2 * PLANE]
    stream_s, weight_s, sems = refs[-3:]
    copies = []
    for k in range(PLANE):
        source = packs[k].at[pl.ds(BLOCK, TRACES * STEPS)]
        copies.append(pltpu.make_async_copy(source, stream_s.at[k], sems.at[2 * k]))
        copies.append(pltpu.make_async_copy(weights[k], weight_s.at[k], sems.at[2 * k + 1]))
    for copy in copies:
        copy.start()
    place = me_ref[0] % PLANE
    slot = lax.broadcasted_iota(jnp.int32, (GROUP, TRACES * STEPS), 0)
    at = lax.broadcasted_iota(jnp.int32, (GROUP, TRACES * STEPS), 1)
    trace = slot & (PAD - 1)
    wanted = trace * STEPS + PLANE * (slot >> 3) + place
    chosen = jnp.where((at == wanted) & (trace < TRACES), 1.0, 0.0).astype(BF16)
    for k in range(PLANE):
        copies[2 * k].wait()
        base = jnp.dot(chosen, stream_s[k], preferred_element_type=F32)
        stream = (base + total_ref[:, k * 256 : (k + 1) * 256]).astype(BF16)
        copies[2 * k + 1].wait()
        part = jnp.dot(stream, weight_s[k], preferred_element_type=F32)
        out_ref[...] = part if k == 0 else out_ref[...] + part


def hidden_kernel(inner_ref, class_ref, out_ref):
    hidden = jnp.maximum(inner_ref[...], 0.0).astype(BF16)
    logits = jnp.dot(hidden, class_ref[...], preferred_element_type=F32)
    gap = logits[:, 1:2] - logits[:, 0:1]
    lane = lax.broadcasted_iota(jnp.int32, (PAD, HD), 1)
    row = lax.broadcasted_iota(jnp.int32, (PAD, HD), 0)
    mine = jnp.sum(jnp.where(lane == row, gap, 0.0), axis=0, keepdims=True)
    for k in range(out_ref.shape[0]):
        out_ref[k] = mine


def vote_kernel(prompts, clusters, got_ref, scores_ref, votes_ref):
    gap = jnp.concatenate([got_ref[k] for k in range(STEPS)], axis=0)
    scores = 1.0 / (1.0 + jnp.exp(-gap.T[:PAD]))
    scores_ref[...] = scores[:TRACES]
    chain = jnp.min(scores, axis=1, keepdims=True)
    prompt = lax.broadcasted_iota(jnp.int32, (PROMPTS, CLUSTERS), 0)
    cluster = lax.broadcasted_iota(jnp.int32, (PROMPTS, CLUSTERS), 1)
    votes = jnp.zeros((PROMPTS, CLUSTERS), F32)
    for t in range(TRACES):
        here = (prompt == prompts[t]) & (cluster == clusters[t])
        votes = votes + jnp.where(here, chain[t : t + 1, :], 0.0)
    votes_ref[...] = votes


def swapped(value, axis, bit):
    count = lax.axis_size(axis)
    return lax.ppermute(value, axis, [(s, s ^ bit) for s in range(count)])


def raised(value, planes):
    count = lax.axis_size("ctx")
    steps = planes * PLANE
    return lax.ppermute(value, "ctx", [(s, (s + steps) % count) for s in range(count)])


def per_device(
    queries,
    keys_values,
    trace_lengths,
    step_rows,
    prompt_ids,
    cluster_ids,
    step_stream,
    out_weight,
    score_weight,
    class_weight,
):
    me = lax.axis_index("ctx").astype(jnp.int32).reshape(1)
    columns = [[PLANE * z + j for z in range(Z)] for j in range(PLANE)]
    tie = lambda *values: lax.optimization_barrier(values)
    add = functools.partial(attend, me=me, lengths=trace_lengths, queries=queries)

    kv0 = keys_values
    core0 = swapped(kv0, "ctx", 1)

    half = PER_GROUP * HD
    packed = (BLOCK + TRACES * STEPS, 256)
    keep, passed, sent, weight = small_call(
        pick_kernel,
        tuple(jax.ShapeDtypeStruct((n * GROUP, half), BF16) for n in (1, 1, 2))
        + (pltpu.VMEM(packed, BF16),),
        [me, *pinned([step_rows, queries, out_weight, step_stream])],
        [SMEM] + [HBM] * 4,
        [VMEM] * 4,
        scratch_shapes=[
            pltpu.VMEM((PLANE * GROUP, half), BF16),
            pltpu.VMEM((TRACES, STEPS), jnp.int32),
            pltpu.VMEM((BLOCK, half), BF16),
            pltpu.SemaphoreType.DMA((7,)),
        ],
        name="pick",
    )
    arrived = swapped(sent, "ctx", 1)
    across = swapped(passed + arrived[GROUP:], "ctx", 2)
    wanted = keep + arrived[:GROUP] + across
    wanted, kv0y, core0 = tie(wanted, kv0, core0)
    wanted1, wanted2 = raised(wanted, -1), raised(wanted, -2)
    across0 = swapped(kv0y, "ctx", 2)
    across0, wanted1, wanted2 = tie(across0, wanted1, wanted2)
    core0y = swapped(across0, "ctx", 1)
    state = add([(0, 0, 0, 0), (0, 1, 1, 0)], kvs=[pinned([kv0y])[0], core0], state=None)
    wanted, wanted1, wanted2, *state = tie(wanted, wanted1, wanted2, *state)

    kv1, wanted = tie(raised(kv0, 1), wanted)
    across1 = swapped(kv1, "ctx", 2)

    parts, moved = small_call(
        picked_kernel,
        (jax.ShapeDtypeStruct((GROUP, half), F32), pltpu.HBM((PLANE, BLOCK, HD), BF16)),
        [
            me,
            *pinned([trace_lengths, step_rows]),
            wanted,
            wanted1,
            wanted2,
            *pinned([kv0]),
            core0,
            across0,
            core0y,
        ],
        [SMEM, HBM, HBM] + [VMEM] * 3 + [HBM] * 4,
        [VMEM, HBM],
        scratch_shapes=[
            pltpu.VMEM((2 * PLANE, BLOCK, HD), BF16),
            pltpu.SMEM((TRACES,), jnp.int32),
            pltpu.VMEM((TRACES, STEPS), jnp.int32),
            pltpu.SemaphoreType.DMA((PLANE + 3,)),
        ],
        name="picked",
    )
    parts, kv1, across1, weight, *state = tie(parts, kv1, across1, weight, *state)

    firsts = [weight] + [swapped(weight, "ctx", bits) for bits in (1, 2, 3)]

    parts = jnp.broadcast_to(parts.astype(jnp.float16)[None], (Z, GROUP, half))
    parts = lax.all_to_all(parts, "ctx", 0, 0, axis_index_groups=columns).astype(F32)
    state, pair1 = add(
        [(0, 2, 0, 0), (0, 3, 0, 1), (1, 0, 1, 0), (1, 2, 2, 0)],
        kvs=pinned([moved, kv1, across1]),
        state=state,
        joined=2,
    )
    parts, pair1, weight, *state = tie(parts, pair1, score_weight, *state)
    weights = [weight, swapped(weight, "ctx", 1), swapped(weight, "ctx", 2)]

    projected = small_call(
        project_kernel,
        jax.ShapeDtypeStruct((GROUP, WIDE), F32),
        [parts, *firsts],
        [VMEM] + [HBM] * 4,
        scratch_shapes=[
            pltpu.VMEM((PLANE, BLOCK, 256), BF16),
            pltpu.SemaphoreType.DMA((PLANE,)),
        ],
        name="project",
    )
    projected, pair1 = tie((projected * 0.25).astype(jnp.float16), pair1)
    pair2, cores1 = raised(pair1, 1), swapped(pair1, "ctx", 1)
    projected = projected + swapped(projected, "head", 2)
    projected = projected + swapped(projected, "head", 4)
    projected, cores1, weights[2] = tie(projected, cores1, weights[2])
    weights.append(swapped(weights[2], "ctx", 1))
    other = swapped(projected, "head", 1)
    state = add([(1, 1, 0, 0), (1, 3, 0, 1)], kvs=[cores1], state=state)
    other, pair2, *state = tie(other, pair2, *state)
    cores2 = swapped(pair2, "ctx", 1)
    projected = (projected.astype(F32) + other.astype(F32)) * 4.0

    inner = small_call(
        inner_kernel,
        jax.ShapeDtypeStruct((GROUP, WIDE), F32),
        [me, projected, *firsts, *weights],
        [SMEM, VMEM] + [HBM] * 8,
        scratch_shapes=[
            pltpu.VMEM((PLANE, TRACES * STEPS, 256), BF16),
            pltpu.VMEM((PLANE, 256, WIDE), BF16),
            pltpu.SemaphoreType.DMA((2 * PLANE,)),
        ],
        name="inner",
    )
    inner, pair2, *state = tie(inner, pair2, *state)
    inner = (inner * 2.0**-10).astype(jnp.float16).reshape(Z, PAD, WIDE)
    state = add([(2, 0, 0, 0), (2, 2, 0, 1)], kvs=pinned([pair2]), state=state)
    inner = lax.all_to_all(inner, "ctx", 0, 0, axis_index_groups=columns)
    inner, *state = tie(inner, *state)
    inner = jnp.sum(inner.astype(F32), axis=0) * 2.0**10
    heads, count = lax.axis_size("head"), lax.axis_size("ctx")
    gap = small_call(
        hidden_kernel,
        jax.ShapeDtypeStruct((heads, 1, HD), F32),
        [inner, class_weight],
        name="hidden",
    )
    gap, cores2, *state = tie(gap, cores2, *state)
    attended = add([(2, 1, 0, 0), (2, 3, 0, 1)], kvs=[cores2], state=state, last=True)
    gap = lax.all_to_all(gap, "head", 0, 0)
    gap, attended = tie(gap, attended)
    gap = jnp.sum(gap, axis=0)
    gap = lax.all_to_all(jnp.broadcast_to(gap[None], (count, 1, HD)), "ctx", 0, 0)
    step_scores, votes = small_call(
        vote_kernel,
        (
            jax.ShapeDtypeStruct((TRACES, STEPS), F32),
            jax.ShapeDtypeStruct((PROMPTS, CLUSTERS), F32),
        ),
        [prompt_ids, cluster_ids, gap],
        [SMEM, SMEM, VMEM],
        name="vote",
    )
    return (attended, step_scores, votes)


def solution(mesh):
    placed = (
        P("ctx", "head"),
        P(None, "ctx", "head"),
        P(),
        P(),
        P(),
        P(),
        P(None, "ctx"),
        P("head", "ctx"),
        P("ctx", "head"),
        P("head", None),
    )
    return jax.shard_map(
        per_device,
        mesh=mesh,
        in_specs=placed,
        out_specs=(P("ctx", "head"), P(), P()),
        check_vma=False,
    )
```

```python
import functools
import math

import jax
import jax.numpy as jnp
from jax import lax
from jax.experimental import pallas as pl
from jax.experimental.pallas import tpu as pltpu
from jax.sharding import PartitionSpec as P

HD = 128
PROMPTS = 2
CLUSTERS = 4
TRACES = 7
STEPS = 32
PER_GROUP = 4
BLOCK = 512
TILE = 512
OWN_TILE = 256
Z = 8
PLANE = 4
PAD = 8
GROUP = Z * PAD
WIDE = 1024
COEF = HD**-0.5 * math.log2(math.e)
LOW = -1e30
NONE = -60000.0
VMEM = pl.BlockSpec(memory_space=pltpu.VMEM)
SMEM = pl.BlockSpec(memory_space=pltpu.SMEM)
HBM = pl.BlockSpec(memory_space=pltpu.HBM)
BF16 = jnp.bfloat16
F32 = jnp.float32


def first_key(row, lengths):
    start = row * 0
    end = jnp.int32(0)
    for t in range(TRACES):
        end = end + lengths[t]
        start = jnp.where(row >= end, end, start)
    return start


def pick_kernel(me_ref, steps_hbm, q_hbm, weight_hbm, stream_hbm, *refs):
    keep_ref, pass_ref, send_ref, pack_ref, all_ref, steps_ref, q_ref, sems = refs
    copies = [pltpu.make_async_copy(steps_hbm, steps_ref, sems.at[0])]
    for k in range(4):
        part = pl.ds(k * BLOCK // 4, BLOCK // 4)
        copies.append(pltpu.make_async_copy(q_hbm.at[part], q_ref.at[part], sems.at[1 + k]))
    for k, (source, begin) in enumerate([(weight_hbm, 0), (stream_hbm, BLOCK)]):
        target = pack_ref.at[pl.ds(begin, source.shape[0])]
        copies.append(pltpu.make_async_copy(source, target, sems.at[5 + k]))
    for copy in copies:
        copy.start()
    for copy in copies[:5]:
        copy.wait()
    me = me_ref[0]
    core, side = me % 2, (me // 2) % 2
    at = lax.broadcasted_iota(jnp.int32, (TRACES, BLOCK), 1) + me * BLOCK
    none = jnp.zeros((PAD - TRACES, BLOCK), F32)
    steps = steps_ref[...]
    for c in range(2):
        for y in range(2):
            parts = []
            for z in range(Z):
                step = PLANE * z + 2 * y + c
                parts.append(jnp.where(steps[:, step : step + 1] == at, 1.0, 0.0))
                parts.append(none)
            chosen = jnp.concatenate(parts, axis=0).astype(BF16)
            got = jnp.dot(chosen, q_ref[...], preferred_element_type=F32)
            all_ref[pl.ds((2 * c + y) * GROUP, GROUP), :] = got.astype(BF16)

    def group(c, y):
        return all_ref[pl.ds(pl.multiple_of((2 * c + y) * GROUP, GROUP), GROUP), :]

    keep_ref[...] = group(core, side)
    pass_ref[...] = group(core, 1 - side)
    send_ref[:GROUP] = group(1 - core, side)
    send_ref[GROUP:] = group(1 - core, 1 - side)
    for copy in copies[5:]:
        copy.wait()


def picked_kernel(me_ref, lengths_hbm, steps_hbm, q_ref, q1_ref, q2_ref, *refs):
    kv_refs, out_ref, moved_hbm = refs[:PLANE], refs[PLANE], refs[PLANE + 1]
    kv_s, lengths, steps_ref, sems = refs[-4:]
    lengths_copy = pltpu.make_async_copy(lengths_hbm, lengths, sems.at[PLANE])
    steps_copy = pltpu.make_async_copy(steps_hbm, steps_ref, sems.at[PLANE + 1])
    copies = [
        pltpu.make_async_copy(kv, kv_s.at[pl.ds(2 * k, 2)], sems.at[k])
        for k, kv in enumerate(kv_refs)
    ]
    half = pl.ds(PLANE, PLANE)
    moved_copy = pltpu.make_async_copy(kv_s.at[half], moved_hbm, sems.at[PLANE + 2])
    for copy in [lengths_copy, steps_copy] + copies:
        copy.start()
    lengths_copy.wait()
    steps_copy.wait()
    me = me_ref[0]
    place = me % PLANE
    steps = steps_ref[...]
    lane = lax.broadcasted_iota(jnp.int32, (TRACES, STEPS), 1)
    none = jnp.full((PAD - TRACES, HD), -1, jnp.int32)
    parts = []
    for z in range(Z):
        mine = jnp.where(lane == PLANE * z + place, steps, 0)
        mine = jnp.sum(mine, axis=1, keepdims=True)
        parts.append(jnp.broadcast_to(mine, (TRACES, HD)))
        parts.append(none)
    row = jnp.concatenate(parts, axis=0)
    start = first_key(row, lengths)
    row = jnp.concatenate([row] * (BLOCK // HD), axis=1)
    start = jnp.concatenate([start] * (BLOCK // HD), axis=1)
    k_pos = lax.broadcasted_iota(jnp.int32, (GROUP, BLOCK), 1)
    q = (q_ref[...].astype(F32) + q1_ref[...].astype(F32) + q2_ref[...].astype(F32)).astype(BF16)
    q = jnp.concatenate([q[:, h * HD : (h + 1) * HD] for h in range(PER_GROUP)], axis=0)
    scores = []
    for k in range(PLANE):
        key0 = (me - place + (place ^ k)) * BLOCK
        mask = (k_pos <= row - key0) & (k_pos >= start - key0)
        mask = jnp.concatenate([mask] * PER_GROUP, axis=0)
        copies[k].wait()
        s = lax.dot_general(
            q, kv_s[2 * k], (((1,), (1,)), ((), ())), preferred_element_type=F32
        )
        scores.append(jnp.where(mask, s, LOW))
    moved_copy.start()
    top = jnp.maximum(jnp.maximum(scores[0], scores[1]), jnp.maximum(scores[2], scores[3]))
    top = jnp.maximum(jnp.max(top, axis=1, keepdims=True), 0.1 * LOW)
    ones = jnp.ones((BLOCK, HD), BF16)
    pv = jnp.zeros((PER_GROUP * GROUP, 2 * HD), F32)
    for k, s in enumerate(scores):
        p = jnp.exp2((s - top) * COEF).astype(BF16)
        ext = jnp.concatenate([kv_s[2 * k + 1], ones], axis=1)
        pv = pv + jnp.dot(p, ext, preferred_element_type=F32)
    total = pv[:, HD:]
    some = total > 0.0
    total = jnp.where(some, total, 1.0)
    value = pv[:, :HD] / total
    size = jnp.where(some, top * COEF + jnp.log2(total), NONE)
    lanes = lax.broadcasted_iota(jnp.int32, (GROUP, HD), 1)
    stats = jnp.zeros((GROUP, HD), F32)
    for h in range(PER_GROUP):
        rows = slice(h * GROUP, (h + 1) * GROUP)
        out_ref[:, h * HD : (h + 1) * HD] = value[rows]
        rest = size[rows]
        for k in range(3):
            coarse = rest.astype(BF16).astype(F32)
            stats = jnp.where(lanes == PER_GROUP * k + h, coarse, stats)
            rest = rest - coarse
    for z in range(Z):
        packed = jnp.zeros((1, HD), F32)
        for t in range(TRACES):
            at = z * PAD + t
            packed = packed + pltpu.roll(stats[at : at + 1], 16 * t, 1)
        out_ref[z * PAD + TRACES : (z + 1) * PAD, :HD] = packed
    moved_copy.wait()


def attend_kernel(slots, first, last, joined, *refs):
    n = len(slots)
    arrays = 1 + max(slot[2] for slot in slots)
    me_ref, lengths_hbm, q_hbm = refs[:3]
    kv_hbm = [refs[3 + array].at[pl.ds(2 * at, 2)] for _, _, array, at in slots]
    m_ref, l_ref, acc_ref = refs[3 + arrays : 6 + arrays]
    q_ref, kv_ref, lengths, sems = refs[-4:]
    copies = [
        pltpu.make_async_copy(kv, kv_ref.at[k], sems.at[k]) for k, kv in enumerate(kv_hbm)
    ]
    copies.append(pltpu.make_async_copy(lengths_hbm, lengths, sems.at[n]))
    for k in range(4):
        part = pl.ds(k * BLOCK // 4, BLOCK // 4)
        copies.append(
            pltpu.make_async_copy(q_hbm.at[part], q_ref.at[part], sems.at[n + 1 + k])
        )
    pair_copies = []
    for k in range(joined):
        target = refs[-5].at[pl.ds(2 * k, 2)]
        pair_copies.append(
            pltpu.make_async_copy(kv_ref.at[n - joined + k], target, sems.at[n + 5 + k])
        )
    for copy in copies:
        copy.start()
    for copy in copies:
        copy.wait()
    for copy in pair_copies:
        copy.start()
    me = me_ref[0]
    place = me % PLANE
    row0 = me * BLOCK
    ones = jnp.ones((BLOCK, HD), BF16)
    blocks = [me - place - back * PLANE + (place ^ flip) for back, flip, _, _ in slots]

    def weigh(rows, count, keys, ext, mask, fresh):
        q = q_ref[rows, :]
        q = jnp.concatenate([q[:, h * HD : (h + 1) * HD] for h in range(PER_GROUP)], axis=0)
        s = lax.dot_general(q, keys, (((1,), (1,)), ((), ())), preferred_element_type=F32)
        for h in range(PER_GROUP):
            cols = slice(h * HD, (h + 1) * HD)
            mine = s[h * count : (h + 1) * count]
            if mask is not None:
                mine = jnp.where(mask, mine, LOW)
            top = jnp.max(mine, axis=1, keepdims=True)
            if fresh:
                top = jnp.broadcast_to(top, (count, HD))
            else:
                before = m_ref[rows, cols]
                top = jnp.maximum(before, top)
            wide = jnp.concatenate([top] * (mine.shape[1] // HD), axis=1)
            p = jnp.exp2((mine - wide) * COEF).astype(BF16)
            pv = jnp.dot(p, ext, preferred_element_type=F32)
            m_ref[rows, cols] = top
            if fresh:
                acc_ref[rows, cols] = pv[:, :HD]
                l_ref[rows, cols] = pv[:, HD:]
            else:
                scale = jnp.exp2((before - top) * COEF)
                acc_ref[rows, cols] = acc_ref[rows, cols] * scale + pv[:, :HD]
                l_ref[rows, cols] = l_ref[rows, cols] * scale + pv[:, HD:]

    def own_block():
        for tile in range(BLOCK // OWN_TILE):
            width = (tile + 1) * OWN_TILE
            rows = slice(tile * OWN_TILE, width)
            keys = kv_ref[0, 0, :width, :]
            ext = jnp.concatenate([kv_ref[0, 1, :width, :], ones[:width]], axis=1)
            shape = (OWN_TILE, width)
            q_pos = row0 + tile * OWN_TILE + lax.broadcasted_iota(jnp.int32, shape, 0)
            k_pos = row0 + lax.broadcasted_iota(jnp.int32, shape, 1)
            starts = first_key(q_pos[:, :HD], lengths)
            starts = jnp.concatenate([starts] * (width // HD), axis=1)
            mask = (k_pos <= q_pos) & (k_pos >= starts)
            weigh(rows, OWN_TILE, keys, ext, mask, True)

    def other_tile(index, carry):
        tile, k = index % (BLOCK // TILE), index // (BLOCK // TILE)
        block = blocks[-1]
        for other in range(n - 1):
            block = jnp.where(k == other, blocks[other], block)
        key0 = block * BLOCK
        begin = pl.multiple_of(tile * TILE, TILE)
        rows = pl.ds(begin, TILE)
        low = first_key(row0 + begin, lengths)
        high = first_key(row0 + begin + TILE - 1, lengths)
        some = (block < me) & (key0 + BLOCK > low)
        every = key0 >= high

        def run(masked):
            keys = kv_ref[k, 0]
            ext = jnp.concatenate([kv_ref[k, 1], ones], axis=1)
            mask = None
            if masked:
                starts = first_key(
                    row0 + begin + lax.broadcasted_iota(jnp.int32, (TILE, HD), 0), lengths
                )
                starts = jnp.concatenate([starts] * (BLOCK // HD), axis=1)
                k_pos = key0 + lax.broadcasted_iota(jnp.int32, (TILE, BLOCK), 1)
                mask = k_pos >= starts
            weigh(rows, TILE, keys, ext, mask, False)

        pl.when(some & every)(functools.partial(run, False))
        pl.when(some & jnp.logical_not(every))(functools.partial(run, True))
        return carry

    if first:
        own_block()
    tiles = BLOCK // TILE
    lax.fori_loop(tiles * int(first), tiles * n, other_tile, 0)
    if last:
        out_ref = refs[-5]
        out_ref[...] = acc_ref[...] / l_ref[...]
    for copy in pair_copies:
        copy.wait()


def attend(slots, me, lengths, queries, kvs, state, last=False, joined=0):
    shape = (BLOCK, PER_GROUP * HD)
    first = state is None
    operands = [me, *pinned([lengths, queries]), *kvs]
    specs = [SMEM] + [HBM] * (len(operands) - 1)
    shapes, aliases = (pltpu.VMEM(shape, F32),) * 3, {}
    if not first:
        at = len(operands)
        operands += [pltpu.with_memory_space_constraint(x, pltpu.VMEM) for x in state]
        specs += [VMEM] * 3
        aliases = {at + k: k for k in range(3)}
    if last:
        shapes, aliases = (jax.ShapeDtypeStruct(shape, F32),), {}
    if joined:
        shapes += (pltpu.VMEM((2 * joined, BLOCK, HD), BF16),)
    work = PER_GROUP * BLOCK * BLOCK * len(slots)
    got = pl.pallas_call(
        functools.partial(attend_kernel, slots, first, last, joined),
        out_shape=shapes,
        in_specs=specs,
        out_specs=[VMEM] * len(shapes),
        scratch_shapes=[
            pltpu.VMEM(shape, BF16),
            pltpu.VMEM((len(slots), 2, BLOCK, HD), BF16),
            pltpu.SMEM((TRACES,), jnp.int32),
            pltpu.SemaphoreType.DMA((len(slots) + 5 + joined,)),
        ],
        input_output_aliases=aliases,
        compiler_params=pltpu.CompilerParams(vmem_limit_bytes=20 << 20),
        cost_estimate=pl.CostEstimate(
            flops=4 * HD * work, bytes_accessed=1 << 20, transcendentals=work
        ),
        name="attend_%d_%d" % slots[0][:2],
    )(*operands)
    if last:
        return got[0]
    return (list(got[:3]), got[3]) if joined else list(got)


def pinned(values):
    return [pltpu.with_memory_space_constraint(value, pltpu.HBM) for value in values]


def small_call(kernel, shape, operands, specs=None, out_specs=None, **kw):
    return pl.pallas_call(
        kernel,
        out_shape=shape,
        in_specs=specs or [VMEM] * len(operands),
        out_specs=out_specs or ([VMEM] * len(shape) if type(shape) is tuple else VMEM),
        compiler_params=pltpu.CompilerParams(vmem_limit_bytes=16 << 20),
        **kw,
    )(*operands)


def project_kernel(got_ref, *refs):
    packs, out_ref, weight_s, sems = refs[:PLANE], refs[PLANE], refs[-2], refs[-1]
    copies = [
        pltpu.make_async_copy(pack.at[pl.ds(0, BLOCK)], weight_s.at[k], sems.at[k])
        for k, pack in enumerate(packs)
    ]
    for copy in copies:
        copy.start()
    sizes = []
    for z in range(Z):
        stats = []
        for step in range(Z):
            packed = got_ref[z, step * PAD + TRACES : (step + 1) * PAD, :HD]
            for t in range(PAD):
                stats.append(pltpu.roll(packed, (HD - 16 * t) % HD, 1))
        sizes.append(jnp.concatenate(stats, axis=0))
    sizes = [
        size
        + pltpu.roll(size, HD - PER_GROUP, 1)
        + pltpu.roll(size, HD - 2 * PER_GROUP, 1)
        for size in sizes
    ]
    top = functools.reduce(jnp.maximum, sizes)
    weights = [jnp.exp2(size - top) for size in sizes]
    total = functools.reduce(jnp.add, weights)
    weights = [weight / total for weight in weights]
    slot = lax.broadcasted_iota(jnp.int32, (GROUP, HD), 0)
    picked = []
    for h in range(PER_GROUP):
        joined = jnp.zeros((GROUP, HD), F32)
        for z in range(Z):
            joined = joined + got_ref[z, :, h * HD : (h + 1) * HD] * weights[z][:, h : h + 1]
        joined = jnp.where((slot & (PAD - 1)) < TRACES, joined, 0.0)
        picked.append(joined.astype(BF16))
    picked = jnp.concatenate(picked, axis=1)
    for k in range(PLANE):
        copies[k].wait()
        part = jnp.dot(picked, weight_s[k], preferred_element_type=F32)
        out_ref[:, k * 256 : (k + 1) * 256] = part


def inner_kernel(me_ref, total_ref, *refs):
    packs, weights, out_ref = refs[:PLANE], refs[PLANE : 2 * PLANE], refs[2 * PLANE]
    stream_s, weight_s, sems = refs[-3:]
    copies = []
    for k in range(PLANE):
        source = packs[k].at[pl.ds(BLOCK, TRACES * STEPS)]
        copies.append(pltpu.make_async_copy(source, stream_s.at[k], sems.at[2 * k]))
        copies.append(pltpu.make_async_copy(weights[k], weight_s.at[k], sems.at[2 * k + 1]))
    for copy in copies:
        copy.start()
    place = me_ref[0] % PLANE
    slot = lax.broadcasted_iota(jnp.int32, (GROUP, TRACES * STEPS), 0)
    at = lax.broadcasted_iota(jnp.int32, (GROUP, TRACES * STEPS), 1)
    trace = slot & (PAD - 1)
    wanted = trace * STEPS + PLANE * (slot >> 3) + place
    chosen = jnp.where((at == wanted) & (trace < TRACES), 1.0, 0.0).astype(BF16)
    for k in range(PLANE):
        copies[2 * k].wait()
        base = jnp.dot(chosen, stream_s[k], preferred_element_type=F32)
        stream = (base + total_ref[:, k * 256 : (k + 1) * 256]).astype(BF16)
        copies[2 * k + 1].wait()
        part = jnp.dot(stream, weight_s[k], preferred_element_type=F32)
        out_ref[...] = part if k == 0 else out_ref[...] + part


def hidden_kernel(inner_ref, class_ref, out_ref):
    hidden = jnp.maximum(inner_ref[...], 0.0).astype(BF16)
    logits = jnp.dot(hidden, class_ref[...], preferred_element_type=F32)
    gap = logits[:, 1:2] - logits[:, 0:1]
    lane = lax.broadcasted_iota(jnp.int32, (PAD, HD), 1)
    row = lax.broadcasted_iota(jnp.int32, (PAD, HD), 0)
    mine = jnp.sum(jnp.where(lane == row, gap, 0.0), axis=0, keepdims=True)
    for k in range(out_ref.shape[0]):
        out_ref[k] = mine


def vote_kernel(prompts, clusters, got_ref, scores_ref, votes_ref):
    gap = jnp.concatenate([got_ref[k] for k in range(STEPS)], axis=0)
    scores = 1.0 / (1.0 + jnp.exp(-gap.T[:PAD]))
    scores_ref[...] = scores[:TRACES]
    chain = jnp.min(scores, axis=1, keepdims=True)
    prompt = lax.broadcasted_iota(jnp.int32, (PROMPTS, CLUSTERS), 0)
    cluster = lax.broadcasted_iota(jnp.int32, (PROMPTS, CLUSTERS), 1)
    votes = jnp.zeros((PROMPTS, CLUSTERS), F32)
    for t in range(TRACES):
        here = (prompt == prompts[t]) & (cluster == clusters[t])
        votes = votes + jnp.where(here, chain[t : t + 1, :], 0.0)
    votes_ref[...] = votes


def swapped(value, axis, bit):
    count = lax.axis_size(axis)
    return lax.ppermute(value, axis, [(s, s ^ bit) for s in range(count)])


def raised(value, planes):
    count = lax.axis_size("ctx")
    steps = planes * PLANE
    return lax.ppermute(value, "ctx", [(s, (s + steps) % count) for s in range(count)])


def per_device(
    queries,
    keys_values,
    trace_lengths,
    step_rows,
    prompt_ids,
    cluster_ids,
    step_stream,
    out_weight,
    score_weight,
    class_weight,
):
    me = lax.axis_index("ctx").astype(jnp.int32).reshape(1)
    columns = [[PLANE * z + j for z in range(Z)] for j in range(PLANE)]
    tie = lambda *values: lax.optimization_barrier(values)
    add = functools.partial(attend, me=me, lengths=trace_lengths, queries=queries)

    kv0 = keys_values
    core0 = swapped(kv0, "ctx", 1)

    half = PER_GROUP * HD
    packed = (BLOCK + TRACES * STEPS, 256)
    keep, passed, sent, weight = small_call(
        pick_kernel,
        tuple(jax.ShapeDtypeStruct((n * GROUP, half), BF16) for n in (1, 1, 2))
        + (pltpu.VMEM(packed, BF16),),
        [me, *pinned([step_rows, queries, out_weight, step_stream])],
        [SMEM] + [HBM] * 4,
        [VMEM] * 4,
        scratch_shapes=[
            pltpu.VMEM((PLANE * GROUP, half), BF16),
            pltpu.VMEM((TRACES, STEPS), jnp.int32),
            pltpu.VMEM((BLOCK, half), BF16),
            pltpu.SemaphoreType.DMA((7,)),
        ],
        name="pick",
    )
    arrived = swapped(sent, "ctx", 1)
    across = swapped(passed + arrived[GROUP:], "ctx", 2)
    wanted = keep + arrived[:GROUP] + across
    wanted, kv0y, core0 = tie(wanted, kv0, core0)
    wanted1, wanted2 = raised(wanted, -1), raised(wanted, -2)
    across0 = swapped(kv0y, "ctx", 2)
    across0, wanted1, wanted2 = tie(across0, wanted1, wanted2)
    core0y = swapped(across0, "ctx", 1)
    kv1, own_core = tie(raised(kv0, 1), core0)
    state = add([(0, 0, 0, 0), (0, 1, 1, 0)], kvs=[pinned([kv0y])[0], own_core], state=None)
    wanted, wanted1, wanted2, *state = tie(wanted, wanted1, wanted2, *state)

    weight, wanted = tie(weight, wanted)
    firsts = [weight, swapped(weight, "ctx", 1), swapped(weight, "ctx", 2)]
    firsts.append(swapped(firsts[2], "ctx", 1))

    parts, moved = small_call(
        picked_kernel,
        (jax.ShapeDtypeStruct((GROUP, half), F32), pltpu.HBM((PLANE, BLOCK, HD), BF16)),
        [
            me,
            *pinned([trace_lengths, step_rows]),
            wanted,
            wanted1,
            wanted2,
            *pinned([kv0]),
            core0,
            across0,
            core0y,
        ],
        [SMEM, HBM, HBM] + [VMEM] * 3 + [HBM] * 4,
        [VMEM, HBM],
        scratch_shapes=[
            pltpu.VMEM((2 * PLANE, BLOCK, HD), BF16),
            pltpu.SMEM((TRACES,), jnp.int32),
            pltpu.VMEM((TRACES, STEPS), jnp.int32),
            pltpu.SemaphoreType.DMA((PLANE + 3,)),
        ],
        name="picked",
    )
    parts, kv1, *state = tie(parts, kv1, *state)
    across1 = swapped(kv1, "ctx", 2)
    *firsts, across1, weight = tie(*firsts, across1, score_weight)
    weights = [weight, None, swapped(weight, "ctx", 2)]
    parts = jnp.broadcast_to(parts.astype(jnp.float16)[None], (Z, GROUP, half))
    parts = lax.all_to_all(parts, "ctx", 0, 0, axis_index_groups=columns).astype(F32)
    state, pair1 = add(
        [(0, 2, 0, 0), (0, 3, 0, 1), (1, 0, 1, 0), (1, 2, 2, 0)],
        kvs=[*pinned([moved]), kv1, across1],
        state=state,
        joined=2,
    )
    parts, pair1, weight, *state = tie(parts, pair1, weight, *state)
    weights[1] = swapped(weight, "ctx", 1)

    projected = small_call(
        project_kernel,
        jax.ShapeDtypeStruct((GROUP, WIDE), F32),
        [parts, *firsts],
        [VMEM] + [HBM] * 4,
        scratch_shapes=[
            pltpu.VMEM((PLANE, BLOCK, 256), BF16),
            pltpu.SemaphoreType.DMA((PLANE,)),
        ],
        name="project",
    )
    projected, pair1 = tie((projected * 0.25).astype(jnp.float16), pair1)
    pair2, cores1 = raised(pair1, 1), swapped(pair1, "ctx", 1)
    projected = projected + swapped(projected, "head", 2)
    projected, weights[2] = tie(projected, weights[2])
    projected = projected + swapped(projected, "head", 4)
    projected, cores1 = tie(projected, cores1)
    weights.append(swapped(weights[2], "ctx", 1))
    other = swapped(projected, "head", 1)
    state = add([(1, 1, 0, 0), (1, 3, 0, 1)], kvs=[cores1], state=state)
    other, pair2, *state = tie(other, pair2, *state)
    cores2 = swapped(pair2, "ctx", 1)
    projected = (projected.astype(F32) + other.astype(F32)) * 4.0

    inner = small_call(
        inner_kernel,
        jax.ShapeDtypeStruct((GROUP, WIDE), F32),
        [me, projected, *firsts, *weights],
        [SMEM, VMEM] + [HBM] * 8,
        scratch_shapes=[
            pltpu.VMEM((PLANE, TRACES * STEPS, 256), BF16),
            pltpu.VMEM((PLANE, 256, WIDE), BF16),
            pltpu.SemaphoreType.DMA((2 * PLANE,)),
        ],
        name="inner",
    )
    inner, pair2, *state = tie(inner, pair2, *state)
    inner = (inner * 2.0**-10).astype(jnp.float16).reshape(Z, PAD, WIDE)
    state = add([(2, 0, 0, 0), (2, 2, 0, 1)], kvs=pinned([pair2]), state=state)
    inner = lax.all_to_all(inner, "ctx", 0, 0, axis_index_groups=columns)
    inner, *state = tie(inner, *state)
    inner = jnp.sum(inner.astype(F32), axis=0) * 2.0**10
    heads, count = lax.axis_size("head"), lax.axis_size("ctx")
    gap = small_call(
        hidden_kernel,
        jax.ShapeDtypeStruct((heads, 1, HD), F32),
        [inner, class_weight],
        name="hidden",
    )
    gap, cores2, *state = tie(gap, cores2, *state)
    attended = add([(2, 1, 0, 0), (2, 3, 0, 1)], kvs=[cores2], state=state, last=True)
    gap = lax.all_to_all(gap, "head", 0, 0)
    gap, attended = tie(gap, attended)
    gap = jnp.sum(gap, axis=0)
    gap = lax.all_to_all(jnp.broadcast_to(gap[None], (count, 1, HD)), "ctx", 0, 0)
    step_scores, votes = small_call(
        vote_kernel,
        (
            jax.ShapeDtypeStruct((TRACES, STEPS), F32),
            jax.ShapeDtypeStruct((PROMPTS, CLUSTERS), F32),
        ),
        [prompt_ids, cluster_ids, gap],
        [SMEM, SMEM, VMEM],
        name="vote",
    )
    return (attended, step_scores, votes)


def solution(mesh):
    placed = (
        P("ctx", "head"),
        P(None, "ctx", "head"),
        P(),
        P(),
        P(),
        P(),
        P(None, "ctx"),
        P("head", "ctx"),
        P("ctx", "head"),
        P("head", None),
    )
    return jax.shard_map(
        per_device,
        mesh=mesh,
        in_specs=placed,
        out_specs=(P("ctx", "head"), P(), P()),
        check_vma=False,
    )
```

```python
import functools
import math

import jax
import jax.numpy as jnp
from jax import lax
from jax.experimental import pallas as pl
from jax.experimental.pallas import tpu as pltpu
from jax.sharding import PartitionSpec as P

HD = 128
PROMPTS = 2
CLUSTERS = 4
TRACES = 7
STEPS = 32
PER_GROUP = 4
BLOCK = 512
TILE = 512
OWN_TILE = 256
Z = 8
PLANE = 4
PAD = 8
GROUP = Z * PAD
WIDE = 1024
COEF = HD**-0.5 * math.log2(math.e)
LOW = -1e30
NONE = -60000.0
VMEM = pl.BlockSpec(memory_space=pltpu.VMEM)
SMEM = pl.BlockSpec(memory_space=pltpu.SMEM)
HBM = pl.BlockSpec(memory_space=pltpu.HBM)
BF16 = jnp.bfloat16
F32 = jnp.float32


def first_key(row, lengths):
    start = row * 0
    end = jnp.int32(0)
    for t in range(TRACES):
        end = end + lengths[t]
        start = jnp.where(row >= end, end, start)
    return start


def pick_kernel(me_ref, steps_hbm, q_hbm, weight_hbm, stream_hbm, *refs):
    keep_ref, pass_ref, send_ref, pack_ref, all_ref, steps_ref, q_ref, sems = refs
    copies = [pltpu.make_async_copy(steps_hbm, steps_ref, sems.at[0])]
    for k in range(4):
        part = pl.ds(k * BLOCK // 4, BLOCK // 4)
        copies.append(pltpu.make_async_copy(q_hbm.at[part], q_ref.at[part], sems.at[1 + k]))
    for k, (source, begin) in enumerate([(weight_hbm, 0), (stream_hbm, BLOCK)]):
        target = pack_ref.at[pl.ds(begin, source.shape[0])]
        copies.append(pltpu.make_async_copy(source, target, sems.at[5 + k]))
    for copy in copies:
        copy.start()
    for copy in copies[:5]:
        copy.wait()
    me = me_ref[0]
    core, side = me % 2, (me // 2) % 2
    at = lax.broadcasted_iota(jnp.int32, (TRACES, BLOCK), 1) + me * BLOCK
    none = jnp.zeros((PAD - TRACES, BLOCK), F32)
    steps = steps_ref[...]
    for c in range(2):
        for y in range(2):
            parts = []
            for z in range(Z):
                step = PLANE * z + 2 * y + c
                parts.append(jnp.where(steps[:, step : step + 1] == at, 1.0, 0.0))
                parts.append(none)
            chosen = jnp.concatenate(parts, axis=0).astype(BF16)
            got = jnp.dot(chosen, q_ref[...], preferred_element_type=F32)
            all_ref[pl.ds((2 * c + y) * GROUP, GROUP), :] = got.astype(BF16)

    def group(c, y):
        return all_ref[pl.ds(pl.multiple_of((2 * c + y) * GROUP, GROUP), GROUP), :]

    keep_ref[...] = group(core, side)
    pass_ref[...] = group(core, 1 - side)
    send_ref[:GROUP] = group(1 - core, side)
    send_ref[GROUP:] = group(1 - core, 1 - side)
    for copy in copies[5:]:
        copy.wait()


def picked_kernel(me_ref, lengths_hbm, steps_hbm, q_ref, q1_ref, q2_ref, *refs):
    kv_refs, out_ref, moved_hbm = refs[:PLANE], refs[PLANE], refs[PLANE + 1]
    kv_s, lengths, steps_ref, sems = refs[-4:]
    lengths_copy = pltpu.make_async_copy(lengths_hbm, lengths, sems.at[PLANE])
    steps_copy = pltpu.make_async_copy(steps_hbm, steps_ref, sems.at[PLANE + 1])
    copies = [
        pltpu.make_async_copy(kv, kv_s.at[pl.ds(2 * k, 2)], sems.at[k])
        for k, kv in enumerate(kv_refs)
    ]
    half = pl.ds(PLANE, PLANE)
    moved_copy = pltpu.make_async_copy(kv_s.at[half], moved_hbm, sems.at[PLANE + 2])
    for copy in [lengths_copy, steps_copy] + copies:
        copy.start()
    lengths_copy.wait()
    steps_copy.wait()
    me = me_ref[0]
    place = me % PLANE
    steps = steps_ref[...]
    lane = lax.broadcasted_iota(jnp.int32, (TRACES, STEPS), 1)
    none = jnp.full((PAD - TRACES, HD), -1, jnp.int32)
    parts = []
    for z in range(Z):
        mine = jnp.where(lane == PLANE * z + place, steps, 0)
        mine = jnp.sum(mine, axis=1, keepdims=True)
        parts.append(jnp.broadcast_to(mine, (TRACES, HD)))
        parts.append(none)
    row = jnp.concatenate(parts, axis=0)
    start = first_key(row, lengths)
    row = jnp.concatenate([row] * (BLOCK // HD), axis=1)
    start = jnp.concatenate([start] * (BLOCK // HD), axis=1)
    k_pos = lax.broadcasted_iota(jnp.int32, (GROUP, BLOCK), 1)
    q = (q_ref[...].astype(F32) + q1_ref[...].astype(F32) + q2_ref[...].astype(F32)).astype(BF16)
    q = jnp.concatenate([q[:, h * HD : (h + 1) * HD] for h in range(PER_GROUP)], axis=0)
    scores = []
    for k in range(PLANE):
        key0 = (me - place + (place ^ k)) * BLOCK
        mask = (k_pos <= row - key0) & (k_pos >= start - key0)
        mask = jnp.concatenate([mask] * PER_GROUP, axis=0)
        copies[k].wait()
        s = lax.dot_general(
            q, kv_s[2 * k], (((1,), (1,)), ((), ())), preferred_element_type=F32
        )
        scores.append(jnp.where(mask, s, LOW))
    moved_copy.start()
    top = jnp.maximum(jnp.maximum(scores[0], scores[1]), jnp.maximum(scores[2], scores[3]))
    top = jnp.maximum(jnp.max(top, axis=1, keepdims=True), 0.1 * LOW)
    ones = jnp.ones((BLOCK, HD), BF16)
    pv = jnp.zeros((PER_GROUP * GROUP, 2 * HD), F32)
    for k, s in enumerate(scores):
        p = jnp.exp2((s - top) * COEF).astype(BF16)
        ext = jnp.concatenate([kv_s[2 * k + 1], ones], axis=1)
        pv = pv + jnp.dot(p, ext, preferred_element_type=F32)
    total = pv[:, HD:]
    some = total > 0.0
    total = jnp.where(some, total, 1.0)
    value = pv[:, :HD] / total
    size = jnp.where(some, top * COEF + jnp.log2(total), NONE)
    lanes = lax.broadcasted_iota(jnp.int32, (GROUP, HD), 1)
    stats = jnp.zeros((GROUP, HD), F32)
    for h in range(PER_GROUP):
        rows = slice(h * GROUP, (h + 1) * GROUP)
        out_ref[:, h * HD : (h + 1) * HD] = value[rows]
        rest = size[rows]
        for k in range(3):
            coarse = rest.astype(BF16).astype(F32)
            stats = jnp.where(lanes == PER_GROUP * k + h, coarse, stats)
            rest = rest - coarse
    for z in range(Z):
        packed = jnp.zeros((1, HD), F32)
        for t in range(TRACES):
            at = z * PAD + t
            packed = packed + pltpu.roll(stats[at : at + 1], 16 * t, 1)
        out_ref[z * PAD + TRACES : (z + 1) * PAD, :HD] = packed
    moved_copy.wait()


def attend_kernel(slots, first, last, *refs):
    n = len(slots)
    arrays = 1 + max(slot[2] for slot in slots)
    me_ref, lengths_hbm, q_hbm = refs[:3]
    kv_hbm = [refs[3 + array].at[pl.ds(2 * at, 2)] for _, _, array, at in slots]
    m_ref, l_ref, acc_ref = refs[3 + arrays : 6 + arrays]
    q_ref, kv_ref, lengths, sems = refs[-4:]
    copies = [
        pltpu.make_async_copy(kv, kv_ref.at[k], sems.at[k]) for k, kv in enumerate(kv_hbm)
    ]
    copies.append(pltpu.make_async_copy(lengths_hbm, lengths, sems.at[n]))
    for k in range(4):
        part = pl.ds(k * BLOCK // 4, BLOCK // 4)
        copies.append(
            pltpu.make_async_copy(q_hbm.at[part], q_ref.at[part], sems.at[n + 1 + k])
        )
    for copy in copies:
        copy.start()
    for copy in copies:
        copy.wait()
    me = me_ref[0]
    place = me % PLANE
    row0 = me * BLOCK
    ones = jnp.ones((BLOCK, HD), BF16)
    blocks = [me - place - back * PLANE + (place ^ flip) for back, flip, _, _ in slots]

    def weigh(rows, count, keys, ext, mask, fresh):
        q = q_ref[rows, :]
        q = jnp.concatenate([q[:, h * HD : (h + 1) * HD] for h in range(PER_GROUP)], axis=0)
        s = lax.dot_general(q, keys, (((1,), (1,)), ((), ())), preferred_element_type=F32)
        for h in range(PER_GROUP):
            cols = slice(h * HD, (h + 1) * HD)
            mine = s[h * count : (h + 1) * count]
            if mask is not None:
                mine = jnp.where(mask, mine, LOW)
            top = jnp.max(mine, axis=1, keepdims=True)
            if fresh:
                top = jnp.broadcast_to(top, (count, HD))
            else:
                before = m_ref[rows, cols]
                top = jnp.maximum(before, top)
            wide = jnp.concatenate([top] * (mine.shape[1] // HD), axis=1)
            p = jnp.exp2((mine - wide) * COEF).astype(BF16)
            pv = jnp.dot(p, ext, preferred_element_type=F32)
            m_ref[rows, cols] = top
            if fresh:
                acc_ref[rows, cols] = pv[:, :HD]
                l_ref[rows, cols] = pv[:, HD:]
            else:
                scale = jnp.exp2((before - top) * COEF)
                acc_ref[rows, cols] = acc_ref[rows, cols] * scale + pv[:, :HD]
                l_ref[rows, cols] = l_ref[rows, cols] * scale + pv[:, HD:]

    def own_block():
        for tile in range(BLOCK // OWN_TILE):
            width = (tile + 1) * OWN_TILE
            rows = slice(tile * OWN_TILE, width)
            keys = kv_ref[0, 0, :width, :]
            ext = jnp.concatenate([kv_ref[0, 1, :width, :], ones[:width]], axis=1)
            shape = (OWN_TILE, width)
            q_pos = row0 + tile * OWN_TILE + lax.broadcasted_iota(jnp.int32, shape, 0)
            k_pos = row0 + lax.broadcasted_iota(jnp.int32, shape, 1)
            starts = first_key(q_pos[:, :HD], lengths)
            starts = jnp.concatenate([starts] * (width // HD), axis=1)
            mask = (k_pos <= q_pos) & (k_pos >= starts)
            weigh(rows, OWN_TILE, keys, ext, mask, True)

    def other_tile(index, carry):
        tile, k = index % (BLOCK // TILE), index // (BLOCK // TILE)
        block = blocks[-1]
        for other in range(n - 1):
            block = jnp.where(k == other, blocks[other], block)
        key0 = block * BLOCK
        begin = pl.multiple_of(tile * TILE, TILE)
        rows = pl.ds(begin, TILE)
        low = first_key(row0 + begin, lengths)
        high = first_key(row0 + begin + TILE - 1, lengths)
        some = (block < me) & (key0 + BLOCK > low)
        every = key0 >= high

        def run(masked):
            keys = kv_ref[k, 0]
            ext = jnp.concatenate([kv_ref[k, 1], ones], axis=1)
            mask = None
            if masked:
                starts = first_key(
                    row0 + begin + lax.broadcasted_iota(jnp.int32, (TILE, HD), 0), lengths
                )
                starts = jnp.concatenate([starts] * (BLOCK // HD), axis=1)
                k_pos = key0 + lax.broadcasted_iota(jnp.int32, (TILE, BLOCK), 1)
                mask = k_pos >= starts
            weigh(rows, TILE, keys, ext, mask, False)

        pl.when(some & every)(functools.partial(run, False))
        pl.when(some & jnp.logical_not(every))(functools.partial(run, True))
        return carry

    if first:
        own_block()
    tiles = BLOCK // TILE
    lax.fori_loop(tiles * int(first), tiles * n, other_tile, 0)
    if last:
        out_ref = refs[-5]
        out_ref[...] = acc_ref[...] / l_ref[...]


def attend(slots, me, lengths, queries, kvs, state, last=False):
    shape = (BLOCK, PER_GROUP * HD)
    first = state is None
    operands = [me, *pinned([lengths, queries]), *kvs]
    specs = [SMEM] + [HBM] * (len(operands) - 1)
    shapes, aliases = (pltpu.VMEM(shape, F32),) * 3, {}
    if not first:
        at = len(operands)
        operands += [pltpu.with_memory_space_constraint(x, pltpu.VMEM) for x in state]
        specs += [VMEM] * 3
        aliases = {at + k: k for k in range(3)}
    if last:
        shapes, aliases = (jax.ShapeDtypeStruct(shape, F32),), {}
    work = PER_GROUP * BLOCK * BLOCK * len(slots)
    got = pl.pallas_call(
        functools.partial(attend_kernel, slots, first, last),
        out_shape=shapes,
        in_specs=specs,
        out_specs=[VMEM] * len(shapes),
        scratch_shapes=[
            pltpu.VMEM(shape, BF16),
            pltpu.VMEM((len(slots), 2, BLOCK, HD), BF16),
            pltpu.SMEM((TRACES,), jnp.int32),
            pltpu.SemaphoreType.DMA((len(slots) + 5,)),
        ],
        input_output_aliases=aliases,
        compiler_params=pltpu.CompilerParams(vmem_limit_bytes=20 << 20),
        cost_estimate=pl.CostEstimate(
            flops=4 * HD * work, bytes_accessed=1 << 20, transcendentals=work
        ),
        name="attend_%d_%d" % slots[0][:2],
    )(*operands)
    if last:
        return got[0]
    return list(got)


def pinned(values):
    return [pltpu.with_memory_space_constraint(value, pltpu.HBM) for value in values]


def small_call(kernel, shape, operands, specs=None, out_specs=None, **kw):
    return pl.pallas_call(
        kernel,
        out_shape=shape,
        in_specs=specs or [VMEM] * len(operands),
        out_specs=out_specs or ([VMEM] * len(shape) if type(shape) is tuple else VMEM),
        compiler_params=pltpu.CompilerParams(vmem_limit_bytes=16 << 20),
        **kw,
    )(*operands)


def project_kernel(got_ref, *refs):
    packs, blocks, out_ref, pair_ref = refs[:PLANE], refs[PLANE:-4], refs[-4], refs[-3]
    weight_s, sems = refs[-2:]
    copies = [
        pltpu.make_async_copy(pack.at[pl.ds(0, BLOCK)], weight_s.at[k], sems.at[k])
        for k, pack in enumerate(packs)
    ]
    for k, block in enumerate(blocks):
        target = pair_ref.at[pl.ds(2 * k, 2)]
        copies.append(pltpu.make_async_copy(block, target, sems.at[PLANE + k]))
    for copy in copies:
        copy.start()
    sizes = []
    for z in range(Z):
        stats = []
        for step in range(Z):
            packed = got_ref[z, step * PAD + TRACES : (step + 1) * PAD, :HD]
            for t in range(PAD):
                stats.append(pltpu.roll(packed, (HD - 16 * t) % HD, 1))
        sizes.append(jnp.concatenate(stats, axis=0))
    sizes = [
        size
        + pltpu.roll(size, HD - PER_GROUP, 1)
        + pltpu.roll(size, HD - 2 * PER_GROUP, 1)
        for size in sizes
    ]
    top = functools.reduce(jnp.maximum, sizes)
    weights = [jnp.exp2(size - top) for size in sizes]
    total = functools.reduce(jnp.add, weights)
    weights = [weight / total for weight in weights]
    slot = lax.broadcasted_iota(jnp.int32, (GROUP, HD), 0)
    picked = []
    for h in range(PER_GROUP):
        joined = jnp.zeros((GROUP, HD), F32)
        for z in range(Z):
            joined = joined + got_ref[z, :, h * HD : (h + 1) * HD] * weights[z][:, h : h + 1]
        joined = jnp.where((slot & (PAD - 1)) < TRACES, joined, 0.0)
        picked.append(joined.astype(BF16))
    picked = jnp.concatenate(picked, axis=1)
    for k in range(PLANE):
        copies[k].wait()
        part = jnp.dot(picked, weight_s[k], preferred_element_type=F32)
        out_ref[:, k * 256 : (k + 1) * 256] = part
    for copy in copies[PLANE:]:
        copy.wait()


def inner_kernel(me_ref, total_ref, *refs):
    packs, weights, out_ref = refs[:PLANE], refs[PLANE : 2 * PLANE], refs[2 * PLANE]
    stream_s, weight_s, sems = refs[-3:]
    copies = []
    for k in range(PLANE):
        source = packs[k].at[pl.ds(BLOCK, TRACES * STEPS)]
        copies.append(pltpu.make_async_copy(source, stream_s.at[k], sems.at[2 * k]))
        copies.append(pltpu.make_async_copy(weights[k], weight_s.at[k], sems.at[2 * k + 1]))
    for copy in copies:
        copy.start()
    place = me_ref[0] % PLANE
    slot = lax.broadcasted_iota(jnp.int32, (GROUP, TRACES * STEPS), 0)
    at = lax.broadcasted_iota(jnp.int32, (GROUP, TRACES * STEPS), 1)
    trace = slot & (PAD - 1)
    wanted = trace * STEPS + PLANE * (slot >> 3) + place
    chosen = jnp.where((at == wanted) & (trace < TRACES), 1.0, 0.0).astype(BF16)
    for k in range(PLANE):
        copies[2 * k].wait()
        base = jnp.dot(chosen, stream_s[k], preferred_element_type=F32)
        stream = (base + total_ref[:, k * 256 : (k + 1) * 256]).astype(BF16)
        copies[2 * k + 1].wait()
        part = jnp.dot(stream, weight_s[k], preferred_element_type=F32)
        out_ref[...] = part if k == 0 else out_ref[...] + part


def hidden_kernel(inner_ref, class_ref, out_ref):
    hidden = jnp.maximum(inner_ref[...], 0.0).astype(BF16)
    logits = jnp.dot(hidden, class_ref[...], preferred_element_type=F32)
    gap = logits[:, 1:2] - logits[:, 0:1]
    lane = lax.broadcasted_iota(jnp.int32, (PAD, HD), 1)
    row = lax.broadcasted_iota(jnp.int32, (PAD, HD), 0)
    mine = jnp.sum(jnp.where(lane == row, gap, 0.0), axis=0, keepdims=True)
    for k in range(out_ref.shape[0]):
        out_ref[k] = mine


def vote_kernel(prompts, clusters, got_ref, scores_ref, votes_ref):
    gap = jnp.concatenate([got_ref[k] for k in range(STEPS)], axis=0)
    scores = 1.0 / (1.0 + jnp.exp(-gap.T[:PAD]))
    scores_ref[...] = scores[:TRACES]
    chain = jnp.min(scores, axis=1, keepdims=True)
    prompt = lax.broadcasted_iota(jnp.int32, (PROMPTS, CLUSTERS), 0)
    cluster = lax.broadcasted_iota(jnp.int32, (PROMPTS, CLUSTERS), 1)
    votes = jnp.zeros((PROMPTS, CLUSTERS), F32)
    for t in range(TRACES):
        here = (prompt == prompts[t]) & (cluster == clusters[t])
        votes = votes + jnp.where(here, chain[t : t + 1, :], 0.0)
    votes_ref[...] = votes


def swapped(value, axis, bit):
    count = lax.axis_size(axis)
    return lax.ppermute(value, axis, [(s, s ^ bit) for s in range(count)])


def raised(value, planes):
    count = lax.axis_size("ctx")
    steps = planes * PLANE
    return lax.ppermute(value, "ctx", [(s, (s + steps) % count) for s in range(count)])


def per_device(
    queries,
    keys_values,
    trace_lengths,
    step_rows,
    prompt_ids,
    cluster_ids,
    step_stream,
    out_weight,
    score_weight,
    class_weight,
):
    me = lax.axis_index("ctx").astype(jnp.int32).reshape(1)
    columns = [[PLANE * z + j for z in range(Z)] for j in range(PLANE)]
    tie = lambda *values: lax.optimization_barrier(values)
    add = functools.partial(attend, me=me, lengths=trace_lengths, queries=queries)

    kv0 = keys_values
    core0 = swapped(kv0, "ctx", 1)

    half = PER_GROUP * HD
    packed = (BLOCK + TRACES * STEPS, 256)
    keep, passed, sent, weight = small_call(
        pick_kernel,
        tuple(jax.ShapeDtypeStruct((n * GROUP, half), BF16) for n in (1, 1, 2))
        + (pltpu.VMEM(packed, BF16),),
        [me, *pinned([step_rows, queries, out_weight, step_stream])],
        [SMEM] + [HBM] * 4,
        [VMEM] * 4,
        scratch_shapes=[
            pltpu.VMEM((PLANE * GROUP, half), BF16),
            pltpu.VMEM((TRACES, STEPS), jnp.int32),
            pltpu.VMEM((BLOCK, half), BF16),
            pltpu.SemaphoreType.DMA((7,)),
        ],
        name="pick",
    )
    arrived = swapped(sent, "ctx", 1)
    across = swapped(passed + arrived[GROUP:], "ctx", 2)
    wanted = keep + arrived[:GROUP] + across
    wanted, kv0y, core0 = tie(wanted, kv0, core0)
    wanted1, wanted2 = raised(wanted, -1), raised(wanted, -2)
    across0 = swapped(kv0y, "ctx", 2)
    across0, wanted1, wanted2 = tie(across0, wanted1, wanted2)
    core0y = swapped(across0, "ctx", 1)
    state = add([(0, 0, 0, 0), (0, 1, 1, 0)], kvs=[pinned([kv0y])[0], core0], state=None)
    wanted, wanted1, wanted2, *state = tie(wanted, wanted1, wanted2, *state)

    kv1, weight, wanted = tie(raised(kv0, 1), weight, wanted)
    firsts = [weight, swapped(weight, "ctx", 1), swapped(weight, "ctx", 2)]
    firsts.append(swapped(firsts[2], "ctx", 1))

    parts, moved = small_call(
        picked_kernel,
        (jax.ShapeDtypeStruct((GROUP, half), F32), pltpu.HBM((PLANE, BLOCK, HD), BF16)),
        [
            me,
            *pinned([trace_lengths, step_rows]),
            wanted,
            wanted1,
            wanted2,
            *pinned([kv0]),
            core0,
            across0,
            core0y,
        ],
        [SMEM, HBM, HBM] + [VMEM] * 3 + [HBM] * 4,
        [VMEM, HBM],
        scratch_shapes=[
            pltpu.VMEM((2 * PLANE, BLOCK, HD), BF16),
            pltpu.SMEM((TRACES,), jnp.int32),
            pltpu.VMEM((TRACES, STEPS), jnp.int32),
            pltpu.SemaphoreType.DMA((PLANE + 3,)),
        ],
        name="picked",
    )
    parts, kv1, *state = tie(parts, kv1, *state)
    across1 = swapped(kv1, "ctx", 2)
    *firsts, moved, weight = tie(*firsts, moved, score_weight)
    weights = [weight, None, swapped(weight, "ctx", 2)]
    parts = jnp.broadcast_to(parts.astype(jnp.float16)[None], (Z, GROUP, half))
    parts = lax.all_to_all(parts, "ctx", 0, 0, axis_index_groups=columns).astype(F32)
    state = add(
        [(0, 2, 0, 0), (0, 3, 0, 1), (1, 0, 1, 0)], kvs=[*pinned([moved]), kv1], state=state
    )
    parts, weight, *state = tie(parts, weight, *state)
    weights[1] = swapped(weight, "ctx", 1)

    projected, pair1 = small_call(
        project_kernel,
        (jax.ShapeDtypeStruct((GROUP, WIDE), F32), pltpu.VMEM((4, BLOCK, HD), BF16)),
        [parts, *firsts, kv1, across1],
        [VMEM] + [HBM] * 6,
        scratch_shapes=[
            pltpu.VMEM((PLANE, BLOCK, 256), BF16),
            pltpu.SemaphoreType.DMA((PLANE + 2,)),
        ],
        name="project",
    )
    projected, pair1 = tie((projected * 0.25).astype(jnp.float16), pair1)
    pair2, cores1 = raised(pair1, 1), swapped(pair1, "ctx", 1)
    projected = projected + swapped(projected, "head", 2)
    projected, weights[2] = tie(projected, weights[2])
    projected = projected + swapped(projected, "head", 4)
    projected, cores1 = tie(projected, cores1)
    weights.append(swapped(weights[2], "ctx", 1))
    other = swapped(projected, "head", 1)
    state = add([(1, 1, 0, 0), (1, 3, 0, 1)], kvs=[cores1], state=state)
    other, pair2, *state = tie(other, pair2, *state)
    cores2 = swapped(pair2, "ctx", 1)
    projected = (projected.astype(F32) + other.astype(F32)) * 4.0

    inner = small_call(
        inner_kernel,
        jax.ShapeDtypeStruct((GROUP, WIDE), F32),
        [me, projected, *firsts, *weights],
        [SMEM, VMEM] + [HBM] * 8,
        scratch_shapes=[
            pltpu.VMEM((PLANE, TRACES * STEPS, 256), BF16),
            pltpu.VMEM((PLANE, 256, WIDE), BF16),
            pltpu.SemaphoreType.DMA((2 * PLANE,)),
        ],
        name="inner",
    )
    inner, pair2, *state = tie(inner, pair2, *state)
    inner = (inner * 2.0**-10).astype(jnp.float16).reshape(Z, PAD, WIDE)
    state = add(
        [(1, 2, 0, 1), (2, 0, 1, 0), (2, 2, 1, 1)], kvs=[pair1, *pinned([pair2])], state=state
    )
    inner = lax.all_to_all(inner, "ctx", 0, 0, axis_index_groups=columns)
    inner, *state = tie(inner, *state)
    inner = jnp.sum(inner.astype(F32), axis=0) * 2.0**10
    heads, count = lax.axis_size("head"), lax.axis_size("ctx")
    gap = small_call(
        hidden_kernel,
        jax.ShapeDtypeStruct((heads, 1, HD), F32),
        [inner, class_weight],
        name="hidden",
    )
    gap, cores2, *state = tie(gap, cores2, *state)
    attended = add([(2, 1, 0, 0), (2, 3, 0, 1)], kvs=[cores2], state=state, last=True)
    gap = lax.all_to_all(gap, "head", 0, 0)
    gap, attended = tie(gap, attended)
    gap = jnp.sum(gap, axis=0)
    gap = lax.all_to_all(jnp.broadcast_to(gap[None], (count, 1, HD)), "ctx", 0, 0)
    step_scores, votes = small_call(
        vote_kernel,
        (
            jax.ShapeDtypeStruct((TRACES, STEPS), F32),
            jax.ShapeDtypeStruct((PROMPTS, CLUSTERS), F32),
        ),
        [prompt_ids, cluster_ids, gap],
        [SMEM, SMEM, VMEM],
        name="vote",
    )
    return (attended, step_scores, votes)


def solution(mesh):
    placed = (
        P("ctx", "head"),
        P(None, "ctx", "head"),
        P(),
        P(),
        P(),
        P(),
        P(None, "ctx"),
        P("head", "ctx"),
        P("ctx", "head"),
        P("head", None),
    )
    return jax.shard_map(
        per_device,
        mesh=mesh,
        in_specs=placed,
        out_specs=(P("ctx", "head"), P(), P()),
        check_vma=False,
    )
```

```python
import functools
import math

import jax
import jax.numpy as jnp
from jax import lax
from jax.experimental import pallas as pl
from jax.experimental.pallas import tpu as pltpu
from jax.sharding import PartitionSpec as P

HD = 128
PROMPTS = 2
CLUSTERS = 4
TRACES = 7
STEPS = 32
PER_GROUP = 4
BLOCK = 512
TILE = 512
OWN_TILE = 256
Z = 8
PLANE = 4
PAD = 8
GROUP = Z * PAD
WIDE = 1024
COEF = HD**-0.5 * math.log2(math.e)
LOW = -1e30
NONE = -60000.0
VMEM = pl.BlockSpec(memory_space=pltpu.VMEM)
SMEM = pl.BlockSpec(memory_space=pltpu.SMEM)
HBM = pl.BlockSpec(memory_space=pltpu.HBM)
BF16 = jnp.bfloat16
F32 = jnp.float32


def first_key(row, lengths):
    start = row * 0
    end = jnp.int32(0)
    for t in range(TRACES):
        end = end + lengths[t]
        start = jnp.where(row >= end, end, start)
    return start


def pick_kernel(me_ref, steps_hbm, q_hbm, weight_hbm, stream_hbm, *refs):
    keep_ref, pass_ref, send_ref, pack_ref, all_ref, steps_ref, q_ref, sems = refs
    copies = [pltpu.make_async_copy(steps_hbm, steps_ref, sems.at[0])]
    for k in range(4):
        part = pl.ds(k * BLOCK // 4, BLOCK // 4)
        copies.append(pltpu.make_async_copy(q_hbm.at[part], q_ref.at[part], sems.at[1 + k]))
    for k, (source, begin) in enumerate([(weight_hbm, 0), (stream_hbm, BLOCK)]):
        target = pack_ref.at[pl.ds(begin, source.shape[0])]
        copies.append(pltpu.make_async_copy(source, target, sems.at[5 + k]))
    for copy in copies:
        copy.start()
    for copy in copies[:5]:
        copy.wait()
    me = me_ref[0]
    core, side = me % 2, (me // 2) % 2
    at = lax.broadcasted_iota(jnp.int32, (TRACES, BLOCK), 1) + me * BLOCK
    none = jnp.zeros((PAD - TRACES, BLOCK), F32)
    steps = steps_ref[...]
    for c in range(2):
        for y in range(2):
            parts = []
            for z in range(Z):
                step = PLANE * z + 2 * y + c
                parts.append(jnp.where(steps[:, step : step + 1] == at, 1.0, 0.0))
                parts.append(none)
            chosen = jnp.concatenate(parts, axis=0).astype(BF16)
            got = jnp.dot(chosen, q_ref[...], preferred_element_type=F32)
            all_ref[pl.ds((2 * c + y) * GROUP, GROUP), :] = got.astype(BF16)

    def group(c, y):
        return all_ref[pl.ds(pl.multiple_of((2 * c + y) * GROUP, GROUP), GROUP), :]

    keep_ref[...] = group(core, side)
    pass_ref[...] = group(core, 1 - side)
    send_ref[:GROUP] = group(1 - core, side)
    send_ref[GROUP:] = group(1 - core, 1 - side)
    for copy in copies[5:]:
        copy.wait()


def picked_kernel(me_ref, lengths_hbm, steps_hbm, q_ref, q1_ref, q2_ref, *refs):
    kv_refs, out_ref, moved_hbm = refs[:PLANE], refs[PLANE], refs[PLANE + 1]
    kv_s, lengths, steps_ref, sems = refs[-4:]
    lengths_copy = pltpu.make_async_copy(lengths_hbm, lengths, sems.at[PLANE])
    steps_copy = pltpu.make_async_copy(steps_hbm, steps_ref, sems.at[PLANE + 1])
    copies = [
        pltpu.make_async_copy(kv, kv_s.at[pl.ds(2 * k, 2)], sems.at[k])
        for k, kv in enumerate(kv_refs)
    ]
    half = pl.ds(PLANE, PLANE)
    moved_copy = pltpu.make_async_copy(kv_s.at[half], moved_hbm, sems.at[PLANE + 2])
    for copy in [lengths_copy, steps_copy] + copies:
        copy.start()
    lengths_copy.wait()
    steps_copy.wait()
    me = me_ref[0]
    place = me % PLANE
    steps = steps_ref[...]
    lane = lax.broadcasted_iota(jnp.int32, (TRACES, STEPS), 1)
    none = jnp.full((PAD - TRACES, HD), -1, jnp.int32)
    parts = []
    for z in range(Z):
        mine = jnp.where(lane == PLANE * z + place, steps, 0)
        mine = jnp.sum(mine, axis=1, keepdims=True)
        parts.append(jnp.broadcast_to(mine, (TRACES, HD)))
        parts.append(none)
    row = jnp.concatenate(parts, axis=0)
    start = first_key(row, lengths)
    row = jnp.concatenate([row] * (BLOCK // HD), axis=1)
    start = jnp.concatenate([start] * (BLOCK // HD), axis=1)
    k_pos = lax.broadcasted_iota(jnp.int32, (GROUP, BLOCK), 1)
    q = (q_ref[...].astype(F32) + q1_ref[...].astype(F32) + q2_ref[...].astype(F32)).astype(BF16)
    q = jnp.concatenate([q[:, h * HD : (h + 1) * HD] for h in range(PER_GROUP)], axis=0)
    scores = []
    for k in range(PLANE):
        key0 = (me - place + (place ^ k)) * BLOCK
        mask = (k_pos <= row - key0) & (k_pos >= start - key0)
        mask = jnp.concatenate([mask] * PER_GROUP, axis=0)
        copies[k].wait()
        s = lax.dot_general(
            q, kv_s[2 * k], (((1,), (1,)), ((), ())), preferred_element_type=F32
        )
        scores.append(jnp.where(mask, s, LOW))
    moved_copy.start()
    top = jnp.maximum(jnp.maximum(scores[0], scores[1]), jnp.maximum(scores[2], scores[3]))
    top = jnp.maximum(jnp.max(top, axis=1, keepdims=True), 0.1 * LOW)
    ones = jnp.ones((BLOCK, HD), BF16)
    pv = jnp.zeros((PER_GROUP * GROUP, 2 * HD), F32)
    for k, s in enumerate(scores):
        p = jnp.exp2((s - top) * COEF).astype(BF16)
        ext = jnp.concatenate([kv_s[2 * k + 1], ones], axis=1)
        pv = pv + jnp.dot(p, ext, preferred_element_type=F32)
    total = pv[:, HD:]
    some = total > 0.0
    total = jnp.where(some, total, 1.0)
    value = pv[:, :HD] / total
    size = jnp.where(some, top * COEF + jnp.log2(total), NONE)
    lanes = lax.broadcasted_iota(jnp.int32, (GROUP, HD), 1)
    stats = jnp.zeros((GROUP, HD), F32)
    for h in range(PER_GROUP):
        rows = slice(h * GROUP, (h + 1) * GROUP)
        out_ref[:, h * HD : (h + 1) * HD] = value[rows]
        rest = size[rows]
        for k in range(3):
            coarse = rest.astype(BF16).astype(F32)
            stats = jnp.where(lanes == PER_GROUP * k + h, coarse, stats)
            rest = rest - coarse
    for z in range(Z):
        packed = jnp.zeros((1, HD), F32)
        for t in range(TRACES):
            at = z * PAD + t
            packed = packed + pltpu.roll(stats[at : at + 1], 16 * t, 1)
        out_ref[z * PAD + TRACES : (z + 1) * PAD, :HD] = packed
    moved_copy.wait()


def attend_kernel(slots, first, last, *refs):
    n = len(slots)
    arrays = 1 + max(slot[2] for slot in slots)
    me_ref, lengths_hbm, q_hbm = refs[:3]
    kv_hbm = [refs[3 + array].at[pl.ds(2 * at, 2)] for _, _, array, at in slots]
    m_ref, l_ref, acc_ref = refs[3 + arrays : 6 + arrays]
    q_ref, kv_ref, lengths, sems = refs[-4:]
    copies = [
        pltpu.make_async_copy(kv, kv_ref.at[k], sems.at[k]) for k, kv in enumerate(kv_hbm)
    ]
    copies.append(pltpu.make_async_copy(lengths_hbm, lengths, sems.at[n]))
    for k in range(4):
        part = pl.ds(k * BLOCK // 4, BLOCK // 4)
        copies.append(
            pltpu.make_async_copy(q_hbm.at[part], q_ref.at[part], sems.at[n + 1 + k])
        )
    for copy in copies:
        copy.start()
    for copy in copies:
        copy.wait()
    me = me_ref[0]
    place = me % PLANE
    row0 = me * BLOCK
    ones = jnp.ones((BLOCK, HD), BF16)
    blocks = [me - place - back * PLANE + (place ^ flip) for back, flip, _, _ in slots]

    def weigh(rows, count, keys, ext, mask, fresh):
        q = q_ref[rows, :]
        q = jnp.concatenate([q[:, h * HD : (h + 1) * HD] for h in range(PER_GROUP)], axis=0)
        s = lax.dot_general(q, keys, (((1,), (1,)), ((), ())), preferred_element_type=F32)
        for h in range(PER_GROUP):
            cols = slice(h * HD, (h + 1) * HD)
            mine = s[h * count : (h + 1) * count]
            if mask is not None:
                mine = jnp.where(mask, mine, LOW)
            top = jnp.max(mine, axis=1, keepdims=True)
            if fresh:
                top = jnp.broadcast_to(top, (count, HD))
            else:
                before = m_ref[rows, cols]
                top = jnp.maximum(before, top)
            wide = jnp.concatenate([top] * (mine.shape[1] // HD), axis=1)
            p = jnp.exp2((mine - wide) * COEF).astype(BF16)
            pv = jnp.dot(p, ext, preferred_element_type=F32)
            m_ref[rows, cols] = top
            if fresh:
                acc_ref[rows, cols] = pv[:, :HD]
                l_ref[rows, cols] = pv[:, HD:]
            else:
                scale = jnp.exp2((before - top) * COEF)
                acc_ref[rows, cols] = acc_ref[rows, cols] * scale + pv[:, :HD]
                l_ref[rows, cols] = l_ref[rows, cols] * scale + pv[:, HD:]

    def own_block():
        for tile in range(BLOCK // OWN_TILE):
            width = (tile + 1) * OWN_TILE
            rows = slice(tile * OWN_TILE, width)
            keys = kv_ref[0, 0, :width, :]
            ext = jnp.concatenate([kv_ref[0, 1, :width, :], ones[:width]], axis=1)
            shape = (OWN_TILE, width)
            q_pos = row0 + tile * OWN_TILE + lax.broadcasted_iota(jnp.int32, shape, 0)
            k_pos = row0 + lax.broadcasted_iota(jnp.int32, shape, 1)
            starts = first_key(q_pos[:, :HD], lengths)
            starts = jnp.concatenate([starts] * (width // HD), axis=1)
            mask = (k_pos <= q_pos) & (k_pos >= starts)
            weigh(rows, OWN_TILE, keys, ext, mask, True)

    def other_tile(index, carry):
        tile, k = index % (BLOCK // TILE), index // (BLOCK // TILE)
        block = blocks[-1]
        for other in range(n - 1):
            block = jnp.where(k == other, blocks[other], block)
        key0 = block * BLOCK
        begin = pl.multiple_of(tile * TILE, TILE)
        rows = pl.ds(begin, TILE)
        low = first_key(row0 + begin, lengths)
        high = first_key(row0 + begin + TILE - 1, lengths)
        some = (block < me) & (key0 + BLOCK > low)
        every = key0 >= high

        def run(masked):
            keys = kv_ref[k, 0]
            ext = jnp.concatenate([kv_ref[k, 1], ones], axis=1)
            mask = None
            if masked:
                starts = first_key(
                    row0 + begin + lax.broadcasted_iota(jnp.int32, (TILE, HD), 0), lengths
                )
                starts = jnp.concatenate([starts] * (BLOCK // HD), axis=1)
                k_pos = key0 + lax.broadcasted_iota(jnp.int32, (TILE, BLOCK), 1)
                mask = k_pos >= starts
            weigh(rows, TILE, keys, ext, mask, False)

        pl.when(some & every)(functools.partial(run, False))
        pl.when(some & jnp.logical_not(every))(functools.partial(run, True))
        return carry

    if first:
        own_block()
    tiles = BLOCK // TILE
    lax.fori_loop(tiles * int(first), tiles * n, other_tile, 0)
    if last:
        out_ref = refs[-5]
        out_ref[...] = acc_ref[...] / l_ref[...]


def attend(slots, me, lengths, queries, kvs, state, last=False):
    shape = (BLOCK, PER_GROUP * HD)
    first = state is None
    operands = [me, *pinned([lengths, queries]), *kvs]
    specs = [SMEM] + [HBM] * (len(operands) - 1)
    shapes, aliases = (pltpu.VMEM(shape, F32),) * 3, {}
    if not first:
        at = len(operands)
        operands += [pltpu.with_memory_space_constraint(x, pltpu.VMEM) for x in state]
        specs += [VMEM] * 3
        aliases = {at + k: k for k in range(3)}
    if last:
        shapes, aliases = (jax.ShapeDtypeStruct(shape, F32),), {}
    work = PER_GROUP * BLOCK * BLOCK * len(slots)
    got = pl.pallas_call(
        functools.partial(attend_kernel, slots, first, last),
        out_shape=shapes,
        in_specs=specs,
        out_specs=[VMEM] * len(shapes),
        scratch_shapes=[
            pltpu.VMEM(shape, BF16),
            pltpu.VMEM((len(slots), 2, BLOCK, HD), BF16),
            pltpu.SMEM((TRACES,), jnp.int32),
            pltpu.SemaphoreType.DMA((len(slots) + 5,)),
        ],
        input_output_aliases=aliases,
        compiler_params=pltpu.CompilerParams(vmem_limit_bytes=20 << 20),
        cost_estimate=pl.CostEstimate(
            flops=4 * HD * work, bytes_accessed=1 << 20, transcendentals=work
        ),
        name="attend_%d_%d" % slots[0][:2],
    )(*operands)
    if last:
        return got[0]
    return list(got)


def pinned(values):
    return [pltpu.with_memory_space_constraint(value, pltpu.HBM) for value in values]


def small_call(kernel, shape, operands, specs=None, out_specs=None, **kw):
    return pl.pallas_call(
        kernel,
        out_shape=shape,
        in_specs=specs or [VMEM] * len(operands),
        out_specs=out_specs or ([VMEM] * len(shape) if type(shape) is tuple else VMEM),
        compiler_params=pltpu.CompilerParams(vmem_limit_bytes=16 << 20),
        **kw,
    )(*operands)


def project_kernel(got_ref, *refs):
    packs, blocks, out_ref, pair_ref = refs[:PLANE], refs[PLANE:-4], refs[-4], refs[-3]
    weight_s, sems = refs[-2:]
    copies = [
        pltpu.make_async_copy(pack.at[pl.ds(0, BLOCK)], weight_s.at[k], sems.at[k])
        for k, pack in enumerate(packs)
    ]
    for k, block in enumerate(blocks):
        target = pair_ref.at[pl.ds(2 * k, 2)]
        copies.append(pltpu.make_async_copy(block, target, sems.at[PLANE + k]))
    for copy in copies:
        copy.start()
    sizes = []
    for z in range(Z):
        stats = []
        for step in range(Z):
            packed = got_ref[z, step * PAD + TRACES : (step + 1) * PAD, :HD]
            for t in range(PAD):
                stats.append(pltpu.roll(packed, (HD - 16 * t) % HD, 1))
        sizes.append(jnp.concatenate(stats, axis=0))
    sizes = [
        size
        + pltpu.roll(size, HD - PER_GROUP, 1)
        + pltpu.roll(size, HD - 2 * PER_GROUP, 1)
        for size in sizes
    ]
    top = functools.reduce(jnp.maximum, sizes)
    weights = [jnp.exp2(size - top) for size in sizes]
    total = functools.reduce(jnp.add, weights)
    weights = [weight / total for weight in weights]
    slot = lax.broadcasted_iota(jnp.int32, (GROUP, HD), 0)
    picked = []
    for h in range(PER_GROUP):
        joined = jnp.zeros((GROUP, HD), F32)
        for z in range(Z):
            joined = joined + got_ref[z, :, h * HD : (h + 1) * HD] * weights[z][:, h : h + 1]
        joined = jnp.where((slot & (PAD - 1)) < TRACES, joined, 0.0)
        picked.append(joined.astype(BF16))
    picked = jnp.concatenate(picked, axis=1)
    for k in range(PLANE):
        copies[k].wait()
        part = jnp.dot(picked, weight_s[k], preferred_element_type=F32)
        out_ref[:, k * 256 : (k + 1) * 256] = part
    for copy in copies[PLANE:]:
        copy.wait()


def inner_kernel(me_ref, total_ref, *refs):
    packs, weights, out_ref = refs[:PLANE], refs[PLANE : 2 * PLANE], refs[2 * PLANE]
    stream_s, weight_s, sems = refs[-3:]
    copies = []
    for k in range(PLANE):
        source = packs[k].at[pl.ds(BLOCK, TRACES * STEPS)]
        copies.append(pltpu.make_async_copy(source, stream_s.at[k], sems.at[2 * k]))
        copies.append(pltpu.make_async_copy(weights[k], weight_s.at[k], sems.at[2 * k + 1]))
    for copy in copies:
        copy.start()
    place = me_ref[0] % PLANE
    slot = lax.broadcasted_iota(jnp.int32, (GROUP, TRACES * STEPS), 0)
    at = lax.broadcasted_iota(jnp.int32, (GROUP, TRACES * STEPS), 1)
    trace = slot & (PAD - 1)
    wanted = trace * STEPS + PLANE * (slot >> 3) + place
    chosen = jnp.where((at == wanted) & (trace < TRACES), 1.0, 0.0).astype(BF16)
    for k in range(PLANE):
        copies[2 * k].wait()
        base = jnp.dot(chosen, stream_s[k], preferred_element_type=F32)
        stream = (base + total_ref[:, k * 256 : (k + 1) * 256]).astype(BF16)
        copies[2 * k + 1].wait()
        part = jnp.dot(stream, weight_s[k], preferred_element_type=F32)
        out_ref[...] = part if k == 0 else out_ref[...] + part


def hidden_kernel(inner_ref, class_ref, out_ref):
    hidden = jnp.maximum(inner_ref[...], 0.0).astype(BF16)
    logits = jnp.dot(hidden, class_ref[...], preferred_element_type=F32)
    gap = logits[:, 1:2] - logits[:, 0:1]
    lane = lax.broadcasted_iota(jnp.int32, (PAD, HD), 1)
    row = lax.broadcasted_iota(jnp.int32, (PAD, HD), 0)
    mine = jnp.sum(jnp.where(lane == row, gap, 0.0), axis=0, keepdims=True)
    for k in range(out_ref.shape[0]):
        out_ref[k] = mine


def vote_kernel(prompts, clusters, got_ref, scores_ref, votes_ref):
    gap = jnp.concatenate([got_ref[k] for k in range(STEPS)], axis=0)
    scores = 1.0 / (1.0 + jnp.exp(-gap.T[:PAD]))
    scores_ref[...] = scores[:TRACES]
    chain = jnp.min(scores, axis=1, keepdims=True)
    prompt = lax.broadcasted_iota(jnp.int32, (PROMPTS, CLUSTERS), 0)
    cluster = lax.broadcasted_iota(jnp.int32, (PROMPTS, CLUSTERS), 1)
    votes = jnp.zeros((PROMPTS, CLUSTERS), F32)
    for t in range(TRACES):
        here = (prompt == prompts[t]) & (cluster == clusters[t])
        votes = votes + jnp.where(here, chain[t : t + 1, :], 0.0)
    votes_ref[...] = votes


def swapped(value, axis, bit):
    count = lax.axis_size(axis)
    return lax.ppermute(value, axis, [(s, s ^ bit) for s in range(count)])


def raised(value, planes):
    count = lax.axis_size("ctx")
    steps = planes * PLANE
    return lax.ppermute(value, "ctx", [(s, (s + steps) % count) for s in range(count)])


def per_device(
    queries,
    keys_values,
    trace_lengths,
    step_rows,
    prompt_ids,
    cluster_ids,
    step_stream,
    out_weight,
    score_weight,
    class_weight,
):
    me = lax.axis_index("ctx").astype(jnp.int32).reshape(1)
    columns = [[PLANE * z + j for z in range(Z)] for j in range(PLANE)]
    tie = lambda *values: lax.optimization_barrier(values)
    add = functools.partial(attend, me=me, lengths=trace_lengths, queries=queries)

    kv0 = keys_values
    core0 = swapped(kv0, "ctx", 1)

    half = PER_GROUP * HD
    packed = (BLOCK + TRACES * STEPS, 256)
    keep, passed, sent, weight = small_call(
        pick_kernel,
        tuple(jax.ShapeDtypeStruct((n * GROUP, half), BF16) for n in (1, 1, 2))
        + (pltpu.VMEM(packed, BF16),),
        [me, *pinned([step_rows, queries, out_weight, step_stream])],
        [SMEM] + [HBM] * 4,
        [VMEM] * 4,
        scratch_shapes=[
            pltpu.VMEM((PLANE * GROUP, half), BF16),
            pltpu.VMEM((TRACES, STEPS), jnp.int32),
            pltpu.VMEM((BLOCK, half), BF16),
            pltpu.SemaphoreType.DMA((7,)),
        ],
        name="pick",
    )
    arrived = swapped(sent, "ctx", 1)
    across = swapped(passed + arrived[GROUP:], "ctx", 2)
    wanted = keep + arrived[:GROUP] + across
    wanted, kv0y, core0 = tie(wanted, kv0, core0)
    wanted1, wanted2 = raised(wanted, -1), raised(wanted, -2)
    across0 = swapped(kv0y, "ctx", 2)
    state = add([(0, 0, 0, 0), (0, 1, 1, 0)], kvs=[pinned([kv0y])[0], core0], state=None)
    kv1 = raised(kv0, 1)
    across0, wanted1, wanted2, kv1, *state = tie(across0, wanted1, wanted2, kv1, *state)
    core0y = swapped(across0, "ctx", 1)
    wanted, wanted1, wanted2, *state = tie(wanted, wanted1, wanted2, *state)

    weight, wanted = tie(weight, wanted)
    firsts = [weight, swapped(weight, "ctx", 1), swapped(weight, "ctx", 2)]

    parts, moved = small_call(
        picked_kernel,
        (jax.ShapeDtypeStruct((GROUP, half), F32), pltpu.HBM((PLANE, BLOCK, HD), BF16)),
        [
            me,
            *pinned([trace_lengths, step_rows]),
            wanted,
            wanted1,
            wanted2,
            *pinned([kv0]),
            core0,
            across0,
            core0y,
        ],
        [SMEM, HBM, HBM] + [VMEM] * 3 + [HBM] * 4,
        [VMEM, HBM],
        scratch_shapes=[
            pltpu.VMEM((2 * PLANE, BLOCK, HD), BF16),
            pltpu.SMEM((TRACES,), jnp.int32),
            pltpu.VMEM((TRACES, STEPS), jnp.int32),
            pltpu.SemaphoreType.DMA((PLANE + 3,)),
        ],
        name="picked",
    )
    parts, kv1, *state = tie(parts, kv1, *state)
    across1 = swapped(kv1, "ctx", 2)
    *firsts, moved, weight = tie(*firsts, moved, score_weight)
    firsts = [*pinned(firsts), swapped(firsts[2], "ctx", 1)]
    weights = [weight, None, swapped(weight, "ctx", 2)]
    parts = jnp.broadcast_to(parts.astype(jnp.float16)[None], (Z, GROUP, half))
    parts = lax.all_to_all(parts, "ctx", 0, 0, axis_index_groups=columns).astype(F32)
    state = add(
        [(0, 2, 0, 0), (0, 3, 0, 1), (1, 0, 1, 0)], kvs=pinned([moved, kv1]), state=state
    )
    parts, weight, *state = tie(parts, weight, *state)
    weights[1] = swapped(weight, "ctx", 1)

    projected, pair1 = small_call(
        project_kernel,
        (jax.ShapeDtypeStruct((GROUP, WIDE), F32), pltpu.VMEM((4, BLOCK, HD), BF16)),
        [parts, *firsts, *pinned([kv1]), across1],
        [VMEM] + [HBM] * 6,
        scratch_shapes=[
            pltpu.VMEM((PLANE, BLOCK, 256), BF16),
            pltpu.SemaphoreType.DMA((PLANE + 2,)),
        ],
        name="project",
    )
    projected, pair1 = tie((projected * 0.25).astype(jnp.float16), pair1)
    pair2, cores1 = raised(pair1, 1), swapped(pair1, "ctx", 1)
    projected = projected + swapped(projected, "head", 2)
    projected, weights[2] = tie(projected, weights[2])
    projected = projected + swapped(projected, "head", 4)
    projected, cores1 = tie(projected, cores1)
    weights.append(swapped(weights[2], "ctx", 1))
    other = swapped(projected, "head", 1)
    state = add([(1, 1, 0, 0), (1, 3, 0, 1)], kvs=[cores1], state=state)
    other, pair2, *state = tie(other, pair2, *state)
    cores2 = swapped(pair2, "ctx", 1)
    projected = (projected.astype(F32) + other.astype(F32)) * 4.0

    inner = small_call(
        inner_kernel,
        jax.ShapeDtypeStruct((GROUP, WIDE), F32),
        [me, projected, *firsts, *weights],
        [SMEM, VMEM] + [HBM] * 8,
        scratch_shapes=[
            pltpu.VMEM((PLANE, TRACES * STEPS, 256), BF16),
            pltpu.VMEM((PLANE, 256, WIDE), BF16),
            pltpu.SemaphoreType.DMA((2 * PLANE,)),
        ],
        name="inner",
    )
    inner, pair2, *state = tie(inner, pair2, *state)
    inner = (inner * 2.0**-10).astype(jnp.float16).reshape(Z, PAD, WIDE)
    state = add(
        [(1, 2, 0, 1), (2, 0, 1, 0), (2, 2, 1, 1)], kvs=pinned([pair1, pair2]), state=state
    )
    inner = lax.all_to_all(inner, "ctx", 0, 0, axis_index_groups=columns)
    inner, *state = tie(inner, *state)
    inner = jnp.sum(inner.astype(F32), axis=0) * 2.0**10
    heads, count = lax.axis_size("head"), lax.axis_size("ctx")
    gap = small_call(
        hidden_kernel,
        jax.ShapeDtypeStruct((heads, 1, HD), F32),
        [inner, class_weight],
        name="hidden",
    )
    gap, cores2, *state = tie(gap, cores2, *state)
    attended = add([(2, 1, 0, 0), (2, 3, 0, 1)], kvs=[cores2], state=state, last=True)
    gap = lax.all_to_all(gap, "head", 0, 0)
    gap, attended = tie(gap, attended)
    gap = jnp.sum(gap, axis=0)
    gap = lax.all_to_all(jnp.broadcast_to(gap[None], (count, 1, HD)), "ctx", 0, 0)
    step_scores, votes = small_call(
        vote_kernel,
        (
            jax.ShapeDtypeStruct((TRACES, STEPS), F32),
            jax.ShapeDtypeStruct((PROMPTS, CLUSTERS), F32),
        ),
        [prompt_ids, cluster_ids, gap],
        [SMEM, SMEM, VMEM],
        name="vote",
    )
    return (attended, step_scores, votes)


def solution(mesh):
    placed = (
        P("ctx", "head"),
        P(None, "ctx", "head"),
        P(),
        P(),
        P(),
        P(),
        P(None, "ctx"),
        P("head", "ctx"),
        P("ctx", "head"),
        P("head", None),
    )
    return jax.shard_map(
        per_device,
        mesh=mesh,
        in_specs=placed,
        out_specs=(P("ctx", "head"), P(), P()),
        check_vma=False,
    )
```

```python
import functools
import math

import jax
import jax.numpy as jnp
from jax import lax
from jax.experimental import pallas as pl
from jax.experimental.pallas import tpu as pltpu
from jax.sharding import PartitionSpec as P

HD = 128
PROMPTS = 2
CLUSTERS = 4
TRACES = 7
STEPS = 32
PER_GROUP = 4
BLOCK = 512
TILE = 512
OWN_TILE = 256
Z = 8
PLANE = 4
PAD = 8
GROUP = Z * PAD
WIDE = 1024
COEF = HD**-0.5 * math.log2(math.e)
LOW = -1e30
NONE = -60000.0
VMEM = pl.BlockSpec(memory_space=pltpu.VMEM)
SMEM = pl.BlockSpec(memory_space=pltpu.SMEM)
HBM = pl.BlockSpec(memory_space=pltpu.HBM)
BF16 = jnp.bfloat16
F32 = jnp.float32


def first_key(row, lengths):
    start = row * 0
    end = jnp.int32(0)
    for t in range(TRACES):
        end = end + lengths[t]
        start = jnp.where(row >= end, end, start)
    return start


def pick_kernel(me_ref, steps_hbm, q_hbm, weight_hbm, stream_hbm, *refs):
    keep_ref, pass_ref, send_ref, pack_ref, all_ref, steps_ref, q_ref, sems = refs
    copies = [pltpu.make_async_copy(steps_hbm, steps_ref, sems.at[0])]
    for k in range(4):
        part = pl.ds(k * BLOCK // 4, BLOCK // 4)
        copies.append(pltpu.make_async_copy(q_hbm.at[part], q_ref.at[part], sems.at[1 + k]))
    for k, (source, begin) in enumerate([(weight_hbm, 0), (stream_hbm, BLOCK)]):
        target = pack_ref.at[pl.ds(begin, source.shape[0])]
        copies.append(pltpu.make_async_copy(source, target, sems.at[5 + k]))
    for copy in copies:
        copy.start()
    for copy in copies[:5]:
        copy.wait()
    me = me_ref[0]
    core, side = me % 2, (me // 2) % 2
    at = lax.broadcasted_iota(jnp.int32, (TRACES, BLOCK), 1) + me * BLOCK
    none = jnp.zeros((PAD - TRACES, BLOCK), F32)
    steps = steps_ref[...]
    for c in range(2):
        for y in range(2):
            parts = []
            for z in range(Z):
                step = PLANE * z + 2 * y + c
                parts.append(jnp.where(steps[:, step : step + 1] == at, 1.0, 0.0))
                parts.append(none)
            chosen = jnp.concatenate(parts, axis=0).astype(BF16)
            got = jnp.dot(chosen, q_ref[...], preferred_element_type=F32)
            all_ref[pl.ds((2 * c + y) * GROUP, GROUP), :] = got.astype(BF16)

    def group(c, y):
        return all_ref[pl.ds(pl.multiple_of((2 * c + y) * GROUP, GROUP), GROUP), :]

    keep_ref[...] = group(core, side)
    pass_ref[...] = group(core, 1 - side)
    send_ref[:GROUP] = group(1 - core, side)
    send_ref[GROUP:] = group(1 - core, 1 - side)
    for copy in copies[5:]:
        copy.wait()


def picked_kernel(me_ref, lengths_hbm, steps_hbm, q_ref, q1_ref, q2_ref, *refs):
    kv_refs, out_ref, moved_hbm = refs[:PLANE], refs[PLANE], refs[PLANE + 1]
    kv_s, lengths, steps_ref, sems = refs[-4:]
    lengths_copy = pltpu.make_async_copy(lengths_hbm, lengths, sems.at[PLANE])
    steps_copy = pltpu.make_async_copy(steps_hbm, steps_ref, sems.at[PLANE + 1])
    copies = [
        pltpu.make_async_copy(kv, kv_s.at[pl.ds(2 * k, 2)], sems.at[k])
        for k, kv in enumerate(kv_refs)
    ]
    half = pl.ds(PLANE, PLANE)
    moved_copy = pltpu.make_async_copy(kv_s.at[half], moved_hbm, sems.at[PLANE + 2])
    for copy in [lengths_copy, steps_copy] + copies:
        copy.start()
    lengths_copy.wait()
    steps_copy.wait()
    me = me_ref[0]
    place = me % PLANE
    steps = steps_ref[...]
    lane = lax.broadcasted_iota(jnp.int32, (TRACES, STEPS), 1)
    none = jnp.full((PAD - TRACES, HD), -1, jnp.int32)
    parts = []
    for z in range(Z):
        mine = jnp.where(lane == PLANE * z + place, steps, 0)
        mine = jnp.sum(mine, axis=1, keepdims=True)
        parts.append(jnp.broadcast_to(mine, (TRACES, HD)))
        parts.append(none)
    row = jnp.concatenate(parts, axis=0)
    start = first_key(row, lengths)
    row = jnp.concatenate([row] * (BLOCK // HD), axis=1)
    start = jnp.concatenate([start] * (BLOCK // HD), axis=1)
    k_pos = lax.broadcasted_iota(jnp.int32, (GROUP, BLOCK), 1)
    q = (q_ref[...].astype(F32) + q1_ref[...].astype(F32) + q2_ref[...].astype(F32)).astype(BF16)
    q = jnp.concatenate([q[:, h * HD : (h + 1) * HD] for h in range(PER_GROUP)], axis=0)
    scores = []
    for k in range(PLANE):
        key0 = (me - place + (place ^ k)) * BLOCK
        mask = (k_pos <= row - key0) & (k_pos >= start - key0)
        mask = jnp.concatenate([mask] * PER_GROUP, axis=0)
        copies[k].wait()
        s = lax.dot_general(
            q, kv_s[2 * k], (((1,), (1,)), ((), ())), preferred_element_type=F32
        )
        scores.append(jnp.where(mask, s, LOW))
    moved_copy.start()
    top = jnp.maximum(jnp.maximum(scores[0], scores[1]), jnp.maximum(scores[2], scores[3]))
    top = jnp.maximum(jnp.max(top, axis=1, keepdims=True), 0.1 * LOW)
    ones = jnp.ones((BLOCK, HD), BF16)
    pv = jnp.zeros((PER_GROUP * GROUP, 2 * HD), F32)
    for k, s in enumerate(scores):
        p = jnp.exp2((s - top) * COEF).astype(BF16)
        ext = jnp.concatenate([kv_s[2 * k + 1], ones], axis=1)
        pv = pv + jnp.dot(p, ext, preferred_element_type=F32)
    total = pv[:, HD:]
    some = total > 0.0
    total = jnp.where(some, total, 1.0)
    value = pv[:, :HD] / total
    size = jnp.where(some, top * COEF + jnp.log2(total), NONE)
    lanes = lax.broadcasted_iota(jnp.int32, (GROUP, HD), 1)
    stats = jnp.zeros((GROUP, HD), F32)
    for h in range(PER_GROUP):
        rows = slice(h * GROUP, (h + 1) * GROUP)
        out_ref[:, h * HD : (h + 1) * HD] = value[rows]
        rest = size[rows]
        for k in range(3):
            coarse = rest.astype(BF16).astype(F32)
            stats = jnp.where(lanes == PER_GROUP * k + h, coarse, stats)
            rest = rest - coarse
    for z in range(Z):
        packed = jnp.zeros((1, HD), F32)
        for t in range(TRACES):
            at = z * PAD + t
            packed = packed + pltpu.roll(stats[at : at + 1], 16 * t, 1)
        out_ref[z * PAD + TRACES : (z + 1) * PAD, :HD] = packed
    moved_copy.wait()


def attend_kernel(slots, first, last, *refs):
    n = len(slots)
    arrays = 1 + max(slot[2] for slot in slots)
    me_ref, lengths_hbm, q_hbm = refs[:3]
    kv_hbm = [refs[3 + array].at[pl.ds(2 * at, 2)] for _, _, array, at in slots]
    m_ref, l_ref, acc_ref = refs[3 + arrays : 6 + arrays]
    q_ref, kv_ref, lengths, sems = refs[-4:]
    copies = [
        pltpu.make_async_copy(kv, kv_ref.at[k], sems.at[k]) for k, kv in enumerate(kv_hbm)
    ]
    copies.append(pltpu.make_async_copy(lengths_hbm, lengths, sems.at[n]))
    for k in range(4):
        part = pl.ds(k * BLOCK // 4, BLOCK // 4)
        copies.append(
            pltpu.make_async_copy(q_hbm.at[part], q_ref.at[part], sems.at[n + 1 + k])
        )
    for copy in copies:
        copy.start()
    for copy in copies:
        copy.wait()
    me = me_ref[0]
    place = me % PLANE
    row0 = me * BLOCK
    ones = jnp.ones((BLOCK, HD), BF16)
    blocks = [me - place - back * PLANE + (place ^ flip) for back, flip, _, _ in slots]

    def weigh(rows, count, keys, ext, mask, fresh):
        q = q_ref[rows, :]
        q = jnp.concatenate([q[:, h * HD : (h + 1) * HD] for h in range(PER_GROUP)], axis=0)
        s = lax.dot_general(q, keys, (((1,), (1,)), ((), ())), preferred_element_type=F32)
        for h in range(PER_GROUP):
            cols = slice(h * HD, (h + 1) * HD)
            mine = s[h * count : (h + 1) * count]
            if mask is not None:
                mine = jnp.where(mask, mine, LOW)
            top = jnp.max(mine, axis=1, keepdims=True)
            if fresh:
                top = jnp.broadcast_to(top, (count, HD))
            else:
                before = m_ref[rows, cols]
                top = jnp.maximum(before, top)
            wide = jnp.concatenate([top] * (mine.shape[1] // HD), axis=1)
            p = jnp.exp2((mine - wide) * COEF).astype(BF16)
            pv = jnp.dot(p, ext, preferred_element_type=F32)
            m_ref[rows, cols] = top
            if fresh:
                acc_ref[rows, cols] = pv[:, :HD]
                l_ref[rows, cols] = pv[:, HD:]
            else:
                scale = jnp.exp2((before - top) * COEF)
                acc_ref[rows, cols] = acc_ref[rows, cols] * scale + pv[:, :HD]
                l_ref[rows, cols] = l_ref[rows, cols] * scale + pv[:, HD:]

    def own_block():
        for tile in range(BLOCK // OWN_TILE):
            width = (tile + 1) * OWN_TILE
            rows = slice(tile * OWN_TILE, width)
            keys = kv_ref[0, 0, :width, :]
            ext = jnp.concatenate([kv_ref[0, 1, :width, :], ones[:width]], axis=1)
            shape = (OWN_TILE, width)
            q_pos = row0 + tile * OWN_TILE + lax.broadcasted_iota(jnp.int32, shape, 0)
            k_pos = row0 + lax.broadcasted_iota(jnp.int32, shape, 1)
            starts = first_key(q_pos[:, :HD], lengths)
            starts = jnp.concatenate([starts] * (width // HD), axis=1)
            mask = (k_pos <= q_pos) & (k_pos >= starts)
            weigh(rows, OWN_TILE, keys, ext, mask, True)

    def other_tile(index, carry):
        tile, k = index % (BLOCK // TILE), index // (BLOCK // TILE)
        block = blocks[-1]
        for other in range(n - 1):
            block = jnp.where(k == other, blocks[other], block)
        key0 = block * BLOCK
        begin = pl.multiple_of(tile * TILE, TILE)
        rows = pl.ds(begin, TILE)
        low = first_key(row0 + begin, lengths)
        high = first_key(row0 + begin + TILE - 1, lengths)
        some = (block < me) & (key0 + BLOCK > low)
        every = key0 >= high

        def run(masked):
            keys = kv_ref[k, 0]
            ext = jnp.concatenate([kv_ref[k, 1], ones], axis=1)
            mask = None
            if masked:
                starts = first_key(
                    row0 + begin + lax.broadcasted_iota(jnp.int32, (TILE, HD), 0), lengths
                )
                starts = jnp.concatenate([starts] * (BLOCK // HD), axis=1)
                k_pos = key0 + lax.broadcasted_iota(jnp.int32, (TILE, BLOCK), 1)
                mask = k_pos >= starts
            weigh(rows, TILE, keys, ext, mask, False)

        pl.when(some & every)(functools.partial(run, False))
        pl.when(some & jnp.logical_not(every))(functools.partial(run, True))
        return carry

    if first:
        own_block()
    tiles = BLOCK // TILE
    lax.fori_loop(tiles * int(first), tiles * n, other_tile, 0)
    if last:
        out_ref = refs[-5]
        out_ref[...] = acc_ref[...] / l_ref[...]


def attend(slots, me, lengths, queries, kvs, state, last=False):
    shape = (BLOCK, PER_GROUP * HD)
    first = state is None
    operands = [me, *pinned([lengths, queries]), *kvs]
    specs = [SMEM] + [HBM] * (len(operands) - 1)
    shapes, aliases = (pltpu.VMEM(shape, F32),) * 3, {}
    if not first:
        at = len(operands)
        operands += [pltpu.with_memory_space_constraint(x, pltpu.VMEM) for x in state]
        specs += [VMEM] * 3
        aliases = {at + k: k for k in range(3)}
    if last:
        shapes, aliases = (jax.ShapeDtypeStruct(shape, F32),), {}
    work = PER_GROUP * BLOCK * BLOCK * len(slots)
    got = pl.pallas_call(
        functools.partial(attend_kernel, slots, first, last),
        out_shape=shapes,
        in_specs=specs,
        out_specs=[VMEM] * len(shapes),
        scratch_shapes=[
            pltpu.VMEM(shape, BF16),
            pltpu.VMEM((len(slots), 2, BLOCK, HD), BF16),
            pltpu.SMEM((TRACES,), jnp.int32),
            pltpu.SemaphoreType.DMA((len(slots) + 5,)),
        ],
        input_output_aliases=aliases,
        compiler_params=pltpu.CompilerParams(vmem_limit_bytes=20 << 20),
        cost_estimate=pl.CostEstimate(
            flops=4 * HD * work, bytes_accessed=1 << 20, transcendentals=work
        ),
        name="attend_%d_%d" % slots[0][:2],
    )(*operands)
    if last:
        return got[0]
    return list(got)


def pinned(values):
    return [pltpu.with_memory_space_constraint(value, pltpu.HBM) for value in values]


def small_call(kernel, shape, operands, specs=None, out_specs=None, **kw):
    return pl.pallas_call(
        kernel,
        out_shape=shape,
        in_specs=specs or [VMEM] * len(operands),
        out_specs=out_specs or ([VMEM] * len(shape) if type(shape) is tuple else VMEM),
        compiler_params=pltpu.CompilerParams(vmem_limit_bytes=16 << 20),
        **kw,
    )(*operands)


def project_kernel(got_ref, *refs):
    packs, blocks, out_ref, pair_ref = refs[:PLANE], refs[PLANE:-4], refs[-4], refs[-3]
    weight_s, sems = refs[-2:]
    copies = [
        pltpu.make_async_copy(pack.at[pl.ds(0, BLOCK)], weight_s.at[k], sems.at[k])
        for k, pack in enumerate(packs)
    ]
    for k, block in enumerate(blocks):
        target = pair_ref.at[pl.ds(2 * k, 2)]
        copies.append(pltpu.make_async_copy(block, target, sems.at[PLANE + k]))
    for copy in copies:
        copy.start()
    sizes = []
    for z in range(Z):
        stats = []
        for step in range(Z):
            packed = got_ref[z, step * PAD + TRACES : (step + 1) * PAD, :HD]
            for t in range(PAD):
                stats.append(pltpu.roll(packed, (HD - 16 * t) % HD, 1))
        sizes.append(jnp.concatenate(stats, axis=0))
    sizes = [
        size
        + pltpu.roll(size, HD - PER_GROUP, 1)
        + pltpu.roll(size, HD - 2 * PER_GROUP, 1)
        for size in sizes
    ]
    top = functools.reduce(jnp.maximum, sizes)
    weights = [jnp.exp2(size - top) for size in sizes]
    total = functools.reduce(jnp.add, weights)
    weights = [weight / total for weight in weights]
    slot = lax.broadcasted_iota(jnp.int32, (GROUP, HD), 0)
    picked = []
    for h in range(PER_GROUP):
        joined = jnp.zeros((GROUP, HD), F32)
        for z in range(Z):
            joined = joined + got_ref[z, :, h * HD : (h + 1) * HD] * weights[z][:, h : h + 1]
        joined = jnp.where((slot & (PAD - 1)) < TRACES, joined, 0.0)
        picked.append(joined.astype(BF16))
    picked = jnp.concatenate(picked, axis=1)
    for k in range(PLANE):
        copies[k].wait()
        part = jnp.dot(picked, weight_s[k], preferred_element_type=F32)
        out_ref[:, k * 256 : (k + 1) * 256] = part
    for copy in copies[PLANE:]:
        copy.wait()


def inner_kernel(me_ref, total_ref, *refs):
    packs, weights, out_ref = refs[:PLANE], refs[PLANE : 2 * PLANE], refs[2 * PLANE]
    stream_s, weight_s, sems = refs[-3:]
    copies = []
    for k in range(PLANE):
        source = packs[k].at[pl.ds(BLOCK, TRACES * STEPS)]
        copies.append(pltpu.make_async_copy(source, stream_s.at[k], sems.at[2 * k]))
        copies.append(pltpu.make_async_copy(weights[k], weight_s.at[k], sems.at[2 * k + 1]))
    for copy in copies:
        copy.start()
    place = me_ref[0] % PLANE
    slot = lax.broadcasted_iota(jnp.int32, (GROUP, TRACES * STEPS), 0)
    at = lax.broadcasted_iota(jnp.int32, (GROUP, TRACES * STEPS), 1)
    trace = slot & (PAD - 1)
    wanted = trace * STEPS + PLANE * (slot >> 3) + place
    chosen = jnp.where((at == wanted) & (trace < TRACES), 1.0, 0.0).astype(BF16)
    for k in range(PLANE):
        copies[2 * k].wait()
        base = jnp.dot(chosen, stream_s[k], preferred_element_type=F32)
        stream = (base + total_ref[:, k * 256 : (k + 1) * 256]).astype(BF16)
        copies[2 * k + 1].wait()
        part = jnp.dot(stream, weight_s[k], preferred_element_type=F32)
        out_ref[...] = part if k == 0 else out_ref[...] + part


def hidden_kernel(inner_ref, class_ref, out_ref):
    hidden = jnp.maximum(inner_ref[...], 0.0).astype(BF16)
    logits = jnp.dot(hidden, class_ref[...], preferred_element_type=F32)
    gap = logits[:, 1:2] - logits[:, 0:1]
    lane = lax.broadcasted_iota(jnp.int32, (PAD, HD), 1)
    row = lax.broadcasted_iota(jnp.int32, (PAD, HD), 0)
    mine = jnp.sum(jnp.where(lane == row, gap, 0.0), axis=0, keepdims=True)
    for k in range(out_ref.shape[0]):
        out_ref[k] = mine


def vote_kernel(prompts, clusters, got_ref, scores_ref, votes_ref):
    gap = jnp.concatenate([got_ref[k] for k in range(STEPS)], axis=0)
    scores = 1.0 / (1.0 + jnp.exp(-gap.T[:PAD]))
    scores_ref[...] = scores[:TRACES]
    chain = jnp.min(scores, axis=1, keepdims=True)
    prompt = lax.broadcasted_iota(jnp.int32, (PROMPTS, CLUSTERS), 0)
    cluster = lax.broadcasted_iota(jnp.int32, (PROMPTS, CLUSTERS), 1)
    votes = jnp.zeros((PROMPTS, CLUSTERS), F32)
    for t in range(TRACES):
        here = (prompt == prompts[t]) & (cluster == clusters[t])
        votes = votes + jnp.where(here, chain[t : t + 1, :], 0.0)
    votes_ref[...] = votes


def swapped(value, axis, bit):
    count = lax.axis_size(axis)
    return lax.ppermute(value, axis, [(s, s ^ bit) for s in range(count)])


def raised(value, planes):
    count = lax.axis_size("ctx")
    steps = planes * PLANE
    return lax.ppermute(value, "ctx", [(s, (s + steps) % count) for s in range(count)])


def per_device(
    queries,
    keys_values,
    trace_lengths,
    step_rows,
    prompt_ids,
    cluster_ids,
    step_stream,
    out_weight,
    score_weight,
    class_weight,
):
    me = lax.axis_index("ctx").astype(jnp.int32).reshape(1)
    columns = [[PLANE * z + j for z in range(Z)] for j in range(PLANE)]
    tie = lambda *values: lax.optimization_barrier(values)
    add = functools.partial(attend, me=me, lengths=trace_lengths, queries=queries)

    kv0 = keys_values
    core0 = swapped(kv0, "ctx", 1)

    half = PER_GROUP * HD
    packed = (BLOCK + TRACES * STEPS, 256)
    keep, passed, sent, weight = small_call(
        pick_kernel,
        tuple(jax.ShapeDtypeStruct((n * GROUP, half), BF16) for n in (1, 1, 2))
        + (pltpu.VMEM(packed, BF16),),
        [me, *pinned([step_rows, queries, out_weight, step_stream])],
        [SMEM] + [HBM] * 4,
        [VMEM] * 4,
        scratch_shapes=[
            pltpu.VMEM((PLANE * GROUP, half), BF16),
            pltpu.VMEM((TRACES, STEPS), jnp.int32),
            pltpu.VMEM((BLOCK, half), BF16),
            pltpu.SemaphoreType.DMA((7,)),
        ],
        name="pick",
    )
    arrived = swapped(sent, "ctx", 1)
    across = swapped(passed + arrived[GROUP:], "ctx", 2)
    wanted = keep + arrived[:GROUP] + across
    wanted, kv0y, core0 = tie(wanted, kv0, core0)
    wanted1, wanted2 = raised(wanted, -1), raised(wanted, -2)
    across0 = swapped(kv0y, "ctx", 2)
    state = add([(0, 0, 0, 0), (0, 1, 1, 0)], kvs=[pinned([kv0y])[0], core0], state=None)
    kv1 = raised(kv0, 1)
    across0, wanted1, wanted2, kv1, *state = tie(across0, wanted1, wanted2, kv1, *state)
    core0y = swapped(across0, "ctx", 1)
    wanted, wanted1, wanted2, *state = tie(wanted, wanted1, wanted2, *state)

    weight, *state = tie(weight, *state)
    firsts = [weight, swapped(weight, "ctx", 1), swapped(weight, "ctx", 2)]

    parts, moved = small_call(
        picked_kernel,
        (jax.ShapeDtypeStruct((GROUP, half), F32), pltpu.HBM((PLANE, BLOCK, HD), BF16)),
        [
            me,
            *pinned([trace_lengths, step_rows]),
            wanted,
            wanted1,
            wanted2,
            *pinned([kv0]),
            core0,
            across0,
            core0y,
        ],
        [SMEM, HBM, HBM] + [VMEM] * 3 + [HBM] * 4,
        [VMEM, HBM],
        scratch_shapes=[
            pltpu.VMEM((2 * PLANE, BLOCK, HD), BF16),
            pltpu.SMEM((TRACES,), jnp.int32),
            pltpu.VMEM((TRACES, STEPS), jnp.int32),
            pltpu.SemaphoreType.DMA((PLANE + 3,)),
        ],
        name="picked",
    )
    parts, kv1, *firsts = tie(parts, kv1, *firsts)
    across1 = swapped(kv1, "ctx", 2)
    weight, parts = tie(score_weight, parts)
    firsts = [*pinned(firsts), swapped(firsts[2], "ctx", 1)]
    weights = [weight, None, swapped(weight, "ctx", 2)]
    parts = jnp.broadcast_to(parts.astype(jnp.float16)[None], (Z, GROUP, half))
    parts = lax.all_to_all(parts, "ctx", 0, 0, axis_index_groups=columns).astype(F32)
    state = add(
        [(0, 2, 0, 0), (0, 3, 0, 1), (1, 0, 1, 0)], kvs=pinned([moved, kv1]), state=state
    )
    parts, weight, *state = tie(parts, weight, *state)
    weights[1] = swapped(weight, "ctx", 1)

    projected, pair1 = small_call(
        project_kernel,
        (jax.ShapeDtypeStruct((GROUP, WIDE), F32), pltpu.VMEM((4, BLOCK, HD), BF16)),
        [parts, *firsts, *pinned([kv1]), across1],
        [VMEM] + [HBM] * 6,
        scratch_shapes=[
            pltpu.VMEM((PLANE, BLOCK, 256), BF16),
            pltpu.SemaphoreType.DMA((PLANE + 2,)),
        ],
        name="project",
    )
    projected, pair1 = tie((projected * 0.25).astype(jnp.float16), pair1)
    pair2, cores1 = raised(pair1, 1), swapped(pair1, "ctx", 1)
    projected = projected + swapped(projected, "head", 2)
    projected, weights[2] = tie(projected, weights[2])
    projected = projected + swapped(projected, "head", 4)
    projected, cores1 = tie(projected, cores1)
    weights.append(swapped(weights[2], "ctx", 1))
    other = swapped(projected, "head", 1)
    state = add([(1, 1, 0, 0), (1, 3, 0, 1)], kvs=[cores1], state=state)
    other, pair2, *state = tie(other, pair2, *state)
    cores2 = swapped(pair2, "ctx", 1)
    projected = (projected.astype(F32) + other.astype(F32)) * 4.0

    inner = small_call(
        inner_kernel,
        jax.ShapeDtypeStruct((GROUP, WIDE), F32),
        [me, projected, *firsts, *weights],
        [SMEM, VMEM] + [HBM] * 8,
        scratch_shapes=[
            pltpu.VMEM((PLANE, TRACES * STEPS, 256), BF16),
            pltpu.VMEM((PLANE, 256, WIDE), BF16),
            pltpu.SemaphoreType.DMA((2 * PLANE,)),
        ],
        name="inner",
    )
    inner, pair2, *state = tie(inner, pair2, *state)
    inner = (inner * 2.0**-10).astype(jnp.float16).reshape(Z, PAD, WIDE)
    state = add(
        [(1, 2, 0, 1), (2, 0, 1, 0), (2, 2, 1, 1)], kvs=pinned([pair1, pair2]), state=state
    )
    inner = lax.all_to_all(inner, "ctx", 0, 0, axis_index_groups=columns)
    inner, *state = tie(inner, *state)
    inner = jnp.sum(inner.astype(F32), axis=0) * 2.0**10
    heads, count = lax.axis_size("head"), lax.axis_size("ctx")
    gap = small_call(
        hidden_kernel,
        jax.ShapeDtypeStruct((heads, 1, HD), F32),
        [inner, class_weight],
        name="hidden",
    )
    gap, cores2, *state = tie(gap, cores2, *state)
    attended = add([(2, 1, 0, 0), (2, 3, 0, 1)], kvs=[cores2], state=state, last=True)
    gap = lax.all_to_all(gap, "head", 0, 0)
    gap, attended = tie(gap, attended)
    gap = jnp.sum(gap, axis=0)
    gap = lax.all_to_all(jnp.broadcast_to(gap[None], (count, 1, HD)), "ctx", 0, 0)
    step_scores, votes = small_call(
        vote_kernel,
        (
            jax.ShapeDtypeStruct((TRACES, STEPS), F32),
            jax.ShapeDtypeStruct((PROMPTS, CLUSTERS), F32),
        ),
        [prompt_ids, cluster_ids, gap],
        [SMEM, SMEM, VMEM],
        name="vote",
    )
    return (attended, step_scores, votes)


def solution(mesh):
    placed = (
        P("ctx", "head"),
        P(None, "ctx", "head"),
        P(),
        P(),
        P(),
        P(),
        P(None, "ctx"),
        P("head", "ctx"),
        P("ctx", "head"),
        P("head", None),
    )
    return jax.shard_map(
        per_device,
        mesh=mesh,
        in_specs=placed,
        out_specs=(P("ctx", "head"), P(), P()),
        check_vma=False,
    )
```

```python
import functools
import math

import jax
import jax.numpy as jnp
from jax import lax
from jax.experimental import pallas as pl
from jax.experimental.pallas import tpu as pltpu
from jax.sharding import PartitionSpec as P

HD = 128
PROMPTS = 2
CLUSTERS = 4
TRACES = 7
STEPS = 32
PER_GROUP = 4
BLOCK = 512
TILE = 512
OWN_TILE = 256
Z = 8
PLANE = 4
PAD = 8
GROUP = Z * PAD
WIDE = 1024
COEF = HD**-0.5 * math.log2(math.e)
LOW = -1e30
NONE = -60000.0
VMEM = pl.BlockSpec(memory_space=pltpu.VMEM)
SMEM = pl.BlockSpec(memory_space=pltpu.SMEM)
HBM = pl.BlockSpec(memory_space=pltpu.HBM)
BF16 = jnp.bfloat16
F32 = jnp.float32


def first_key(row, lengths):
    start = row * 0
    end = jnp.int32(0)
    for t in range(TRACES):
        end = end + lengths[t]
        start = jnp.where(row >= end, end, start)
    return start


def pick_kernel(me_ref, steps_hbm, q_hbm, weight_hbm, stream_hbm, *refs):
    keep_ref, pass_ref, send_ref, pack_ref, all_ref, steps_ref, q_ref, sems = refs
    copies = [pltpu.make_async_copy(steps_hbm, steps_ref, sems.at[0])]
    for k in range(4):
        part = pl.ds(k * BLOCK // 4, BLOCK // 4)
        copies.append(pltpu.make_async_copy(q_hbm.at[part], q_ref.at[part], sems.at[1 + k]))
    for k, (source, begin) in enumerate([(weight_hbm, 0), (stream_hbm, BLOCK)]):
        target = pack_ref.at[pl.ds(begin, source.shape[0])]
        copies.append(pltpu.make_async_copy(source, target, sems.at[5 + k]))
    for copy in copies:
        copy.start()
    for copy in copies[:5]:
        copy.wait()
    me = me_ref[0]
    core, side = me % 2, (me // 2) % 2
    at = lax.broadcasted_iota(jnp.int32, (TRACES, BLOCK), 1) + me * BLOCK
    none = jnp.zeros((PAD - TRACES, BLOCK), F32)
    steps = steps_ref[...]
    for c in range(2):
        for y in range(2):
            parts = []
            for z in range(Z):
                step = PLANE * z + 2 * y + c
                parts.append(jnp.where(steps[:, step : step + 1] == at, 1.0, 0.0))
                parts.append(none)
            chosen = jnp.concatenate(parts, axis=0).astype(BF16)
            got = jnp.dot(chosen, q_ref[...], preferred_element_type=F32)
            all_ref[pl.ds((2 * c + y) * GROUP, GROUP), :] = got.astype(BF16)

    def group(c, y):
        return all_ref[pl.ds(pl.multiple_of((2 * c + y) * GROUP, GROUP), GROUP), :]

    keep_ref[...] = group(core, side)
    pass_ref[...] = group(core, 1 - side)
    send_ref[:GROUP] = group(1 - core, side)
    send_ref[GROUP:] = group(1 - core, 1 - side)
    for copy in copies[5:]:
        copy.wait()


def picked_kernel(me_ref, lengths_hbm, steps_hbm, q_ref, q1_ref, q2_ref, *refs):
    kv_refs, out_ref, moved_hbm = refs[:PLANE], refs[PLANE], refs[PLANE + 1]
    kv_s, lengths, steps_ref, sems = refs[-4:]
    lengths_copy = pltpu.make_async_copy(lengths_hbm, lengths, sems.at[PLANE])
    steps_copy = pltpu.make_async_copy(steps_hbm, steps_ref, sems.at[PLANE + 1])
    copies = [
        pltpu.make_async_copy(kv, kv_s.at[pl.ds(2 * k, 2)], sems.at[k])
        for k, kv in enumerate(kv_refs)
    ]
    half = pl.ds(PLANE, PLANE)
    moved_copy = pltpu.make_async_copy(kv_s.at[half], moved_hbm, sems.at[PLANE + 2])
    for copy in [lengths_copy, steps_copy] + copies:
        copy.start()
    lengths_copy.wait()
    steps_copy.wait()
    me = me_ref[0]
    place = me % PLANE
    steps = steps_ref[...]
    lane = lax.broadcasted_iota(jnp.int32, (TRACES, STEPS), 1)
    none = jnp.full((PAD - TRACES, HD), -1, jnp.int32)
    parts = []
    for z in range(Z):
        mine = jnp.where(lane == PLANE * z + place, steps, 0)
        mine = jnp.sum(mine, axis=1, keepdims=True)
        parts.append(jnp.broadcast_to(mine, (TRACES, HD)))
        parts.append(none)
    row = jnp.concatenate(parts, axis=0)
    start = first_key(row, lengths)
    row = jnp.concatenate([row] * (BLOCK // HD), axis=1)
    start = jnp.concatenate([start] * (BLOCK // HD), axis=1)
    k_pos = lax.broadcasted_iota(jnp.int32, (GROUP, BLOCK), 1)
    q = (q_ref[...].astype(F32) + q1_ref[...].astype(F32) + q2_ref[...].astype(F32)).astype(BF16)
    q = jnp.concatenate([q[:, h * HD : (h + 1) * HD] for h in range(PER_GROUP)], axis=0)
    scores = []
    for k in range(PLANE):
        key0 = (me - place + (place ^ k)) * BLOCK
        mask = (k_pos <= row - key0) & (k_pos >= start - key0)
        mask = jnp.concatenate([mask] * PER_GROUP, axis=0)
        copies[k].wait()
        s = lax.dot_general(
            q, kv_s[2 * k], (((1,), (1,)), ((), ())), preferred_element_type=F32
        )
        scores.append(jnp.where(mask, s, LOW))
    moved_copy.start()
    top = jnp.maximum(jnp.maximum(scores[0], scores[1]), jnp.maximum(scores[2], scores[3]))
    top = jnp.maximum(jnp.max(top, axis=1, keepdims=True), 0.1 * LOW)
    ones = jnp.ones((BLOCK, HD), BF16)
    pv = jnp.zeros((PER_GROUP * GROUP, 2 * HD), F32)
    for k, s in enumerate(scores):
        p = jnp.exp2((s - top) * COEF).astype(BF16)
        ext = jnp.concatenate([kv_s[2 * k + 1], ones], axis=1)
        pv = pv + jnp.dot(p, ext, preferred_element_type=F32)
    total = pv[:, HD:]
    some = total > 0.0
    total = jnp.where(some, total, 1.0)
    value = pv[:, :HD] / total
    size = jnp.where(some, top * COEF + jnp.log2(total), NONE)
    lanes = lax.broadcasted_iota(jnp.int32, (GROUP, HD), 1)
    stats = jnp.zeros((GROUP, HD), F32)
    for h in range(PER_GROUP):
        rows = slice(h * GROUP, (h + 1) * GROUP)
        out_ref[:, h * HD : (h + 1) * HD] = value[rows]
        rest = size[rows]
        for k in range(3):
            coarse = rest.astype(BF16).astype(F32)
            stats = jnp.where(lanes == PER_GROUP * k + h, coarse, stats)
            rest = rest - coarse
    for z in range(Z):
        packed = jnp.zeros((1, HD), F32)
        for t in range(TRACES):
            at = z * PAD + t
            packed = packed + pltpu.roll(stats[at : at + 1], 16 * t, 1)
        out_ref[z * PAD + TRACES : (z + 1) * PAD, :HD] = packed
    moved_copy.wait()


def attend_kernel(slots, first, last, *refs):
    n = len(slots)
    arrays = 1 + max(slot[2] for slot in slots)
    me_ref, lengths_hbm, q_hbm = refs[:3]
    kv_hbm = [refs[3 + array].at[pl.ds(2 * at, 2)] for _, _, array, at in slots]
    m_ref, l_ref, acc_ref = refs[3 + arrays : 6 + arrays]
    q_ref, kv_ref, lengths, sems = refs[-4:]
    copies = [
        pltpu.make_async_copy(kv, kv_ref.at[k], sems.at[k]) for k, kv in enumerate(kv_hbm)
    ]
    copies.append(pltpu.make_async_copy(lengths_hbm, lengths, sems.at[n]))
    for k in range(4):
        part = pl.ds(k * BLOCK // 4, BLOCK // 4)
        copies.append(
            pltpu.make_async_copy(q_hbm.at[part], q_ref.at[part], sems.at[n + 1 + k])
        )
    for copy in copies:
        copy.start()
    for copy in copies:
        copy.wait()
    me = me_ref[0]
    place = me % PLANE
    row0 = me * BLOCK
    ones = jnp.ones((BLOCK, HD), BF16)
    blocks = [me - place - back * PLANE + (place ^ flip) for back, flip, _, _ in slots]

    def weigh(rows, count, keys, ext, mask, fresh):
        q = q_ref[rows, :]
        q = jnp.concatenate([q[:, h * HD : (h + 1) * HD] for h in range(PER_GROUP)], axis=0)
        s = lax.dot_general(q, keys, (((1,), (1,)), ((), ())), preferred_element_type=F32)
        for h in range(PER_GROUP):
            cols = slice(h * HD, (h + 1) * HD)
            mine = s[h * count : (h + 1) * count]
            if mask is not None:
                mine = jnp.where(mask, mine, LOW)
            top = jnp.max(mine, axis=1, keepdims=True)
            if fresh:
                top = jnp.broadcast_to(top, (count, HD))
            else:
                before = m_ref[rows, cols]
                top = jnp.maximum(before, top)
            wide = jnp.concatenate([top] * (mine.shape[1] // HD), axis=1)
            p = jnp.exp2((mine - wide) * COEF).astype(BF16)
            pv = jnp.dot(p, ext, preferred_element_type=F32)
            m_ref[rows, cols] = top
            if fresh:
                acc_ref[rows, cols] = pv[:, :HD]
                l_ref[rows, cols] = pv[:, HD:]
            else:
                scale = jnp.exp2((before - top) * COEF)
                acc_ref[rows, cols] = acc_ref[rows, cols] * scale + pv[:, :HD]
                l_ref[rows, cols] = l_ref[rows, cols] * scale + pv[:, HD:]

    def own_block():
        for tile in range(BLOCK // OWN_TILE):
            width = (tile + 1) * OWN_TILE
            rows = slice(tile * OWN_TILE, width)
            keys = kv_ref[0, 0, :width, :]
            ext = jnp.concatenate([kv_ref[0, 1, :width, :], ones[:width]], axis=1)
            shape = (OWN_TILE, width)
            q_pos = row0 + tile * OWN_TILE + lax.broadcasted_iota(jnp.int32, shape, 0)
            k_pos = row0 + lax.broadcasted_iota(jnp.int32, shape, 1)
            starts = first_key(q_pos[:, :HD], lengths)
            starts = jnp.concatenate([starts] * (width // HD), axis=1)
            mask = (k_pos <= q_pos) & (k_pos >= starts)
            weigh(rows, OWN_TILE, keys, ext, mask, True)

    def other_tile(index, carry):
        tile, k = index % (BLOCK // TILE), index // (BLOCK // TILE)
        block = blocks[-1]
        for other in range(n - 1):
            block = jnp.where(k == other, blocks[other], block)
        key0 = block * BLOCK
        begin = pl.multiple_of(tile * TILE, TILE)
        rows = pl.ds(begin, TILE)
        low = first_key(row0 + begin, lengths)
        high = first_key(row0 + begin + TILE - 1, lengths)
        some = (block < me) & (key0 + BLOCK > low)
        every = key0 >= high

        def run(masked):
            keys = kv_ref[k, 0]
            ext = jnp.concatenate([kv_ref[k, 1], ones], axis=1)
            mask = None
            if masked:
                starts = first_key(
                    row0 + begin + lax.broadcasted_iota(jnp.int32, (TILE, HD), 0), lengths
                )
                starts = jnp.concatenate([starts] * (BLOCK // HD), axis=1)
                k_pos = key0 + lax.broadcasted_iota(jnp.int32, (TILE, BLOCK), 1)
                mask = k_pos >= starts
            weigh(rows, TILE, keys, ext, mask, False)

        pl.when(some & every)(functools.partial(run, False))
        pl.when(some & jnp.logical_not(every))(functools.partial(run, True))
        return carry

    if first:
        own_block()
    tiles = BLOCK // TILE
    lax.fori_loop(tiles * int(first), tiles * n, other_tile, 0)
    if last:
        out_ref = refs[-5]
        out_ref[...] = acc_ref[...] / l_ref[...]


def attend(slots, me, lengths, queries, kvs, state, last=False):
    shape = (BLOCK, PER_GROUP * HD)
    first = state is None
    operands = [me, *pinned([lengths, queries]), *kvs]
    specs = [SMEM] + [HBM] * (len(operands) - 1)
    shapes, aliases = (pltpu.VMEM(shape, F32),) * 3, {}
    if not first:
        at = len(operands)
        operands += [pltpu.with_memory_space_constraint(x, pltpu.VMEM) for x in state]
        specs += [VMEM] * 3
        aliases = {at + k: k for k in range(3)}
    if last:
        shapes, aliases = (jax.ShapeDtypeStruct(shape, F32),), {}
    work = PER_GROUP * BLOCK * BLOCK * len(slots)
    got = pl.pallas_call(
        functools.partial(attend_kernel, slots, first, last),
        out_shape=shapes,
        in_specs=specs,
        out_specs=[VMEM] * len(shapes),
        scratch_shapes=[
            pltpu.VMEM(shape, BF16),
            pltpu.VMEM((len(slots), 2, BLOCK, HD), BF16),
            pltpu.SMEM((TRACES,), jnp.int32),
            pltpu.SemaphoreType.DMA((len(slots) + 5,)),
        ],
        input_output_aliases=aliases,
        compiler_params=pltpu.CompilerParams(vmem_limit_bytes=20 << 20),
        cost_estimate=pl.CostEstimate(
            flops=4 * HD * work, bytes_accessed=1 << 20, transcendentals=work
        ),
        name="attend_%d_%d" % slots[0][:2],
    )(*operands)
    if last:
        return got[0]
    return list(got)


def pinned(values):
    return [pltpu.with_memory_space_constraint(value, pltpu.HBM) for value in values]


def small_call(kernel, shape, operands, specs=None, out_specs=None, **kw):
    return pl.pallas_call(
        kernel,
        out_shape=shape,
        in_specs=specs or [VMEM] * len(operands),
        out_specs=out_specs or ([VMEM] * len(shape) if type(shape) is tuple else VMEM),
        compiler_params=pltpu.CompilerParams(vmem_limit_bytes=16 << 20),
        **kw,
    )(*operands)


def project_kernel(got_ref, *refs):
    packs, blocks, out_ref, pair_ref = refs[:PLANE], refs[PLANE:-4], refs[-4], refs[-3]
    weight_s, sems = refs[-2:]
    copies = [
        pltpu.make_async_copy(pack.at[pl.ds(0, BLOCK)], weight_s.at[k], sems.at[k])
        for k, pack in enumerate(packs)
    ]
    for k, block in enumerate(blocks):
        target = pair_ref.at[pl.ds(2 * k, 2)]
        copies.append(pltpu.make_async_copy(block, target, sems.at[PLANE + k]))
    for copy in copies:
        copy.start()
    sizes = []
    for z in range(Z):
        stats = []
        for step in range(Z):
            packed = got_ref[z, step * PAD + TRACES : (step + 1) * PAD, :HD]
            for t in range(PAD):
                stats.append(pltpu.roll(packed, (HD - 16 * t) % HD, 1))
        sizes.append(jnp.concatenate(stats, axis=0))
    sizes = [
        size
        + pltpu.roll(size, HD - PER_GROUP, 1)
        + pltpu.roll(size, HD - 2 * PER_GROUP, 1)
        for size in sizes
    ]
    top = functools.reduce(jnp.maximum, sizes)
    weights = [jnp.exp2(size - top) for size in sizes]
    total = functools.reduce(jnp.add, weights)
    weights = [weight / total for weight in weights]
    slot = lax.broadcasted_iota(jnp.int32, (GROUP, HD), 0)
    picked = []
    for h in range(PER_GROUP):
        joined = jnp.zeros((GROUP, HD), F32)
        for z in range(Z):
            joined = joined + got_ref[z, :, h * HD : (h + 1) * HD] * weights[z][:, h : h + 1]
        joined = jnp.where((slot & (PAD - 1)) < TRACES, joined, 0.0)
        picked.append(joined.astype(BF16))
    picked = jnp.concatenate(picked, axis=1)
    for k in range(PLANE):
        copies[k].wait()
        part = jnp.dot(picked, weight_s[k], preferred_element_type=F32)
        out_ref[:, k * 256 : (k + 1) * 256] = part
    for copy in copies[PLANE:]:
        copy.wait()


def inner_kernel(me_ref, total_ref, *refs):
    packs, weights, out_ref = refs[:PLANE], refs[PLANE : 2 * PLANE], refs[2 * PLANE]
    stream_s, weight_s, sems = refs[-3:]
    copies = []
    for k in range(PLANE):
        source = packs[k].at[pl.ds(BLOCK, TRACES * STEPS)]
        copies.append(pltpu.make_async_copy(source, stream_s.at[k], sems.at[2 * k]))
        copies.append(pltpu.make_async_copy(weights[k], weight_s.at[k], sems.at[2 * k + 1]))
    for copy in copies:
        copy.start()
    place = me_ref[0] % PLANE
    slot = lax.broadcasted_iota(jnp.int32, (GROUP, TRACES * STEPS), 0)
    at = lax.broadcasted_iota(jnp.int32, (GROUP, TRACES * STEPS), 1)
    trace = slot & (PAD - 1)
    wanted = trace * STEPS + PLANE * (slot >> 3) + place
    chosen = jnp.where((at == wanted) & (trace < TRACES), 1.0, 0.0).astype(BF16)
    for k in range(PLANE):
        copies[2 * k].wait()
        base = jnp.dot(chosen, stream_s[k], preferred_element_type=F32)
        stream = (base + total_ref[:, k * 256 : (k + 1) * 256]).astype(BF16)
        copies[2 * k + 1].wait()
        part = jnp.dot(stream, weight_s[k], preferred_element_type=F32)
        out_ref[...] = part if k == 0 else out_ref[...] + part


def hidden_kernel(inner_ref, class_ref, out_ref):
    hidden = jnp.maximum(inner_ref[...], 0.0).astype(BF16)
    logits = jnp.dot(hidden, class_ref[...], preferred_element_type=F32)
    gap = logits[:, 1:2] - logits[:, 0:1]
    lane = lax.broadcasted_iota(jnp.int32, (PAD, HD), 1)
    row = lax.broadcasted_iota(jnp.int32, (PAD, HD), 0)
    mine = jnp.sum(jnp.where(lane == row, gap, 0.0), axis=0, keepdims=True)
    for k in range(out_ref.shape[0]):
        out_ref[k] = mine


def vote_kernel(prompts, clusters, got_ref, scores_ref, votes_ref):
    gap = jnp.concatenate([got_ref[k] for k in range(STEPS)], axis=0)
    scores = 1.0 / (1.0 + jnp.exp(-gap.T[:PAD]))
    scores_ref[...] = scores[:TRACES]
    chain = jnp.min(scores, axis=1, keepdims=True)
    prompt = lax.broadcasted_iota(jnp.int32, (PROMPTS, CLUSTERS), 0)
    cluster = lax.broadcasted_iota(jnp.int32, (PROMPTS, CLUSTERS), 1)
    votes = jnp.zeros((PROMPTS, CLUSTERS), F32)
    for t in range(TRACES):
        here = (prompt == prompts[t]) & (cluster == clusters[t])
        votes = votes + jnp.where(here, chain[t : t + 1, :], 0.0)
    votes_ref[...] = votes


def swapped(value, axis, bit):
    count = lax.axis_size(axis)
    return lax.ppermute(value, axis, [(s, s ^ bit) for s in range(count)])


def raised(value, planes):
    count = lax.axis_size("ctx")
    steps = planes * PLANE
    return lax.ppermute(value, "ctx", [(s, (s + steps) % count) for s in range(count)])


def per_device(
    queries,
    keys_values,
    trace_lengths,
    step_rows,
    prompt_ids,
    cluster_ids,
    step_stream,
    out_weight,
    score_weight,
    class_weight,
):
    me = lax.axis_index("ctx").astype(jnp.int32).reshape(1)
    columns = [[PLANE * z + j for z in range(Z)] for j in range(PLANE)]
    tie = lambda *values: lax.optimization_barrier(values)
    add = functools.partial(attend, me=me, lengths=trace_lengths, queries=queries)

    kv0 = keys_values
    core0 = swapped(kv0, "ctx", 1)

    half = PER_GROUP * HD
    packed = (BLOCK + TRACES * STEPS, 256)
    keep, passed, sent, weight = small_call(
        pick_kernel,
        tuple(jax.ShapeDtypeStruct((n * GROUP, half), BF16) for n in (1, 1, 2))
        + (pltpu.VMEM(packed, BF16),),
        [me, *pinned([step_rows, queries, out_weight, step_stream])],
        [SMEM] + [HBM] * 4,
        [VMEM] * 4,
        scratch_shapes=[
            pltpu.VMEM((PLANE * GROUP, half), BF16),
            pltpu.VMEM((TRACES, STEPS), jnp.int32),
            pltpu.VMEM((BLOCK, half), BF16),
            pltpu.SemaphoreType.DMA((7,)),
        ],
        name="pick",
    )
    arrived = swapped(sent, "ctx", 1)
    across = swapped(passed + arrived[GROUP:], "ctx", 2)
    wanted = keep + arrived[:GROUP] + across
    wanted, kv0y, core0 = tie(wanted, kv0, core0)
    wanted1, wanted2 = raised(wanted, -1), raised(wanted, -2)
    across0 = swapped(kv0y, "ctx", 2)
    state = add([(0, 0, 0, 0), (0, 1, 1, 0)], kvs=[pinned([kv0y])[0], core0], state=None)
    kv1 = raised(kv0, 1)
    across0, wanted1, wanted2, kv1, *state = tie(across0, wanted1, wanted2, kv1, *state)
    core0y = swapped(across0, "ctx", 1)
    wanted, wanted1, wanted2, *state = tie(wanted, wanted1, wanted2, *state)

    weight, _ = tie(weight, kv0y)
    firsts = [weight, swapped(weight, "ctx", 1), swapped(weight, "ctx", 2)]
    wanted, firsts[2] = tie(wanted, firsts[2])

    parts, moved = small_call(
        picked_kernel,
        (jax.ShapeDtypeStruct((GROUP, half), F32), pltpu.HBM((PLANE, BLOCK, HD), BF16)),
        [
            me,
            *pinned([trace_lengths, step_rows]),
            wanted,
            wanted1,
            wanted2,
            *pinned([kv0]),
            core0,
            across0,
            core0y,
        ],
        [SMEM, HBM, HBM] + [VMEM] * 3 + [HBM] * 4,
        [VMEM, HBM],
        scratch_shapes=[
            pltpu.VMEM((2 * PLANE, BLOCK, HD), BF16),
            pltpu.SMEM((TRACES,), jnp.int32),
            pltpu.VMEM((TRACES, STEPS), jnp.int32),
            pltpu.SemaphoreType.DMA((PLANE + 3,)),
        ],
        name="picked",
    )
    parts, kv1, firsts[2] = tie(parts, kv1, firsts[2])
    across1 = swapped(kv1, "ctx", 2)
    weight, parts = tie(score_weight, parts)
    firsts.append(swapped(firsts[2], "ctx", 1))
    weights = [weight, None, swapped(weight, "ctx", 2)]
    parts = jnp.broadcast_to(parts.astype(jnp.float16)[None], (Z, GROUP, half))
    parts = lax.all_to_all(parts, "ctx", 0, 0, axis_index_groups=columns).astype(F32)
    state = add(
        [(0, 2, 0, 0), (0, 3, 0, 1), (1, 0, 1, 0)], kvs=pinned([moved, kv1]), state=state
    )
    parts, weight, *state = tie(parts, weight, *state)
    weights[1] = swapped(weight, "ctx", 1)

    projected, pair1 = small_call(
        project_kernel,
        (jax.ShapeDtypeStruct((GROUP, WIDE), F32), pltpu.VMEM((4, BLOCK, HD), BF16)),
        [parts, *firsts, *pinned([kv1]), across1],
        [VMEM] + [HBM] * 6,
        scratch_shapes=[
            pltpu.VMEM((PLANE, BLOCK, 256), BF16),
            pltpu.SemaphoreType.DMA((PLANE + 2,)),
        ],
        name="project",
    )
    projected, pair1 = tie((projected * 0.25).astype(jnp.float16), pair1)
    pair2, cores1 = raised(pair1, 1), swapped(pair1, "ctx", 1)
    projected = projected + swapped(projected, "head", 2)
    projected, weights[2] = tie(projected, weights[2])
    projected = projected + swapped(projected, "head", 4)
    projected, cores1 = tie(projected, cores1)
    weights.append(swapped(weights[2], "ctx", 1))
    other = swapped(projected, "head", 1)
    state = add([(1, 1, 0, 0), (1, 3, 0, 1)], kvs=[cores1], state=state)
    other, pair2, *state = tie(other, pair2, *state)
    cores2 = swapped(pair2, "ctx", 1)
    projected = (projected.astype(F32) + other.astype(F32)) * 4.0

    inner = small_call(
        inner_kernel,
        jax.ShapeDtypeStruct((GROUP, WIDE), F32),
        [me, projected, *firsts, *weights],
        [SMEM, VMEM] + [HBM] * 8,
        scratch_shapes=[
            pltpu.VMEM((PLANE, TRACES * STEPS, 256), BF16),
            pltpu.VMEM((PLANE, 256, WIDE), BF16),
            pltpu.SemaphoreType.DMA((2 * PLANE,)),
        ],
        name="inner",
    )
    inner, pair2, *state = tie(inner, pair2, *state)
    inner = (inner * 2.0**-10).astype(jnp.float16).reshape(Z, PAD, WIDE)
    state = add(
        [(1, 2, 0, 1), (2, 0, 1, 0), (2, 2, 1, 1)], kvs=pinned([pair1, pair2]), state=state
    )
    inner = lax.all_to_all(inner, "ctx", 0, 0, axis_index_groups=columns)
    inner, *state = tie(inner, *state)
    inner = jnp.sum(inner.astype(F32), axis=0) * 2.0**10
    heads, count = lax.axis_size("head"), lax.axis_size("ctx")
    gap = small_call(
        hidden_kernel,
        jax.ShapeDtypeStruct((heads, 1, HD), F32),
        [inner, class_weight],
        name="hidden",
    )
    gap, cores2, *state = tie(gap, cores2, *state)
    attended = add([(2, 1, 0, 0), (2, 3, 0, 1)], kvs=[cores2], state=state, last=True)
    gap = lax.all_to_all(gap, "head", 0, 0)
    gap, attended = tie(gap, attended)
    gap = jnp.sum(gap, axis=0)
    gap = lax.all_to_all(jnp.broadcast_to(gap[None], (count, 1, HD)), "ctx", 0, 0)
    step_scores, votes = small_call(
        vote_kernel,
        (
            jax.ShapeDtypeStruct((TRACES, STEPS), F32),
            jax.ShapeDtypeStruct((PROMPTS, CLUSTERS), F32),
        ),
        [prompt_ids, cluster_ids, gap],
        [SMEM, SMEM, VMEM],
        name="vote",
    )
    return (attended, step_scores, votes)


def solution(mesh):
    placed = (
        P("ctx", "head"),
        P(None, "ctx", "head"),
        P(),
        P(),
        P(),
        P(),
        P(None, "ctx"),
        P("head", "ctx"),
        P("ctx", "head"),
        P("head", None),
    )
    return jax.shard_map(
        per_device,
        mesh=mesh,
        in_specs=placed,
        out_specs=(P("ctx", "head"), P(), P()),
        check_vma=False,
    )
```

```python
import functools
import math

import jax
import jax.numpy as jnp
from jax import lax
from jax.experimental import pallas as pl
from jax.experimental.pallas import tpu as pltpu
from jax.sharding import PartitionSpec as P

HD = 128
PROMPTS = 2
CLUSTERS = 4
TRACES = 7
STEPS = 32
PER_GROUP = 4
BLOCK = 512
TILE = 512
OWN_TILE = 256
Z = 8
PLANE = 4
PAD = 8
GROUP = Z * PAD
WIDE = 1024
COEF = HD**-0.5 * math.log2(math.e)
LOW = -1e30
NONE = -60000.0
VMEM = pl.BlockSpec(memory_space=pltpu.VMEM)
SMEM = pl.BlockSpec(memory_space=pltpu.SMEM)
HBM = pl.BlockSpec(memory_space=pltpu.HBM)
BF16 = jnp.bfloat16
F32 = jnp.float32


def first_key(row, lengths):
    start = row * 0
    end = jnp.int32(0)
    for t in range(TRACES):
        end = end + lengths[t]
        start = jnp.where(row >= end, end, start)
    return start


def pick_kernel(me_ref, steps_hbm, q_hbm, *refs):
    keep_ref, pass_ref, send_ref, all_ref, steps_ref, q_ref, sems = refs
    copies = [pltpu.make_async_copy(steps_hbm, steps_ref, sems.at[0])]
    for k in range(4):
        part = pl.ds(k * BLOCK // 4, BLOCK // 4)
        copies.append(pltpu.make_async_copy(q_hbm.at[part], q_ref.at[part], sems.at[1 + k]))
    for copy in copies:
        copy.start()
    for copy in copies:
        copy.wait()
    me = me_ref[0]
    core, side = me % 2, (me // 2) % 2
    at = lax.broadcasted_iota(jnp.int32, (TRACES, BLOCK), 1) + me * BLOCK
    none = jnp.zeros((PAD - TRACES, BLOCK), F32)
    steps = steps_ref[...]
    for c in range(2):
        for y in range(2):
            parts = []
            for z in range(Z):
                step = PLANE * z + 2 * y + c
                parts.append(jnp.where(steps[:, step : step + 1] == at, 1.0, 0.0))
                parts.append(none)
            chosen = jnp.concatenate(parts, axis=0).astype(BF16)
            got = jnp.dot(chosen, q_ref[...], preferred_element_type=F32)
            all_ref[pl.ds((2 * c + y) * GROUP, GROUP), :] = got.astype(BF16)

    def group(c, y):
        return all_ref[pl.ds(pl.multiple_of((2 * c + y) * GROUP, GROUP), GROUP), :]

    keep_ref[...] = group(core, side)
    pass_ref[...] = group(core, 1 - side)
    send_ref[:GROUP] = group(1 - core, side)
    send_ref[GROUP:] = group(1 - core, 1 - side)


def picked_kernel(me_ref, lengths_hbm, steps_hbm, q_ref, q1_ref, q2_ref, *refs):
    kv_refs, out_ref, moved_hbm = refs[:PLANE], refs[PLANE], refs[PLANE + 1]
    kv_s, lengths, steps_ref, sems = refs[-4:]
    lengths_copy = pltpu.make_async_copy(lengths_hbm, lengths, sems.at[PLANE])
    steps_copy = pltpu.make_async_copy(steps_hbm, steps_ref, sems.at[PLANE + 1])
    copies = [
        pltpu.make_async_copy(kv, kv_s.at[pl.ds(2 * k, 2)], sems.at[k])
        for k, kv in enumerate(kv_refs)
    ]
    half = pl.ds(PLANE, PLANE)
    moved_copy = pltpu.make_async_copy(kv_s.at[half], moved_hbm, sems.at[PLANE + 2])
    for copy in [lengths_copy, steps_copy] + copies:
        copy.start()
    lengths_copy.wait()
    steps_copy.wait()
    me = me_ref[0]
    place = me % PLANE
    steps = steps_ref[...]
    lane = lax.broadcasted_iota(jnp.int32, (TRACES, STEPS), 1)
    none = jnp.full((PAD - TRACES, HD), -1, jnp.int32)
    parts = []
    for z in range(Z):
        mine = jnp.where(lane == PLANE * z + place, steps, 0)
        mine = jnp.sum(mine, axis=1, keepdims=True)
        parts.append(jnp.broadcast_to(mine, (TRACES, HD)))
        parts.append(none)
    row = jnp.concatenate(parts, axis=0)
    start = first_key(row, lengths)
    row = jnp.concatenate([row] * (BLOCK // HD), axis=1)
    start = jnp.concatenate([start] * (BLOCK // HD), axis=1)
    k_pos = lax.broadcasted_iota(jnp.int32, (GROUP, BLOCK), 1)
    q = (q_ref[...].astype(F32) + q1_ref[...].astype(F32) + q2_ref[...].astype(F32)).astype(BF16)
    q = jnp.concatenate([q[:, h * HD : (h + 1) * HD] for h in range(PER_GROUP)], axis=0)
    scores = []
    for k in range(PLANE):
        key0 = (me - place + (place ^ k)) * BLOCK
        mask = (k_pos <= row - key0) & (k_pos >= start - key0)
        mask = jnp.concatenate([mask] * PER_GROUP, axis=0)
        copies[k].wait()
        s = lax.dot_general(
            q, kv_s[2 * k], (((1,), (1,)), ((), ())), preferred_element_type=F32
        )
        scores.append(jnp.where(mask, s, LOW))
    moved_copy.start()
    top = jnp.maximum(jnp.maximum(scores[0], scores[1]), jnp.maximum(scores[2], scores[3]))
    top = jnp.maximum(jnp.max(top, axis=1, keepdims=True), 0.1 * LOW)
    ones = jnp.ones((BLOCK, HD), BF16)
    pv = jnp.zeros((PER_GROUP * GROUP, 2 * HD), F32)
    for k, s in enumerate(scores):
        p = jnp.exp2((s - top) * COEF).astype(BF16)
        ext = jnp.concatenate([kv_s[2 * k + 1], ones], axis=1)
        pv = pv + jnp.dot(p, ext, preferred_element_type=F32)
    total = pv[:, HD:]
    some = total > 0.0
    total = jnp.where(some, total, 1.0)
    value = pv[:, :HD] / total
    size = jnp.where(some, top * COEF + jnp.log2(total), NONE)
    lanes = lax.broadcasted_iota(jnp.int32, (GROUP, HD), 1)
    stats = jnp.zeros((GROUP, HD), F32)
    for h in range(PER_GROUP):
        rows = slice(h * GROUP, (h + 1) * GROUP)
        out_ref[:, h * HD : (h + 1) * HD] = value[rows]
        rest = size[rows]
        for k in range(3):
            coarse = rest.astype(BF16).astype(F32)
            stats = jnp.where(lanes == PER_GROUP * k + h, coarse, stats)
            rest = rest - coarse
    for z in range(Z):
        packed = jnp.zeros((1, HD), F32)
        for t in range(TRACES):
            at = z * PAD + t
            packed = packed + pltpu.roll(stats[at : at + 1], 16 * t, 1)
        out_ref[z * PAD + TRACES : (z + 1) * PAD, :HD] = packed
    moved_copy.wait()


def attend_kernel(slots, first, last, *refs):
    n = len(slots)
    arrays = 1 + max(slot[2] for slot in slots)
    me_ref, lengths_hbm, q_hbm = refs[:3]
    kv_hbm = [refs[3 + array].at[pl.ds(2 * at, 2)] for _, _, array, at in slots]
    m_ref, l_ref, acc_ref = refs[3 + arrays : 6 + arrays]
    q_ref, kv_ref, lengths, sems = refs[-4:]
    copies = [
        pltpu.make_async_copy(kv, kv_ref.at[k], sems.at[k]) for k, kv in enumerate(kv_hbm)
    ]
    copies.append(pltpu.make_async_copy(lengths_hbm, lengths, sems.at[n]))
    for k in range(4):
        part = pl.ds(k * BLOCK // 4, BLOCK // 4)
        copies.append(
            pltpu.make_async_copy(q_hbm.at[part], q_ref.at[part], sems.at[n + 1 + k])
        )
    for copy in copies:
        copy.start()
    for copy in copies:
        copy.wait()
    me = me_ref[0]
    place = me % PLANE
    row0 = me * BLOCK
    ones = jnp.ones((BLOCK, HD), BF16)
    blocks = [me - place - back * PLANE + (place ^ flip) for back, flip, _, _ in slots]

    def weigh(rows, count, keys, ext, mask, fresh):
        q = q_ref[rows, :]
        q = jnp.concatenate([q[:, h * HD : (h + 1) * HD] for h in range(PER_GROUP)], axis=0)
        s = lax.dot_general(q, keys, (((1,), (1,)), ((), ())), preferred_element_type=F32)
        for h in range(PER_GROUP):
            cols = slice(h * HD, (h + 1) * HD)
            mine = s[h * count : (h + 1) * count]
            if mask is not None:
                mine = jnp.where(mask, mine, LOW)
            top = jnp.max(mine, axis=1, keepdims=True)
            if fresh:
                top = jnp.broadcast_to(top, (count, HD))
            else:
                before = m_ref[rows, cols]
                top = jnp.maximum(before, top)
            wide = jnp.concatenate([top] * (mine.shape[1] // HD), axis=1)
            p = jnp.exp2((mine - wide) * COEF).astype(BF16)
            pv = jnp.dot(p, ext, preferred_element_type=F32)
            m_ref[rows, cols] = top
            if fresh:
                acc_ref[rows, cols] = pv[:, :HD]
                l_ref[rows, cols] = pv[:, HD:]
            else:
                scale = jnp.exp2((before - top) * COEF)
                acc_ref[rows, cols] = acc_ref[rows, cols] * scale + pv[:, :HD]
                l_ref[rows, cols] = l_ref[rows, cols] * scale + pv[:, HD:]

    def own_block():
        for tile in range(BLOCK // OWN_TILE):
            width = (tile + 1) * OWN_TILE
            rows = slice(tile * OWN_TILE, width)
            keys = kv_ref[0, 0, :width, :]
            ext = jnp.concatenate([kv_ref[0, 1, :width, :], ones[:width]], axis=1)
            shape = (OWN_TILE, width)
            q_pos = row0 + tile * OWN_TILE + lax.broadcasted_iota(jnp.int32, shape, 0)
            k_pos = row0 + lax.broadcasted_iota(jnp.int32, shape, 1)
            starts = first_key(q_pos[:, :HD], lengths)
            starts = jnp.concatenate([starts] * (width // HD), axis=1)
            mask = (k_pos <= q_pos) & (k_pos >= starts)
            weigh(rows, OWN_TILE, keys, ext, mask, True)

    def other_tile(index, carry):
        tile, k = index % (BLOCK // TILE), index // (BLOCK // TILE)
        block = blocks[-1]
        for other in range(n - 1):
            block = jnp.where(k == other, blocks[other], block)
        key0 = block * BLOCK
        begin = pl.multiple_of(tile * TILE, TILE)
        rows = pl.ds(begin, TILE)
        low = first_key(row0 + begin, lengths)
        high = first_key(row0 + begin + TILE - 1, lengths)
        some = (block < me) & (key0 + BLOCK > low)
        every = key0 >= high

        def run(masked):
            keys = kv_ref[k, 0]
            ext = jnp.concatenate([kv_ref[k, 1], ones], axis=1)
            mask = None
            if masked:
                starts = first_key(
                    row0 + begin + lax.broadcasted_iota(jnp.int32, (TILE, HD), 0), lengths
                )
                starts = jnp.concatenate([starts] * (BLOCK // HD), axis=1)
                k_pos = key0 + lax.broadcasted_iota(jnp.int32, (TILE, BLOCK), 1)
                mask = k_pos >= starts
            weigh(rows, TILE, keys, ext, mask, False)

        pl.when(some & every)(functools.partial(run, False))
        pl.when(some & jnp.logical_not(every))(functools.partial(run, True))
        return carry

    if first:
        own_block()
    tiles = BLOCK // TILE
    lax.fori_loop(tiles * int(first), tiles * n, other_tile, 0)
    if last:
        out_ref = refs[-5]
        out_ref[...] = acc_ref[...] / l_ref[...]


def attend(slots, me, lengths, queries, kvs, state, last=False):
    shape = (BLOCK, PER_GROUP * HD)
    first = state is None
    operands = [me, *pinned([lengths, queries]), *kvs]
    specs = [SMEM] + [HBM] * (len(operands) - 1)
    shapes, aliases = (pltpu.VMEM(shape, F32),) * 3, {}
    if not first:
        at = len(operands)
        operands += [pltpu.with_memory_space_constraint(x, pltpu.VMEM) for x in state]
        specs += [VMEM] * 3
        aliases = {at + k: k for k in range(3)}
    if last:
        shapes, aliases = (jax.ShapeDtypeStruct(shape, F32),), {}
    work = PER_GROUP * BLOCK * BLOCK * len(slots)
    got = pl.pallas_call(
        functools.partial(attend_kernel, slots, first, last),
        out_shape=shapes,
        in_specs=specs,
        out_specs=[VMEM] * len(shapes),
        scratch_shapes=[
            pltpu.VMEM(shape, BF16),
            pltpu.VMEM((len(slots), 2, BLOCK, HD), BF16),
            pltpu.SMEM((TRACES,), jnp.int32),
            pltpu.SemaphoreType.DMA((len(slots) + 5,)),
        ],
        input_output_aliases=aliases,
        compiler_params=pltpu.CompilerParams(vmem_limit_bytes=20 << 20),
        cost_estimate=pl.CostEstimate(
            flops=4 * HD * work, bytes_accessed=1 << 20, transcendentals=work
        ),
        name="attend_%d_%d" % slots[0][:2],
    )(*operands)
    if last:
        return got[0]
    return list(got)


def pinned(values):
    return [pltpu.with_memory_space_constraint(value, pltpu.HBM) for value in values]


def small_call(kernel, shape, operands, specs=None, out_specs=None, **kw):
    return pl.pallas_call(
        kernel,
        out_shape=shape,
        in_specs=specs or [VMEM] * len(operands),
        out_specs=out_specs or ([VMEM] * len(shape) if type(shape) is tuple else VMEM),
        compiler_params=pltpu.CompilerParams(vmem_limit_bytes=16 << 20),
        **kw,
    )(*operands)


def project_kernel(got_ref, *refs):
    packs, blocks, out_ref, pair_ref = refs[:PLANE], refs[PLANE:-4], refs[-4], refs[-3]
    weight_s, sems = refs[-2:]
    copies = [
        pltpu.make_async_copy(pack.at[pl.ds(0, BLOCK)], weight_s.at[k], sems.at[k])
        for k, pack in enumerate(packs)
    ]
    for k, block in enumerate(blocks):
        target = pair_ref.at[pl.ds(2 * k, 2)]
        copies.append(pltpu.make_async_copy(block, target, sems.at[PLANE + k]))
    for copy in copies:
        copy.start()
    sizes = []
    for z in range(Z):
        stats = []
        for step in range(Z):
            packed = got_ref[z, step * PAD + TRACES : (step + 1) * PAD, :HD]
            for t in range(PAD):
                stats.append(pltpu.roll(packed, (HD - 16 * t) % HD, 1))
        sizes.append(jnp.concatenate(stats, axis=0))
    sizes = [
        size
        + pltpu.roll(size, HD - PER_GROUP, 1)
        + pltpu.roll(size, HD - 2 * PER_GROUP, 1)
        for size in sizes
    ]
    top = functools.reduce(jnp.maximum, sizes)
    weights = [jnp.exp2(size - top) for size in sizes]
    total = functools.reduce(jnp.add, weights)
    weights = [weight / total for weight in weights]
    slot = lax.broadcasted_iota(jnp.int32, (GROUP, HD), 0)
    picked = []
    for h in range(PER_GROUP):
        joined = jnp.zeros((GROUP, HD), F32)
        for z in range(Z):
            joined = joined + got_ref[z, :, h * HD : (h + 1) * HD] * weights[z][:, h : h + 1]
        joined = jnp.where((slot & (PAD - 1)) < TRACES, joined, 0.0)
        picked.append(joined.astype(BF16))
    picked = jnp.concatenate(picked, axis=1)
    for k in range(PLANE):
        copies[k].wait()
        part = jnp.dot(picked, weight_s[k], preferred_element_type=F32)
        out_ref[:, k * 256 : (k + 1) * 256] = part
    for copy in copies[PLANE:]:
        copy.wait()


def inner_kernel(me_ref, total_ref, *refs):
    packs, weights, out_ref = refs[:PLANE], refs[PLANE : 2 * PLANE], refs[2 * PLANE]
    stream_s, weight_s, sems = refs[-3:]
    copies = []
    for k in range(PLANE):
        copies.append(pltpu.make_async_copy(packs[k], stream_s.at[k], sems.at[2 * k]))
        copies.append(pltpu.make_async_copy(weights[k], weight_s.at[k], sems.at[2 * k + 1]))
    for copy in copies:
        copy.start()
    place = me_ref[0] % PLANE
    slot = lax.broadcasted_iota(jnp.int32, (GROUP, TRACES * STEPS), 0)
    at = lax.broadcasted_iota(jnp.int32, (GROUP, TRACES * STEPS), 1)
    trace = slot & (PAD - 1)
    wanted = trace * STEPS + PLANE * (slot >> 3) + place
    chosen = jnp.where((at == wanted) & (trace < TRACES), 1.0, 0.0).astype(BF16)
    for k in range(PLANE):
        copies[2 * k].wait()
        base = jnp.dot(chosen, stream_s[k], preferred_element_type=F32)
        stream = (base + total_ref[:, k * 256 : (k + 1) * 256]).astype(BF16)
        copies[2 * k + 1].wait()
        part = jnp.dot(stream, weight_s[k], preferred_element_type=F32)
        out_ref[...] = part if k == 0 else out_ref[...] + part


def hidden_kernel(inner_ref, class_ref, out_ref):
    hidden = jnp.maximum(inner_ref[...], 0.0).astype(BF16)
    logits = jnp.dot(hidden, class_ref[...], preferred_element_type=F32)
    gap = logits[:, 1:2] - logits[:, 0:1]
    lane = lax.broadcasted_iota(jnp.int32, (PAD, HD), 1)
    row = lax.broadcasted_iota(jnp.int32, (PAD, HD), 0)
    mine = jnp.sum(jnp.where(lane == row, gap, 0.0), axis=0, keepdims=True)
    for k in range(out_ref.shape[0]):
        out_ref[k] = mine


def vote_kernel(prompts, clusters, got_ref, scores_ref, votes_ref):
    gap = jnp.concatenate([got_ref[k] for k in range(STEPS)], axis=0)
    scores = 1.0 / (1.0 + jnp.exp(-gap.T[:PAD]))
    scores_ref[...] = scores[:TRACES]
    chain = jnp.min(scores, axis=1, keepdims=True)
    prompt = lax.broadcasted_iota(jnp.int32, (PROMPTS, CLUSTERS), 0)
    cluster = lax.broadcasted_iota(jnp.int32, (PROMPTS, CLUSTERS), 1)
    votes = jnp.zeros((PROMPTS, CLUSTERS), F32)
    for t in range(TRACES):
        here = (prompt == prompts[t]) & (cluster == clusters[t])
        votes = votes + jnp.where(here, chain[t : t + 1, :], 0.0)
    votes_ref[...] = votes


def swapped(value, axis, bit):
    count = lax.axis_size(axis)
    return lax.ppermute(value, axis, [(s, s ^ bit) for s in range(count)])


def raised(value, planes):
    count = lax.axis_size("ctx")
    steps = planes * PLANE
    return lax.ppermute(value, "ctx", [(s, (s + steps) % count) for s in range(count)])


def per_device(
    queries,
    keys_values,
    trace_lengths,
    step_rows,
    prompt_ids,
    cluster_ids,
    step_stream,
    out_weight,
    score_weight,
    class_weight,
):
    me = lax.axis_index("ctx").astype(jnp.int32).reshape(1)
    columns = [[PLANE * z + j for z in range(Z)] for j in range(PLANE)]
    tie = lambda *values: lax.optimization_barrier(values)
    add = functools.partial(attend, me=me, lengths=trace_lengths, queries=queries)

    kv0 = keys_values
    core0 = swapped(kv0, "ctx", 1)

    half = PER_GROUP * HD
    keep, passed, sent = small_call(
        pick_kernel,
        tuple(jax.ShapeDtypeStruct((n * GROUP, half), BF16) for n in (1, 1, 2)),
        [me, *pinned([step_rows, queries])],
        [SMEM] + [HBM] * 2,
        [VMEM] * 3,
        scratch_shapes=[
            pltpu.VMEM((PLANE * GROUP, half), BF16),
            pltpu.VMEM((TRACES, STEPS), jnp.int32),
            pltpu.VMEM((BLOCK, half), BF16),
            pltpu.SemaphoreType.DMA((7,)),
        ],
        name="pick",
    )
    arrived = swapped(sent, "ctx", 1)
    across = swapped(passed + arrived[GROUP:], "ctx", 2)
    wanted = keep + arrived[:GROUP] + across
    wanted, kv0y, core0 = tie(wanted, kv0, core0)
    wanted1, wanted2 = raised(wanted, -1), raised(wanted, -2)
    across0 = swapped(kv0y, "ctx", 2)
    state = add([(0, 0, 0, 0), (0, 1, 1, 0)], kvs=[pinned([kv0y])[0], core0], state=None)
    kv1 = raised(kv0, 1)
    across0, wanted1, wanted2, kv1, *state = tie(across0, wanted1, wanted2, kv1, *state)
    core0y = swapped(across0, "ctx", 1)
    wanted, wanted1, wanted2, *state = tie(wanted, wanted1, wanted2, *state)

    weight, _ = tie(out_weight, kv0y)
    firsts = [weight, swapped(weight, "ctx", 1), swapped(weight, "ctx", 2)]
    wanted, firsts[2] = tie(wanted, firsts[2])

    parts, moved = small_call(
        picked_kernel,
        (jax.ShapeDtypeStruct((GROUP, half), F32), pltpu.HBM((PLANE, BLOCK, HD), BF16)),
        [
            me,
            *pinned([trace_lengths, step_rows]),
            wanted,
            wanted1,
            wanted2,
            *pinned([kv0]),
            core0,
            across0,
            core0y,
        ],
        [SMEM, HBM, HBM] + [VMEM] * 3 + [HBM] * 4,
        [VMEM, HBM],
        scratch_shapes=[
            pltpu.VMEM((2 * PLANE, BLOCK, HD), BF16),
            pltpu.SMEM((TRACES,), jnp.int32),
            pltpu.VMEM((TRACES, STEPS), jnp.int32),
            pltpu.SemaphoreType.DMA((PLANE + 3,)),
        ],
        name="picked",
    )
    parts, kv1, firsts[2] = tie(parts, kv1, firsts[2])
    across1 = swapped(kv1, "ctx", 2)
    weight, stream, parts = tie(score_weight, step_stream, parts)
    streams = [stream] + [swapped(stream, "ctx", bits) for bits in (1, 2, 3)]
    firsts.append(swapped(firsts[2], "ctx", 1))
    weights = [weight, None, swapped(weight, "ctx", 2)]
    parts = jnp.broadcast_to(parts.astype(jnp.float16)[None], (Z, GROUP, half))
    parts = lax.all_to_all(parts, "ctx", 0, 0, axis_index_groups=columns).astype(F32)
    state = add(
        [(0, 2, 0, 0), (0, 3, 0, 1), (1, 0, 1, 0)], kvs=pinned([moved, kv1]), state=state
    )
    parts, weight, *state = tie(parts, weight, *state)
    weights[1] = swapped(weight, "ctx", 1)

    projected, pair1 = small_call(
        project_kernel,
        (jax.ShapeDtypeStruct((GROUP, WIDE), F32), pltpu.VMEM((4, BLOCK, HD), BF16)),
        [parts, *firsts, *pinned([kv1]), across1],
        [VMEM] + [HBM] * 6,
        scratch_shapes=[
            pltpu.VMEM((PLANE, BLOCK, 256), BF16),
            pltpu.SemaphoreType.DMA((PLANE + 2,)),
        ],
        name="project",
    )
    projected, pair1 = tie((projected * 0.25).astype(jnp.float16), pair1)
    pair2, cores1 = raised(pair1, 1), swapped(pair1, "ctx", 1)
    projected = projected + swapped(projected, "head", 2)
    projected, weights[2] = tie(projected, weights[2])
    projected = projected + swapped(projected, "head", 4)
    projected, cores1 = tie(projected, cores1)
    weights.append(swapped(weights[2], "ctx", 1))
    other = swapped(projected, "head", 1)
    state = add([(1, 1, 0, 0), (1, 3, 0, 1)], kvs=[cores1], state=state)
    other, pair2, *state = tie(other, pair2, *state)
    cores2 = swapped(pair2, "ctx", 1)
    projected = (projected.astype(F32) + other.astype(F32)) * 4.0

    inner = small_call(
        inner_kernel,
        jax.ShapeDtypeStruct((GROUP, WIDE), F32),
        [me, projected, *streams, *weights],
        [SMEM, VMEM] + [HBM] * 8,
        scratch_shapes=[
            pltpu.VMEM((PLANE, TRACES * STEPS, 256), BF16),
            pltpu.VMEM((PLANE, 256, WIDE), BF16),
            pltpu.SemaphoreType.DMA((2 * PLANE,)),
        ],
        name="inner",
    )
    inner, pair2, *state = tie(inner, pair2, *state)
    inner = (inner * 2.0**-10).astype(jnp.float16).reshape(Z, PAD, WIDE)
    state = add(
        [(1, 2, 0, 1), (2, 0, 1, 0), (2, 2, 1, 1)], kvs=pinned([pair1, pair2]), state=state
    )
    inner = lax.all_to_all(inner, "ctx", 0, 0, axis_index_groups=columns)
    inner, *state = tie(inner, *state)
    inner = jnp.sum(inner.astype(F32), axis=0) * 2.0**10
    heads, count = lax.axis_size("head"), lax.axis_size("ctx")
    gap = small_call(
        hidden_kernel,
        jax.ShapeDtypeStruct((heads, 1, HD), F32),
        [inner, class_weight],
        name="hidden",
    )
    gap, cores2, *state = tie(gap, cores2, *state)
    attended = add([(2, 1, 0, 0), (2, 3, 0, 1)], kvs=[cores2], state=state, last=True)
    gap = lax.all_to_all(gap, "head", 0, 0)
    gap, attended = tie(gap, attended)
    gap = jnp.sum(gap, axis=0)
    gap = lax.all_to_all(jnp.broadcast_to(gap[None], (count, 1, HD)), "ctx", 0, 0)
    step_scores, votes = small_call(
        vote_kernel,
        (
            jax.ShapeDtypeStruct((TRACES, STEPS), F32),
            jax.ShapeDtypeStruct((PROMPTS, CLUSTERS), F32),
        ),
        [prompt_ids, cluster_ids, gap],
        [SMEM, SMEM, VMEM],
        name="vote",
    )
    return (attended, step_scores, votes)


def solution(mesh):
    placed = (
        P("ctx", "head"),
        P(None, "ctx", "head"),
        P(),
        P(),
        P(),
        P(),
        P(None, "ctx"),
        P("head", "ctx"),
        P("ctx", "head"),
        P("head", None),
    )
    return jax.shard_map(
        per_device,
        mesh=mesh,
        in_specs=placed,
        out_specs=(P("ctx", "head"), P(), P()),
        check_vma=False,
    )
```
